128 devices in a mesh: lat: 32 (over z_lo, x, y), lon: 4 (over z_hi, core).
Axes of the slice: x: 4, y: 4, z: 4 (z_hi: 2, z_lo: 2; z = z_hi * 2 + z_lo), core: 2. Of those that a mesh axis runs over, the one named last changes fastest.
Arguments:
- grid_field: bfloat16 [64, 1440, 384], P('lat', 'lon'), may hold values from -6 to 6
- cotangent: bfloat16 [64, 1440, 384], P('lat', 'lon'), may hold values from -6 to 6
- analysis_table: bfloat16 [2, 256, 64, 512], P(None, ('lat', 'lon')), may hold values from -0.75 to 0.75
- synthesis_table: bfloat16 [2, 256, 64, 512], P(None, ('lat', 'lon')), may hold values from -0.25 to 0.25
- spectral_weight: bfloat16 [2, 256, 2, 384, 384], P(None, ('lat', 'lon')), may hold values from -0.3125 to 0.3125
- disco_weight: bfloat16 [4, 384, 384], replicated, may hold values from -0.15625 to 0.15625
- disco_kernel: float32 [9, 4, 64], replicated, may hold values from -1 to 1
- neighbour_offsets: int32 [9, 2], replicated, may hold values from -2 to 2, as said below
Outputs:
- block_output: bfloat16 [64, 1440, 384], P('lat', 'lon')
- field_grad: bfloat16 [64, 1440, 384], P('lat', 'lon')
- spectral_grad: float32 [2, 256, 2, 384, 384], P(None, ('lat', 'lon'))
- disco_grad: float32 [4, 384, 384], replicated
The draws below stay inside these ranges and needn't reach their ends.
Inputs may be any that keep to these rules, and one draw needn't show every extreme that they name: `neighbour_offsets`: each row holds one neighbour's latitude offset and longitude offset in cells; each column takes both -2 and 2.
All inputs are finite; a program needn't handle non-finite values.
Results may differ from the reference program's by a relative error of at most 0.019.
Values may be sent and summed in bfloat16 or wider, within the bound.
No kernel may reach another device: no remote copies, remote signals or barrier semaphores. Data moves between devices by JAX's collectives and lax.ppermute only.
A program may use at most 128 MiB of HBM per device.

```python
import math
import jax
import jax.numpy as jnp
from jax import lax

CHANNELS = 384
LON_CELLS = 1440
WAVENUMBERS = 512
DEGREES = 512
BASIS_FUNCS = 4
NEIGHBOURS = 9
HALO_REACH = 2
LAT_CELLS = 64


def draw_neighbour_offsets(key, part):
    key_base = jax.random.fold_in(key, 11)
    key_sign = jax.random.fold_in(key, 12)
    drawn = jax.random.randint(key_base, (NEIGHBOURS - 2, 2), -HALO_REACH, HALO_REACH + 1, dtype=jnp.int32)
    flipped = 2 * jax.random.randint(key_sign, (), 0, 2, dtype=jnp.int32) - 1
    extreme = jnp.stack([jnp.stack([flipped, -flipped]), jnp.stack([-flipped, flipped])]) * HALO_REACH
    return jnp.concatenate([extreme.astype(jnp.int32), drawn], axis=0)


def steps_of(rng, extent, pieces, least, largest):
    loudness, own = 1.0, jax.random.fold_in(rng, 6)
    for dim, parts in pieces:
        heights = jnp.exp(jax.random.uniform(jax.random.fold_in(own, dim), (parts,), jnp.float32, least / len(pieces), largest / len(pieces)))
        loudness = loudness * jnp.repeat(heights, extent[dim] // parts).reshape([-1 if axis == dim else 1 for axis in range(len(extent))])
    return loudness


def normal_values(rng, shape, width, bound, cuts=(), held_as=jnp.bfloat16):
    factor_of = steps_of(rng, shape, cuts, -0.22, 0.18) if cuts else 1.0
    values = jax.random.normal(rng, shape, jnp.float32) * width * factor_of
    return jnp.minimum(jnp.maximum(values, -bound), bound).astype(held_as)


def setup_inputs(seed: int = 0) -> dict:
    seeds = jax.random.split(jax.random.key(seed), 9)
    return {
        "grid_field": normal_values(seeds[0], (LAT_CELLS, LON_CELLS, CHANNELS), 1.0, 6.0, ((0, 32), (1, 4))),
        "cotangent": normal_values(seeds[1], (LAT_CELLS, LON_CELLS, CHANNELS), 1.0, 6.0, ((0, 32), (1, 4))),
        "analysis_table": normal_values(seeds[2], (2, WAVENUMBERS // 2, LAT_CELLS, DEGREES), LAT_CELLS ** -0.5, 0.75, ((1, 128),)),
        "synthesis_table": normal_values(seeds[3], (2, WAVENUMBERS // 2, LAT_CELLS, DEGREES), DEGREES ** -0.5, 0.25, ((1, 128),)),
        "spectral_weight": normal_values(seeds[4], (2, DEGREES // 2, 2, CHANNELS, CHANNELS), CHANNELS ** -0.5, 0.3125, ((1, 128),)),
        "disco_weight": normal_values(seeds[5], (BASIS_FUNCS, CHANNELS, CHANNELS), (BASIS_FUNCS * CHANNELS) ** -0.5, 0.15625),
        "disco_kernel": normal_values(seeds[6], (NEIGHBOURS, BASIS_FUNCS, LAT_CELLS), (4 * NEIGHBOURS) ** -0.5, 1.0, (), jnp.float32),
        "neighbour_offsets": draw_neighbour_offsets(jax.random.fold_in(seeds[8], 71), 0),
    }


def fourier_basis(columns, wave_ids, lon_cells):
    phase_ids = columns[:, None] * wave_ids[None, :] % lon_cells
    radians = phase_ids.astype(jnp.float32) * (2.0 * math.pi / lon_cells)
    factor = 1.0 / math.sqrt(lon_cells)
    return jnp.stack([jnp.cos(radians) * factor, -jnp.sin(radians) * factor]).astype(jnp.bfloat16)

def unfold_halves(folded):
    return jnp.concatenate([folded[0], jnp.flip(folded[1], axis=0)], axis=0)

def contract(pattern, operand, weights):
    return jnp.einsum(pattern, operand.astype(jnp.float32), weights.astype(jnp.float32))

def apply_mix(coefficients, weights):
    real_in = coefficients[:, :, 0]
    imag_in = coefficients[:, :, 1]
    real_w = weights[:, 0]
    imag_w = weights[:, 1]
    real_out = contract('mlc,lcd->mld', real_in, real_w) - contract('mlc,lcd->mld', imag_in, imag_w)
    imag_out = contract('mlc,lcd->mld', real_in, imag_w) + contract('mlc,lcd->mld', imag_in, real_w)
    return jnp.stack([real_out, imag_out], axis=2).astype(jnp.bfloat16)

def mix_back(mixed_grad, weights):
    real_g = mixed_grad[:, :, 0]
    imag_g = mixed_grad[:, :, 1]
    real_w = weights[:, 0]
    imag_w = weights[:, 1]
    real_back = contract('mld,lcd->mlc', real_g, real_w) + contract('mld,lcd->mlc', imag_g, imag_w)
    imag_back = contract('mld,lcd->mlc', imag_g, real_w) - contract('mld,lcd->mlc', real_g, imag_w)
    return jnp.stack([real_back, imag_back], axis=2).astype(jnp.bfloat16)

def weight_grad(coefficients, mixed_grad):
    real_in = coefficients[:, :, 0]
    imag_in = coefficients[:, :, 1]
    real_g = mixed_grad[:, :, 0]
    imag_g = mixed_grad[:, :, 1]
    real_grad = contract('mlc,mld->lcd', real_in, real_g) + contract('mlc,mld->lcd', imag_in, imag_g)
    imag_grad = contract('mlc,mld->lcd', real_in, imag_g) - contract('mlc,mld->lcd', imag_in, real_g)
    return jnp.stack([real_grad, imag_grad], axis=1)

def disco_inputs(padded, kernel_rows, offsets):
    lat_dev = padded.shape[0] - 2 * HALO_REACH
    lon_dev = padded.shape[1] - 2 * HALO_REACH
    channels = padded.shape[2]
    running = jnp.zeros((kernel_rows.shape[1], lat_dev, lon_dev, channels), jnp.float32)
    for neighbour in range(offsets.shape[0]):
        corner = (HALO_REACH + offsets[neighbour, 0], HALO_REACH + offsets[neighbour, 1], jnp.int32(0))
        shifted = lax.dynamic_slice(padded, corner, (lat_dev, lon_dev, channels))
        running = running + kernel_rows[neighbour][:, :, None, None] * shifted[None].astype(jnp.float32)
    return running.astype(jnp.bfloat16)

def disco_back(products, kernel_padded, lat_first, offsets):
    basis_count, lat_wide, lon_wide, channels = products.shape
    lat_dev = lat_wide - 2 * HALO_REACH
    lon_dev = lon_wide - 2 * HALO_REACH
    running = jnp.zeros((lat_dev, lon_dev, channels), jnp.float32)
    for neighbour in range(offsets.shape[0]):
        lat_shift = offsets[neighbour, 0]
        lon_shift = offsets[neighbour, 1]
        weights_now = lax.dynamic_slice(kernel_padded[neighbour], (jnp.int32(0), lat_first + HALO_REACH - lat_shift), (basis_count, lat_dev))
        shifted = lax.dynamic_slice(products, (jnp.int32(0), HALO_REACH - lat_shift, HALO_REACH - lon_shift, jnp.int32(0)), (basis_count, lat_dev, lon_dev, channels))
        running = running + lax.optimization_barrier(jnp.sum(weights_now[:, :, None, None] * shifted.astype(jnp.float32), axis=0))
    return running

def pad_grid(values):
    wrapped = jnp.concatenate([values[:, -HALO_REACH:], values, values[:, :HALO_REACH]], axis=1)
    return jnp.pad(wrapped, ((HALO_REACH, HALO_REACH), (0, 0), (0, 0)))

def reference(grid_field, cotangent, analysis_table, synthesis_table, spectral_weight, disco_weight, disco_kernel, neighbour_offsets):
    analysis_legendre = unfold_halves(analysis_table)
    synthesis_legendre = unfold_halves(synthesis_table)
    degree_weight = unfold_halves(spectral_weight)
    columns = jnp.arange(LON_CELLS, dtype=jnp.int32)
    wave_ids = jnp.arange(WAVENUMBERS, dtype=jnp.int32)
    harmonic = fourier_basis(columns, wave_ids, LON_CELLS).astype(jnp.float32)
    upper_mask = (jnp.arange(DEGREES, dtype=jnp.int32)[None, :] >= wave_ids[:, None])[:, :, None, None]

    def analysis(values, legendre):
        spectra = jnp.einsum('alc,rlm->amrc', values.astype(jnp.float32), harmonic).astype(jnp.bfloat16)
        coefficients = jnp.einsum('mal,amrc->mlrc', legendre.astype(jnp.float32), spectra.astype(jnp.float32))
        return jnp.where(upper_mask, coefficients, 0.0).astype(jnp.bfloat16)

    def synthesis(degree_data, legendre):
        lat_waves = jnp.einsum('mal,mlrc->amrc', legendre.astype(jnp.float32), degree_data.astype(jnp.float32)).astype(jnp.bfloat16)
        return jnp.einsum('amrc,rlm->alc', lat_waves.astype(jnp.float32), harmonic).astype(jnp.bfloat16)
    coefficients = analysis(grid_field, analysis_legendre)
    mixed_modes = apply_mix(coefficients, degree_weight)
    spectral = synthesis(mixed_modes, synthesis_legendre)
    inputs = disco_inputs(pad_grid(grid_field), disco_kernel, neighbour_offsets)
    local_part = jnp.einsum('kabc,kcd->abd', inputs.astype(jnp.float32), disco_weight.astype(jnp.float32))
    hidden = spectral.astype(jnp.float32) + local_part
    activated, gelu_back = jax.vjp(jax.nn.gelu, hidden)
    block_output = activated.astype(jnp.bfloat16)
    upstream = cotangent.astype(jnp.float32)
    hidden_grad = gelu_back(upstream)[0].astype(jnp.bfloat16)
    mixed_grad = analysis(hidden_grad, synthesis_legendre)
    degree_grad = weight_grad(coefficients, mixed_grad)
    half_deg = DEGREES // 2
    spectral_grad = jnp.stack([degree_grad[:half_deg], jnp.flip(degree_grad[half_deg:], axis=0)])
    coefficient_grad = mix_back(mixed_grad, degree_weight)
    spectral_back = synthesis(coefficient_grad, analysis_legendre)
    products = jnp.einsum('abd,kcd->kabc', pad_grid(hidden_grad).astype(jnp.float32), disco_weight.astype(jnp.float32)).astype(jnp.bfloat16)
    kernel_padded = jnp.pad(disco_kernel, ((0, 0), (0, 0), (HALO_REACH, HALO_REACH)))
    local_back = disco_back(products, kernel_padded, jnp.int32(0), neighbour_offsets)
    field_grad = (spectral_back.astype(jnp.float32) + local_back).astype(jnp.bfloat16)
    disco_grad = jnp.einsum('kabc,abd->kcd', inputs.astype(jnp.float32), hidden_grad.astype(jnp.float32)) * (1.0 / math.sqrt(LAT_CELLS * LON_CELLS))
    return (block_output, field_grad, spectral_grad, disco_grad)
```

```python
import functools
import math

import jax
import jax.numpy as jnp
import ml_dtypes
import numpy as np
from jax import lax
from jax.experimental import pallas as pl
from jax.experimental.pallas import tpu as pltpu
from jax.sharding import Mesh
from jax.sharding import PartitionSpec as P

HALO_REACH = 2
LON_CELLS = 1440
LON_DEV = 360
CHANNELS = 384
DEGREES = 512
HALF = 256
DEVICES = 128
ALL = ("lat", "zhi", "core")
CHIPS = ("lat", "zhi")
SWAP = [(0, 1), (1, 0)]


def wave_tables():
    e, a, lh, p, ri = np.meshgrid(*map(np.arange, (64, 2, 2, 2, 2)), indexing="ij")
    e, a, lh, p, ri = (v.reshape(-1) for v in (e, a, lh, p, ri))
    cell_row = np.repeat(np.arange(2), LON_DEV)
    forward = np.zeros((2, 2, 1024, 2 * LON_DEV), np.float32)
    backward = np.zeros((2, 2, 2 * LON_DEV, 1024), np.float32)

    def basis(wave_core, cell_core):
        base = 4 * e + 2 * wave_core + p
        wave = np.where(lh == 0, base, DEGREES - 1 - base)
        column = np.tile(np.arange(LON_DEV), 2) + LON_DEV * cell_core
        angle = (wave[:, None] * column[None, :] % LON_CELLS) * (2.0 * math.pi / LON_CELLS)
        part = np.where(ri[:, None] == 0, np.cos(angle), -np.sin(angle)) / math.sqrt(LON_CELLS)
        return np.where(a[:, None] == cell_row[None, :], part, 0.0)

    for core in range(2):
        for other in range(2):
            forward[core, other] = basis(core, core ^ other)
            backward[core, other] = basis(core ^ other, core).T
    return forward.astype(ml_dtypes.bfloat16), backward.astype(ml_dtypes.bfloat16)


def coefficient_rows():
    axes = np.meshgrid(*map(np.arange, (DEVICES, 2, 2, 2, 2)), indexing="ij")
    return [v.reshape(-1) for v in axes]


def spectrum_columns():
    axes = np.meshgrid(*map(np.arange, (32, 2, 2, 2, 2, 2)), indexing="ij")
    return [v.reshape(-1) for v in axes]


def legendre_selectors():
    d, kind, p, ri, j = coefficient_rows()
    fold = 2 * d + j
    degrees = np.arange(DEGREES)
    low = degrees[None, :] == np.where(kind == 0, DEGREES - 1 - fold, fold)[:, None]
    high = (degrees[None, :] == (DEGREES - 1 - fold)[:, None]) & (kind == 1)[:, None]
    i, h, a, lh, cp, cri = spectrum_columns()
    slh, sp, sa = (v.reshape(-1) for v in np.meshgrid(*map(np.arange, (2, 2, 64)), indexing="ij"))
    spread = (
        (slh[:, None] == lh[None, :])
        & (sp[:, None] == cp[None, :])
        & (sa[:, None] == (2 * i + a)[None, :])
    )
    sign = np.where((h == 1) & ((lh ^ cp) == 1), -1.0, 1.0)
    spread = spread * sign[None, :]
    as_bf16 = lambda v: v.astype(np.float32).astype(ml_dtypes.bfloat16)
    return as_bf16(low), as_bf16(high), as_bf16(spread)


def dot(left, right):
    return jnp.dot(left, right, preferred_element_type=jnp.float32)


def dot_nt(left, right):
    return lax.dot_general(
        left, right, (((1,), (1,)), ((), ())), preferred_element_type=jnp.float32
    )


def legendre_matrices(table, rank, selectors):
    low, high, spread = selectors
    d, kind, p, ri, j = coefficient_rows()
    i, h, a, lh, cp, cri = spectrum_columns()
    lower = table[0].reshape(128, DEGREES)
    upper = table[1].reshape(128, DEGREES)
    picked = jnp.concatenate([dot_nt(low, lower), dot_nt(high, upper)], axis=1).astype(jnp.bfloat16)
    own = 2 * rank + jnp.asarray(p, jnp.int32)
    fold = jnp.asarray(2 * d + j, jnp.int32)
    row_code = jnp.asarray(2 * p + ri, jnp.int32) + 4 * (
        (jnp.asarray(kind, jnp.int32) == 1) & (own > fold)
    ).astype(jnp.int32)
    col_code = jnp.asarray(2 * cp + cri + 4 * lh, jnp.int32)
    matrix = jnp.where(row_code[:, None] == col_code[None, :], dot(picked, spread), 0.0)
    flipped = jnp.where(
        col_code[:, None] == row_code[None, :], dot_nt(jnp.asarray(spread.T), picked), 0.0
    )
    edge_p = jnp.asarray([0, 0, 1, 1], jnp.int32)
    wanted = DEGREES - 1 - (2 * rank + edge_p)
    one_hot = (jnp.arange(DEGREES, dtype=jnp.int32)[None, :] == wanted[:, None]).astype(jnp.bfloat16)
    edge = dot(dot_nt(one_hot, upper).astype(jnp.bfloat16), spread[128:])
    edge_code = jnp.arange(4, dtype=jnp.int32) + 4
    edge = jnp.where(edge_code[:, None] == col_code[None, :], edge, 0.0)
    return tuple(v.astype(jnp.bfloat16) for v in (matrix, flipped, edge))


def complex_weights(weight):
    real, imag = weight[:, :, 0], weight[:, :, 1]
    return jnp.concatenate(
        [jnp.concatenate([real, imag], axis=3), jnp.concatenate([-imag, real], axis=3)], axis=2
    )


def mix_kernel(
    rank_ref, rows_ref, edge_ref, weight_ref, order_ref, out_ref, edge_out_ref, high_ref, low_ref, mixed, *, back
):
    order = order_ref[...]
    for block in range(8):
        turned = dot(order, rows_ref[256 * block : 256 * (block + 1), :]).astype(jnp.bfloat16)
        for q in range(16):
            kind, p, ri, j = q >> 3, (q >> 2) & 1, (q >> 1) & 1, q & 1
            piece = turned[16 * q : 16 * (q + 1), :]
            row = 128 * p + 16 * block
            lanes = slice(CHANNELS * ri, CHANNELS * (ri + 1))
            if kind == 0:
                high_ref[j, row : row + 16, lanes] = piece
            else:
                low_ref[j, row : row + 16, lanes] = piece
    place = lax.broadcasted_iota(jnp.int32, (256, 2 * CHANNELS), 0)
    base = 2 * (place & 127) + (place >> 7)
    for j in range(2):
        fold = 2 * rank_ref[0] + j
        both = low_ref[j].astype(jnp.float32)
        edge = jnp.concatenate([edge_ref[2 * j : 2 * j + 1, :], edge_ref[2 * j + 1 : 2 * j + 2, :]], axis=1)
        high_ref[j, 256:512, :] = jnp.where(
            base > fold, both, jnp.where(base == fold, edge, 0.0)
        ).astype(jnp.bfloat16)
        low_ref[j] = jnp.where(base <= fold, both, 0.0).astype(jnp.bfloat16)
        product = dot_nt if back else dot
        first = product(high_ref[j, 0:256, :], weight_ref[1, j])
        mixed[0, j] = first.astype(jnp.bfloat16)
        high = product(high_ref[j, 256:512, :], weight_ref[1, j])
        low = product(low_ref[j], weight_ref[0, j])
        mixed[1, j] = jnp.where(base <= fold, low, high).astype(jnp.bfloat16)
        corner = jnp.sum(jnp.where(base == fold, high, 0.0), axis=0, keepdims=True)
        edge_out_ref[2 * j : 2 * j + 1, :] = corner[:, :CHANNELS]
        edge_out_ref[2 * j + 1 : 2 * j + 2, :] = corner[:, CHANNELS:]
    for block in range(8):
        pieces = []
        for q in range(16):
            kind, p, ri, j = q >> 3, (q >> 2) & 1, (q >> 1) & 1, q & 1
            row = 128 * p + 16 * block
            pieces.append(mixed[kind, j, row : row + 16, CHANNELS * ri : CHANNELS * (ri + 1)])
        turned = dot(order, jnp.concatenate(pieces, axis=0))
        out_ref[256 * block : 256 * (block + 1), :] = turned.astype(jnp.bfloat16)


def mix(rank, rows, edge, weights, order, back):
    shape = jax.ShapeDtypeStruct
    vmem = pl.BlockSpec(memory_space=pltpu.VMEM)
    flops = 2 * 1536 * 768 * 768 + 4 * 2048 * 256 * 384
    return pl.pallas_call(
        functools.partial(mix_kernel, back=back),
        out_shape=(
            shape((2048, CHANNELS), jnp.bfloat16),
            shape((4, CHANNELS), jnp.float32),
            shape((2, 512, 2 * CHANNELS), jnp.bfloat16),
            shape((2, 256, 2 * CHANNELS), jnp.bfloat16),
        ),
        in_specs=[pl.BlockSpec(memory_space=pltpu.SMEM)] + [vmem] * 4,
        out_specs=(vmem,) * 4,
        scratch_shapes=[pltpu.VMEM((2, 2, 256, 2 * CHANNELS), jnp.bfloat16)],
        compiler_params=pltpu.CompilerParams(vmem_limit_bytes=48 * 1024 * 1024),
        cost_estimate=pl.CostEstimate(flops=flops, bytes_accessed=12_000_000, transcendentals=0),
        name="mix_back" if back else "mix_modes",
    )(rank.reshape(1), rows, edge, weights, order)


def swap_cores(values):
    return lax.ppermute(values, "core", SWAP)


def to_wave_owners(mine, other, tables):
    partial = dot(tables[0], mine) + dot(tables[1], other)
    blocks = partial.astype(jnp.bfloat16).reshape(64, 16, CHANNELS)
    moved = lax.all_to_all(blocks, CHIPS, split_axis=0, concat_axis=0, tiled=True)
    return moved.reshape(1024, CHANNELS)


def between_degrees(rows):
    blocks = rows.reshape(DEVICES, 16, CHANNELS)
    moved = lax.all_to_all(blocks, ALL, split_axis=0, concat_axis=0, tiled=True)
    return moved.reshape(2048, CHANNELS)


def analysis(spectra, matrices):
    matrix, flipped, edge = matrices
    rows = between_degrees(dot(matrix, spectra).astype(jnp.bfloat16))
    corner = dot(edge, spectra).astype(jnp.bfloat16).astype(jnp.float32)
    return rows, corner


def synthesis(rows, corner, matrices, tables):
    matrix, flipped, edge = matrices
    corner_part = dot(edge.T, corner.astype(jnp.bfloat16))
    waves = (dot(flipped, between_degrees(rows)) + corner_part).astype(jnp.bfloat16)
    moved = lax.all_to_all(
        waves.reshape(64, 16, CHANNELS), CHIPS, split_axis=0, concat_axis=0, tiled=True
    ).reshape(1024, CHANNELS)
    return dot(tables[0], moved) + dot(tables[1], swap_cores(moved))


def with_rim(mine, other, core):
    first = core == 0
    head, tail = other[:, :HALO_REACH], other[:, LON_DEV - HALO_REACH :]
    far = lax.ppermute(jnp.where(first, tail, head), "zhi", SWAP)
    near = jnp.where(first, head, tail)
    wide = jnp.concatenate([jnp.where(first, far, near), mine, jnp.where(first, near, far)], axis=1)
    above = lax.ppermute(wide, "lat", [(i, i + 1) for i in range(31)])
    below = lax.ppermute(wide, "lat", [(i + 1, i) for i in range(31)])
    return jnp.concatenate([above, wide, below], axis=0)


def stencil(padded, weights, rows, columns):
    running = jnp.zeros((4, 2, LON_DEV, CHANNELS), jnp.float32)
    for neighbour in range(len(weights)):
        corner = (rows[neighbour], columns[neighbour], jnp.int32(0))
        shifted = lax.dynamic_slice(padded, corner, (2, LON_DEV, CHANNELS))
        running = running + weights[neighbour][:, :, None, None] * shifted[None].astype(jnp.float32)
    return running.astype(jnp.bfloat16)


def local(
    grid_field,
    cotangent,
    analysis_table,
    synthesis_table,
    spectral_weight,
    disco_weight,
    disco_kernel,
    neighbour_offsets,
    *,
    forward_all,
    backward_all,
    selectors,
    order,
):
    lat, zhi, core = (lax.axis_index(name) for name in ALL)
    rank = lat * 4 + zhi * 2 + core
    lat_first = lat * 2
    neighbours = neighbour_offsets.shape[0]
    forward_tables = lax.dynamic_index_in_dim(jnp.asarray(forward_all), core, 0, keepdims=False)
    backward_tables = lax.dynamic_index_in_dim(jnp.asarray(backward_all), core, 0, keepdims=False)
    order = jnp.asarray(order)
    flat = (2 * LON_DEV, CHANNELS)
    grid = (2, LON_DEV, CHANNELS)

    mine = grid_field.reshape(flat)
    other = swap_cores(mine)
    spectra = to_wave_owners(mine, other, forward_tables)
    analysis_parts = legendre_matrices(analysis_table, rank, selectors)
    synthesis_parts = legendre_matrices(synthesis_table, rank, selectors)
    weights = complex_weights(spectral_weight)
    rows, corner = analysis(spectra, analysis_parts)
    mixed, mixed_corner, modes_high, modes_low = mix(rank, rows, corner, weights, order, False)
    spectral = synthesis(mixed, mixed_corner, synthesis_parts, backward_tables)

    padded = with_rim(grid_field, other.reshape(grid), core)
    kernel_rows = lax.dynamic_slice_in_dim(disco_kernel, lat_first, 2, 2)
    row_shift = neighbour_offsets[:, 0]
    col_shift = neighbour_offsets[:, 1]
    inputs = stencil(
        padded,
        [kernel_rows[n] for n in range(neighbours)],
        [HALO_REACH + row_shift[n] for n in range(neighbours)],
        [HALO_REACH + col_shift[n] for n in range(neighbours)],
    )
    local_part = jnp.einsum(
        "kabc,kcd->abd", inputs, disco_weight, preferred_element_type=jnp.float32
    )
    hidden = spectral.astype(jnp.bfloat16).astype(jnp.float32).reshape(grid) + local_part
    activated, gelu_back = jax.vjp(jax.nn.gelu, hidden)
    block_output = activated.astype(jnp.bfloat16)
    hidden_grad = gelu_back(cotangent.astype(jnp.float32))[0].astype(jnp.bfloat16)

    grad_mine = hidden_grad.reshape(flat)
    grad_other = swap_cores(grad_mine)
    grad_spectra = to_wave_owners(grad_mine, grad_other, forward_tables)
    grad_rows, grad_corner = analysis(grad_spectra, synthesis_parts)
    back, back_corner, grads_high, grads_low = mix(
        rank, grad_rows, grad_corner, weights, order, True
    )
    spectral_back = synthesis(back, back_corner, analysis_parts, backward_tables)

    outer = "jrx,jry->jxy"
    high = jnp.einsum(outer, modes_high, grads_high, preferred_element_type=jnp.float32)
    low = jnp.einsum(outer, modes_low, grads_low, preferred_element_type=jnp.float32)

    def parts(both):
        c = CHANNELS
        real = both[:, :c, :c] + both[:, c:, c:]
        imag = both[:, :c, c:] - both[:, c:, :c]
        return jnp.stack([real, imag], axis=1)

    spectral_grad = jnp.stack([parts(low), parts(high)])

    local_grad = jnp.einsum(
        "kabc,abd->kcd", inputs, hidden_grad, preferred_element_type=jnp.float32
    ) * (1.0 / math.sqrt(64 * LON_CELLS))
    halves = local_grad.reshape(2, 2 * CHANNELS, CHANNELS)
    kept = lax.dynamic_index_in_dim(halves, core, 0, keepdims=False)
    given = lax.dynamic_index_in_dim(halves, 1 - core, 0, keepdims=False)
    summed = lax.psum(kept + swap_cores(given), CHIPS)
    summed_other = swap_cores(summed)
    disco_grad = jnp.where(
        core == 0, jnp.stack([summed, summed_other]), jnp.stack([summed_other, summed])
    ).reshape(4, CHANNELS, CHANNELS)

    padded_grad = with_rim(hidden_grad, grad_other.reshape(grid), core)
    kernel_padded = jnp.pad(disco_kernel, ((0, 0), (0, 0), (HALO_REACH, HALO_REACH)))
    back_inputs = stencil(
        padded_grad,
        [
            lax.dynamic_slice(
                kernel_padded[n], (jnp.int32(0), lat_first + HALO_REACH - row_shift[n]), (4, 2)
            )
            for n in range(neighbours)
        ],
        [HALO_REACH - row_shift[n] for n in range(neighbours)],
        [HALO_REACH - col_shift[n] for n in range(neighbours)],
    )
    local_back = jnp.einsum(
        "kabd,kcd->abc", back_inputs, disco_weight, preferred_element_type=jnp.float32
    )
    field_grad = (
        spectral_back.astype(jnp.bfloat16).astype(jnp.float32).reshape(grid) + local_back
    ).astype(jnp.bfloat16)
    return (block_output, field_grad, spectral_grad, disco_grad)


def solution(mesh):
    forward_all, backward_all = wave_tables()
    low, high, spread = legendre_selectors()
    place = np.arange(256)
    order = (place[:, None] == (place % 16 * 16 + place // 16)[None, :]).astype(ml_dtypes.bfloat16)
    split = Mesh(mesh.devices.reshape(32, 2, 2), ALL)
    lon = ("zhi", "core")
    return jax.shard_map(
        functools.partial(
            local,
            forward_all=forward_all,
            backward_all=backward_all,
            selectors=(low, high, spread),
            order=order,
        ),
        mesh=split,
        in_specs=(
            P("lat", lon, None),
            P("lat", lon, None),
            P(None, ALL, None, None),
            P(None, ALL, None, None),
            P(None, ALL, None, None, None),
            P(),
            P(),
            P(),
        ),
        out_specs=(
            P("lat", lon, None),
            P("lat", lon, None),
            P(None, ALL, None, None, None),
            P(),
        ),
        check_vma=False,
    )
```

```python
import functools
import math

import jax
import jax.numpy as jnp
import ml_dtypes
import numpy as np
from jax import lax
from jax.experimental import pallas as pl
from jax.experimental.pallas import tpu as pltpu
from jax.sharding import Mesh
from jax.sharding import PartitionSpec as P

HALO_REACH = 2
LON_CELLS = 1440
LON_DEV = 360
CHANNELS = 384
DEGREES = 512
HALF = 256
DEVICES = 128
ALL = ("lat", "zhi", "core")
CHIPS = ("lat", "zhi")
SWAP = [(0, 1), (1, 0)]


def wave_tables():
    e, lh, p, ri = np.meshgrid(*map(np.arange, (64, 2, 2, 2)), indexing="ij")
    e, lh, p, ri = (v.reshape(-1) for v in (e, lh, p, ri))
    forward = np.zeros((2, 2, 512, LON_DEV), np.float32)
    backward = np.zeros((2, 2, LON_DEV, 512), np.float32)

    def basis(wave_core, cell_core):
        base = 4 * e + 2 * wave_core + p
        wave = np.where(lh == 0, base, DEGREES - 1 - base)
        column = np.arange(LON_DEV) + LON_DEV * cell_core
        angle = (wave[:, None] * column[None, :] % LON_CELLS) * (2.0 * math.pi / LON_CELLS)
        return np.where(ri[:, None] == 0, np.cos(angle), -np.sin(angle)) / math.sqrt(LON_CELLS)

    for core in range(2):
        for other in range(2):
            forward[core, other] = basis(core, core ^ other)
            backward[core, other] = basis(core ^ other, core).T
    return forward.astype(ml_dtypes.bfloat16), backward.astype(ml_dtypes.bfloat16)


def coefficient_rows():
    axes = np.meshgrid(*map(np.arange, (DEVICES, 2, 2, 2, 2)), indexing="ij")
    return [v.reshape(-1) for v in axes]


def spectrum_columns():
    axes = np.meshgrid(*map(np.arange, (32, 2, 2, 2, 2, 2)), indexing="ij")
    return [v.reshape(-1) for v in axes]


def legendre_selectors():
    d, kind, p, ri, j = coefficient_rows()
    fold = 2 * d + j
    degrees = np.arange(DEGREES)
    low = degrees[None, :] == np.where(kind == 0, DEGREES - 1 - fold, fold)[:, None]
    high = (degrees[None, :] == (DEGREES - 1 - fold)[:, None]) & (kind == 1)[:, None]
    i, h, a, lh, cp, cri = spectrum_columns()
    slh, sp, sa = (v.reshape(-1) for v in np.meshgrid(*map(np.arange, (2, 2, 64)), indexing="ij"))
    spread = (
        (slh[:, None] == lh[None, :])
        & (sp[:, None] == cp[None, :])
        & (sa[:, None] == (2 * i + a)[None, :])
    )
    sign = np.where((h == 1) & ((lh ^ cp) == 1), -1.0, 1.0)
    spread = spread * sign[None, :]
    as_bf16 = lambda v: v.astype(np.float32).astype(ml_dtypes.bfloat16)
    return as_bf16(low), as_bf16(high), as_bf16(spread)


def dot(left, right):
    return jnp.dot(left, right, preferred_element_type=jnp.float32)


def dot_nt(left, right):
    return lax.dot_general(
        left, right, (((1,), (1,)), ((), ())), preferred_element_type=jnp.float32
    )


def legendre_matrices(table, rank, selectors):
    low, high, spread = selectors
    d, kind, p, ri, j = coefficient_rows()
    i, h, a, lh, cp, cri = spectrum_columns()
    lower = table[0].reshape(128, DEGREES)
    upper = table[1].reshape(128, DEGREES)
    picked = jnp.concatenate([dot_nt(low, lower), dot_nt(high, upper)], axis=1).astype(jnp.bfloat16)
    own = 2 * rank + jnp.asarray(p, jnp.int32)
    fold = jnp.asarray(2 * d + j, jnp.int32)
    row_code = jnp.asarray(2 * p + ri, jnp.int32) + 4 * (
        (jnp.asarray(kind, jnp.int32) == 1) & (own > fold)
    ).astype(jnp.int32)
    col_code = jnp.asarray(2 * cp + cri + 4 * lh, jnp.int32)
    matrix = jnp.where(row_code[:, None] == col_code[None, :], dot(picked, spread), 0.0)
    flipped = jnp.where(
        col_code[:, None] == row_code[None, :], dot_nt(jnp.asarray(spread.T), picked), 0.0
    )
    edge_p = jnp.asarray([0, 0, 1, 1], jnp.int32)
    wanted = DEGREES - 1 - (2 * rank + edge_p)
    one_hot = (jnp.arange(DEGREES, dtype=jnp.int32)[None, :] == wanted[:, None]).astype(jnp.bfloat16)
    edge = dot(dot_nt(one_hot, upper).astype(jnp.bfloat16), spread[128:])
    edge_code = jnp.arange(4, dtype=jnp.int32) + 4
    edge = jnp.where(edge_code[:, None] == col_code[None, :], edge, 0.0)
    return lax.optimization_barrier(tuple(v.astype(jnp.bfloat16) for v in (matrix, flipped, edge)))


def complex_weights(weight):
    real, imag = weight[:, :, 0], weight[:, :, 1]
    return jnp.concatenate(
        [jnp.concatenate([real, imag], axis=3), jnp.concatenate([-imag, real], axis=3)], axis=2
    )


def mix_kernel(
    rank_ref, rows_ref, edge_ref, weight_ref, order_ref, out_ref, edge_out_ref, high_ref, low_ref, mixed, *, back
):
    order = order_ref[...]
    for block in range(8):
        rows = rows_ref[16 * block : 16 * (block + 1), 0:16, :].reshape(256, CHANNELS)
        turned = dot(order, rows).astype(jnp.bfloat16)
        for q in range(16):
            kind, p, ri, j = q >> 3, (q >> 2) & 1, (q >> 1) & 1, q & 1
            piece = turned[16 * q : 16 * (q + 1), :]
            row = 128 * p + 16 * block
            lanes = slice(CHANNELS * ri, CHANNELS * (ri + 1))
            if kind == 0:
                high_ref[j, row : row + 16, lanes] = piece
            else:
                low_ref[j, row : row + 16, lanes] = piece
    place = lax.broadcasted_iota(jnp.int32, (256, 2 * CHANNELS), 0)
    base = 2 * (place & 127) + (place >> 7)
    for j in range(2):
        fold = 2 * rank_ref[0] + j
        both = low_ref[j].astype(jnp.float32)
        edge = jnp.concatenate([edge_ref[2 * j : 2 * j + 1, :], edge_ref[2 * j + 1 : 2 * j + 2, :]], axis=1)
        high_ref[j, 256:512, :] = jnp.where(
            base > fold, both, jnp.where(base == fold, edge, 0.0)
        ).astype(jnp.bfloat16)
        low_ref[j] = jnp.where(base <= fold, both, 0.0).astype(jnp.bfloat16)
        product = dot_nt if back else dot
        first = product(high_ref[j, 0:256, :], weight_ref[1, j])
        mixed[0, j] = first.astype(jnp.bfloat16)
        high = product(high_ref[j, 256:512, :], weight_ref[1, j])
        low = product(low_ref[j], weight_ref[0, j])
        mixed[1, j] = jnp.where(base <= fold, low, high).astype(jnp.bfloat16)
        corner = jnp.sum(jnp.where(base == fold, high, 0.0), axis=0, keepdims=True)
        edge_out_ref[2 * j : 2 * j + 1, :] = corner[:, :CHANNELS]
        edge_out_ref[2 * j + 1 : 2 * j + 2, :] = corner[:, CHANNELS:]
    for block in range(8):
        pieces = []
        for q in range(16):
            kind, p, ri, j = q >> 3, (q >> 2) & 1, (q >> 1) & 1, q & 1
            row = 128 * p + 16 * block
            pieces.append(mixed[kind, j, row : row + 16, CHANNELS * ri : CHANNELS * (ri + 1)])
        turned = dot(order, jnp.concatenate(pieces, axis=0))
        out_ref[256 * block : 256 * (block + 1), :] = turned.astype(jnp.bfloat16)


def mix(rank, rows, edge, weights, order, back):
    shape = jax.ShapeDtypeStruct
    vmem = pl.BlockSpec(memory_space=pltpu.VMEM)
    flops = 2 * 1536 * 768 * 768 + 4 * 2048 * 256 * 384
    return pl.pallas_call(
        functools.partial(mix_kernel, back=back),
        out_shape=(
            shape((2048, CHANNELS), jnp.bfloat16),
            shape((4, CHANNELS), jnp.float32),
            shape((2, 512, 2 * CHANNELS), jnp.bfloat16),
            shape((2, 256, 2 * CHANNELS), jnp.bfloat16),
        ),
        in_specs=[pl.BlockSpec(memory_space=pltpu.SMEM)] + [vmem] * 4,
        out_specs=(vmem,) * 4,
        scratch_shapes=[pltpu.VMEM((2, 2, 256, 2 * CHANNELS), jnp.bfloat16)],
        compiler_params=pltpu.CompilerParams(vmem_limit_bytes=48 * 1024 * 1024),
        cost_estimate=pl.CostEstimate(flops=flops, bytes_accessed=12_000_000, transcendentals=0),
        name="mix_back" if back else "mix_modes",
    )(rank.reshape(1), rows, edge, weights, order)


def forward_kernel(table_ref, mine_ref, other_ref, out_ref):
    for part in range(4):
        rows = slice(128 * part, 128 * (part + 1))
        lines = []
        for a in range(2):
            sums = dot(table_ref[0, rows, :], mine_ref[a]) + dot(table_ref[1, rows, :], other_ref[a])
            lines.append(sums.reshape(16, 8, CHANNELS))
        out_ref[16 * part : 16 * (part + 1)] = jnp.concatenate(lines, axis=1).astype(jnp.bfloat16)


def inverse_rows(table_ref, mine, other, a):
    def pick(waves):
        return waves[:, 8 * a : 8 * (a + 1), :].reshape(512, CHANNELS).astype(jnp.bfloat16)

    sums = dot(table_ref[0], pick(mine)) + dot(table_ref[1], pick(other))
    return sums.astype(jnp.bfloat16).astype(jnp.float32)


def activate_kernel(table_ref, mine_ref, other_ref, local_ref, cotangent_ref, out_ref, grad_ref):
    mine = mine_ref[:, 0:16, :].astype(jnp.float32)
    other = other_ref[:, 0:16, :].astype(jnp.float32)
    scale = math.sqrt(2.0 / math.pi)
    for a in range(2):
        v = inverse_rows(table_ref, mine, other, a) + local_ref[a]
        square = v * v
        t = jnp.tanh(scale * (v + 0.044715 * (v * square)))
        half = 0.5 * (1.0 + t)
        out_ref[a] = (v * half).astype(jnp.bfloat16)
        slope = half + 0.5 * v * (1.0 - t * t) * (scale * (1.0 + 3 * 0.044715 * square))
        grad_ref[a] = (cotangent_ref[a].astype(jnp.float32) * slope).astype(jnp.bfloat16)


def finish_kernel(table_ref, mine_ref, other_ref, local_ref, out_ref):
    mine = mine_ref[:, 0:16, :].astype(jnp.float32)
    other = other_ref[:, 0:16, :].astype(jnp.float32)
    for a in range(2):
        total = inverse_rows(table_ref, mine, other, a) + local_ref[a]
        out_ref[a] = total.astype(jnp.bfloat16)


MARGIN = 8
CHUNK = 40


def stencil_kernel(
    weight_ref,
    corner_ref,
    above_ref,
    mine_ref,
    below_ref,
    left_ref,
    right_ref,
    out_ref,
    line,
    shifted,
    sums,
):
    blocks = (above_ref, mine_ref, below_ref)
    for row in range(6):
        line[MARGIN : MARGIN + LON_DEV, :] = blocks[row // 2][row % 2].astype(jnp.float32)
        line[MARGIN - HALO_REACH : MARGIN, :] = left_ref[row]
        line[MARGIN + LON_DEV : MARGIN + LON_DEV + HALO_REACH, :] = right_ref[row]
        for shift in range(5):
            first = MARGIN - HALO_REACH + shift
            shifted[shift, row] = line[first : first + LON_DEV, :]

    def step(index, carry):
        first = pl.multiple_of(index * CHUNK, 8)
        for a in range(2):
            for lane in range(3):
                lanes = slice(128 * lane, 128 * (lane + 1))
                totals = [jnp.zeros((CHUNK, 128), jnp.float32)] * 4
                for n in range(9):
                    row = corner_ref[2 * n] + HALO_REACH + a
                    column = corner_ref[2 * n + 1] + HALO_REACH
                    cells = shifted[column, row, pl.ds(first, CHUNK), lanes]
                    totals = [totals[k] + weight_ref[8 * n + 2 * k + a] * cells for k in range(4)]
                for k in range(4):
                    sums[k, a, pl.ds(first, CHUNK), lanes] = totals[k]
        return carry

    lax.fori_loop(0, LON_DEV // CHUNK, step, 0)
    for k in range(4):
        for a in range(2):
            out_ref[k, a] = sums[k, a].astype(jnp.bfloat16)


def outer_kernel(high_ref, high_grad_ref, low_ref, low_grad_ref, out_ref):
    c = CHANNELS
    for kind, (left_ref, right_ref) in enumerate(((low_ref, low_grad_ref), (high_ref, high_grad_ref))):
        for j in range(2):
            right = right_ref[j]
            across = (((0,), (0,)), ((), ()))
            first = lax.dot_general(
                left_ref[j, :, :c], right, across, preferred_element_type=jnp.float32
            )
            second = lax.dot_general(
                left_ref[j, :, c:], right, across, preferred_element_type=jnp.float32
            )
            out_ref[kind, j, 0] = first[:, :c] + second[:, c:]
            out_ref[kind, j, 1] = first[:, c:] - second[:, :c]


def on_device(kernel, shapes, operands, name, flops, scalars=0, scratch=()):
    vmem = pl.BlockSpec(memory_space=pltpu.VMEM)
    smem = pl.BlockSpec(memory_space=pltpu.SMEM)
    shapes = [jax.ShapeDtypeStruct(*s) for s in shapes]
    moved = sum(math.prod(v.shape) * v.dtype.itemsize for v in [*shapes, *operands])
    return pl.pallas_call(
        kernel,
        out_shape=tuple(shapes),
        in_specs=[smem] * scalars + [vmem] * (len(operands) - scalars),
        out_specs=(vmem,) * len(shapes),
        scratch_shapes=list(scratch),
        compiler_params=pltpu.CompilerParams(vmem_limit_bytes=48 * 1024 * 1024),
        cost_estimate=pl.CostEstimate(flops=flops, bytes_accessed=moved, transcendentals=0),
        name=name,
    )(*operands)


BLOCK = (2, LON_DEV, CHANNELS)
WAVE_FLOPS = 2 * 512 * 720 * 768


def swap_cores(values):
    return lax.ppermute(values, "core", SWAP)


def to_wave_owners(mine, other, table):
    shapes = [((64, 16, CHANNELS), jnp.bfloat16)]
    (blocks,) = on_device(forward_kernel, shapes, (table, mine, other), "to_waves", WAVE_FLOPS)
    moved = lax.all_to_all(blocks, CHIPS, split_axis=0, concat_axis=0, tiled=True)
    return moved.reshape(1024, CHANNELS)


def between_degrees(blocks):
    return lax.all_to_all(blocks, ALL, split_axis=0, concat_axis=0, tiled=True)


def analysis(spectra, matrices, rider=None):
    matrix, flipped, edge = matrices
    blocks = dot(matrix, spectra).astype(jnp.bfloat16).reshape(DEVICES, 16, CHANNELS)
    if rider is not None:
        blocks = jnp.concatenate([blocks, rider], axis=1)
    rows = between_degrees(blocks)
    corner = dot(edge, spectra).astype(jnp.bfloat16).astype(jnp.float32)
    return rows, corner


def synthesis(rows, corner, matrices, make_rider=None):
    matrix, flipped, edge = matrices
    corner_part = dot(edge.T, corner.astype(jnp.bfloat16))
    back = between_degrees(rows.reshape(DEVICES, 16, CHANNELS)).reshape(2048, CHANNELS)
    waves = (dot(flipped, back) + corner_part).astype(jnp.bfloat16).reshape(64, 16, CHANNELS)
    if make_rider is not None:
        waves = jnp.concatenate([waves, make_rider], axis=1)
    return lax.all_to_all(waves, CHIPS, split_axis=0, concat_axis=0, tiled=True)


def stencil(block, disco_kernel, offsets, lat_first, sign):
    above = lax.ppermute(block, "lat", [(i, i + 1) for i in range(31)])
    below = lax.ppermute(block, "lat", [(i + 1, i) for i in range(31)])
    tails = [v[:, LON_DEV - HALO_REACH :] for v in (above, block, below)]
    heads = [v[:, :HALO_REACH] for v in (above, block, below)]
    lon = ("zhi", "core")
    left = lax.ppermute(jnp.concatenate(tails), lon, [(i, (i + 1) % 4) for i in range(4)])
    right = lax.ppermute(jnp.concatenate(heads), lon, [((i + 1) % 4, i) for i in range(4)])
    row = lat_first + jnp.arange(2, dtype=jnp.int32)[None, :]
    if sign < 0:
        row = row - offsets[:, :1]
    else:
        row = row + jnp.zeros_like(offsets[:, :1])
    chosen = row[:, :, None] == jnp.arange(64, dtype=jnp.int32)[None, None, :]
    weights = jnp.sum(
        jnp.where(chosen[:, None], disco_kernel[:, :, None, :], 0.0), axis=-1
    ).reshape(-1)
    operands = (
        weights,
        (sign * offsets).reshape(-1),
        above,
        block,
        below,
        left.astype(jnp.float32),
        right.astype(jnp.float32),
    )
    scratch = [
        pltpu.VMEM((LON_DEV + 2 * MARGIN, CHANNELS), jnp.float32),
        pltpu.VMEM((5, 6, LON_DEV, CHANNELS), jnp.float32),
        pltpu.VMEM((4, *BLOCK), jnp.float32),
    ]
    shapes = [((4, *BLOCK), jnp.bfloat16)]
    name = "stencil" if sign > 0 else "stencil_back"
    flops = 2 * 36 * math.prod(BLOCK) * 16
    return on_device(stencil_kernel, shapes, operands, name, flops, 2, scratch)[0]


def local(
    grid_field,
    cotangent,
    analysis_table,
    synthesis_table,
    spectral_weight,
    disco_weight,
    disco_kernel,
    neighbour_offsets,
    *,
    forward_all,
    backward_all,
    selectors,
    order,
):
    lat, zhi, core = (lax.axis_index(name) for name in ALL)
    rank = lat * 4 + zhi * 2 + core
    lat_first = lat * 2
    forward_table = lax.dynamic_index_in_dim(jnp.asarray(forward_all), core, 0, keepdims=False)
    backward_table = lax.dynamic_index_in_dim(jnp.asarray(backward_all), core, 0, keepdims=False)
    order = jnp.asarray(order)
    block_shapes = [(BLOCK, jnp.bfloat16)]

    spectra = to_wave_owners(grid_field, swap_cores(grid_field), forward_table)
    inputs = stencil(grid_field, disco_kernel, neighbour_offsets, lat_first, 1)
    local_part = jnp.einsum(
        "kabc,kcd->abd", inputs, disco_weight, preferred_element_type=jnp.float32
    )
    analysis_parts = legendre_matrices(analysis_table, rank, selectors)
    synthesis_parts = legendre_matrices(synthesis_table, rank, selectors)
    weights = complex_weights(spectral_weight)
    rows, corner = analysis(spectra, analysis_parts)
    mixed, mixed_corner, modes_high, modes_low = mix(rank, rows, corner, weights, order, False)
    waves = synthesis(mixed, mixed_corner, synthesis_parts)
    block_output, hidden_grad = on_device(
        activate_kernel,
        block_shapes * 2,
        (backward_table, waves, swap_cores(waves), local_part, cotangent),
        "activate",
        WAVE_FLOPS,
    )

    grad_spectra = to_wave_owners(hidden_grad, swap_cores(hidden_grad), forward_table)
    local_grad = jnp.einsum(
        "kabc,abd->kcd", inputs, hidden_grad, preferred_element_type=jnp.float32
    ) * (1.0 / math.sqrt(64 * LON_CELLS))
    halves = local_grad.reshape(2, 2 * CHANNELS, CHANNELS)
    kept = lax.dynamic_index_in_dim(halves, core, 0, keepdims=False)
    given = lax.dynamic_index_in_dim(halves, 1 - core, 0, keepdims=False)
    rider = (kept + swap_cores(given)).astype(jnp.bfloat16).reshape(96, 8, CHANNELS)
    rider = jnp.pad(rider, ((0, 32), (0, 0), (0, 0)))

    grad_rows, grad_corner = analysis(grad_spectra, synthesis_parts, rider)
    back, back_corner, grads_high, grads_low = mix(
        rank, grad_rows, grad_corner, weights, order, True
    )
    shares = grad_rows[:, 16:].reshape(64, 16, CHANNELS).astype(jnp.float32)
    owned = jnp.sum(shares, axis=0).astype(jnp.bfloat16)
    waves_back = synthesis(
        back, back_corner, analysis_parts, jnp.broadcast_to(owned[None], (64, 16, CHANNELS))
    )

    (spectral_grad,) = on_device(
        outer_kernel,
        [((2, 2, 2, CHANNELS, CHANNELS), jnp.float32)],
        (modes_high, grads_high, modes_low, grads_low),
        "outer",
        2 * 1536 * 768 * 768,
    )
    back_inputs = stencil(hidden_grad, disco_kernel, neighbour_offsets, lat_first, -1)
    local_back = jnp.einsum(
        "kabd,kcd->abc", back_inputs, disco_weight, preferred_element_type=jnp.float32
    )
    waves_other = swap_cores(waves_back)
    (field_grad,) = on_device(
        finish_kernel,
        block_shapes,
        (backward_table, waves_back, waves_other, local_back),
        "finish",
        WAVE_FLOPS,
    )
    mine_sums = waves_back[:48, 16:].reshape(48, 2, 8, CHANNELS)
    other_sums = waves_other[:48, 16:].reshape(48, 2, 8, CHANNELS)
    first = jnp.where(core == 0, mine_sums, other_sums)
    second = jnp.where(core == 0, other_sums, mine_sums)
    disco_grad = (
        jnp.stack([first, second], axis=1)
        .transpose(2, 0, 1, 3, 4)
        .reshape(4, CHANNELS, CHANNELS)
        .astype(jnp.float32)
    )
    return (block_output, field_grad, spectral_grad, disco_grad)


def solution(mesh):
    forward_all, backward_all = wave_tables()
    low, high, spread = legendre_selectors()
    place = np.arange(256)
    order = (place[:, None] == (place % 16 * 16 + place // 16)[None, :]).astype(ml_dtypes.bfloat16)
    split = Mesh(mesh.devices.reshape(32, 2, 2), ALL)
    lon = ("zhi", "core")
    return jax.shard_map(
        functools.partial(
            local,
            forward_all=forward_all,
            backward_all=backward_all,
            selectors=(low, high, spread),
            order=order,
        ),
        mesh=split,
        in_specs=(
            P("lat", lon, None),
            P("lat", lon, None),
            P(None, ALL, None, None),
            P(None, ALL, None, None),
            P(None, ALL, None, None, None),
            P(),
            P(),
            P(),
        ),
        out_specs=(
            P("lat", lon, None),
            P("lat", lon, None),
            P(None, ALL, None, None, None),
            P(),
        ),
        check_vma=False,
    )
```

```python
import functools
import math

import jax
import jax.numpy as jnp
import ml_dtypes
import numpy as np
from jax import lax
from jax.experimental import pallas as pl
from jax.experimental.pallas import tpu as pltpu
from jax.sharding import Mesh
from jax.sharding import PartitionSpec as P

HALO_REACH = 2
LON_CELLS = 1440
LON_DEV = 360
CHANNELS = 384
DEGREES = 512
HALF = 256
DEVICES = 128
ALL = ("lat", "zhi", "core")
CHIPS = ("lat", "zhi")
SWAP = [(0, 1), (1, 0)]


def wave_tables():
    e, lh, p, ri = np.meshgrid(*map(np.arange, (64, 2, 2, 2)), indexing="ij")
    e, lh, p, ri = (v.reshape(-1) for v in (e, lh, p, ri))
    forward = np.zeros((2, 2, 512, LON_DEV), np.float32)
    backward = np.zeros((2, 2, LON_DEV, 512), np.float32)

    def basis(wave_core, cell_core):
        base = 4 * e + 2 * wave_core + p
        wave = np.where(lh == 0, base, DEGREES - 1 - base)
        column = np.arange(LON_DEV) + LON_DEV * cell_core
        angle = (wave[:, None] * column[None, :] % LON_CELLS) * (2.0 * math.pi / LON_CELLS)
        return np.where(ri[:, None] == 0, np.cos(angle), -np.sin(angle)) / math.sqrt(LON_CELLS)

    for core in range(2):
        for other in range(2):
            forward[core, other] = basis(core, core ^ other)
            backward[core, other] = basis(core ^ other, core).T
    return forward.astype(ml_dtypes.bfloat16), backward.astype(ml_dtypes.bfloat16)


def spread_matrix():
    row, lh, cp, cri = (
        v.reshape(-1) for v in np.meshgrid(*map(np.arange, (64, 2, 2, 2)), indexing="ij")
    )
    slh, sp, sa = (v.reshape(-1) for v in np.meshgrid(*map(np.arange, (2, 2, 64)), indexing="ij"))
    spread = (
        (slh[:, None] == lh[None, :]) & (sp[:, None] == cp[None, :]) & (sa[:, None] == row[None, :])
    )
    return spread.astype(np.float32).astype(ml_dtypes.bfloat16)


def tie(*values):
    return lax.optimization_barrier(values)


def dot(left, right):
    return jnp.dot(left, right, preferred_element_type=jnp.float32)


def dot_nt(left, right):
    return lax.dot_general(
        left, right, (((1,), (1,)), ((), ())), preferred_element_type=jnp.float32
    )


def one_hot(wanted, shape):
    degree = lax.broadcasted_iota(jnp.int32, shape, 1)
    return jnp.where(degree == wanted, 1.0, 0.0).astype(jnp.bfloat16)


def keep(rows, cols, values):
    return jnp.where(rows == cols, values, 0.0).astype(jnp.bfloat16)


def legendre_kernel(
    rank_ref, table_ref, spread_ref, turned_ref, matrix_ref, flipped_ref, edge_ref, edge_flip_ref
):
    rank = rank_ref[0]
    lower = table_ref[0].reshape(128, DEGREES)
    upper = table_ref[1].reshape(128, DEGREES)
    spread = spread_ref[...]
    turned = turned_ref[...]

    def attributes(place):
        p, kind = (place >> 2) & 1, (place >> 3) & 1
        fold = 2 * (place >> 4) + (place & 1)
        high = jnp.where(2 * rank + p > fold, kind, 0)
        return kind, fold, ((place >> 1) & 3) + 4 * high

    for block in range(8):
        rows = slice(256 * block, 256 * (block + 1))
        place = lax.broadcasted_iota(jnp.int32, (256, 1), 0) + 256 * block
        kind, fold, code = attributes(place)
        last = DEGREES - 1 - fold
        low = one_hot(jnp.where(kind == 0, last, fold), (256, DEGREES))
        high = one_hot(jnp.where(kind == 0, -1, last), (256, DEGREES))
        picked = jnp.concatenate([dot_nt(low, lower), dot_nt(high, upper)], axis=1)
        picked = picked.astype(jnp.bfloat16)
        column = lax.broadcasted_iota(jnp.int32, (1, 512), 1) & 7
        matrix_ref[rows, :] = keep(code, column, dot(picked, spread))
        _, _, across = attributes(lax.broadcasted_iota(jnp.int32, (1, 256), 1) + 256 * block)
        down = lax.broadcasted_iota(jnp.int32, (512, 1), 0) & 7
        flipped_ref[:, rows] = keep(down, across, dot_nt(turned, picked))
    place = lax.broadcasted_iota(jnp.int32, (16, 1), 0)
    wanted = jnp.where(place < 4, DEGREES - 1 - (2 * rank + (place >> 1)), -1)
    edge = dot_nt(one_hot(wanted, (16, DEGREES)), upper).astype(jnp.bfloat16)
    column = lax.broadcasted_iota(jnp.int32, (1, 512), 1) & 7
    edge_ref[...] = keep(place + 4, column, dot(edge, spread[128:]))
    across = lax.broadcasted_iota(jnp.int32, (1, 16), 1) + 4
    down = lax.broadcasted_iota(jnp.int32, (512, 1), 0) & 7
    edge_flip_ref[...] = keep(down, across, dot_nt(turned[:, 128:], edge))


def chip_signs():
    line = lax.broadcasted_iota(jnp.int32, (1, 16, CHANNELS), 1)
    odd = ((line >> 2) ^ (line >> 1)) & 1
    return jnp.where(odd == 1, -1.0, 1.0)


def to_coefficients_kernel(matrix_ref, edge_ref, spectra_ref, *refs):
    rider_ref, out_ref, corner_ref = refs if len(refs) == 3 else (None, *refs)
    both = spectra_ref[...].astype(jnp.float32)
    spectra = (both[:, 0] + chip_signs() * both[:, 1]).reshape(512, CHANNELS).astype(jnp.bfloat16)
    for block in range(8):
        sums = dot(matrix_ref[256 * block : 256 * (block + 1), :], spectra)
        places = slice(16 * block, 16 * (block + 1))
        out_ref[places, 0:16, :] = sums.astype(jnp.bfloat16).reshape(16, 16, CHANNELS)
    if rider_ref is not None:
        out_ref[0:96, 16:24, :] = rider_ref[...]
        out_ref[96:128, 16:24, :] = jnp.zeros((32, 8, CHANNELS), jnp.bfloat16)
    corner = dot(edge_ref[...], spectra).astype(jnp.bfloat16)
    corner_ref[...] = corner.astype(jnp.float32)


def to_waves_kernel(flipped_ref, edge_flip_ref, rows_ref, corner_ref, *refs):
    rider_ref, out_ref = refs if len(refs) == 2 else (None, *refs)
    rows = rows_ref[...].reshape(2048, CHANNELS)
    waves = dot(flipped_ref[...], rows) + dot(
        edge_flip_ref[...], corner_ref[...].astype(jnp.bfloat16)
    )
    waves = waves.reshape(32, 16, CHANNELS)
    out_ref[:, 0, 0:16, :] = waves.astype(jnp.bfloat16)
    out_ref[:, 1, 0:16, :] = (waves * chip_signs()).astype(jnp.bfloat16)
    if rider_ref is not None:
        spread = jnp.broadcast_to(rider_ref[...][None, None], (32, 2, 16, CHANNELS))
        out_ref[:, :, 16:32, :] = spread


def legendre_matrices(table, rank, spread):
    shapes = [((2048, 512), jnp.bfloat16), ((512, 2048), jnp.bfloat16)]
    shapes += [((16, 512), jnp.bfloat16), ((512, 16), jnp.bfloat16)]
    operands = (rank.reshape(1), table, jnp.asarray(spread), jnp.asarray(spread.T))
    return on_device(legendre_kernel, shapes, operands, "legendre", 4_000_000_000, 1)


def complex_weights(weight):
    real, imag = weight[:, :, 0], weight[:, :, 1]
    return jnp.concatenate(
        [jnp.concatenate([real, imag], axis=3), jnp.concatenate([-imag, real], axis=3)], axis=2
    )


def mix_kernel(
    rank_ref,
    rows_ref,
    edge_ref,
    order_ref,
    weight_hbm,
    edge_out_ref,
    out_hbm,
    high_hbm,
    low_hbm,
    weight_ref,
    out_ref,
    high_ref,
    low_ref,
    mixed,
    weight_sems,
    out_sems,
    saved_sems,
    *,
    back,
):
    places = [(1, 0), (0, 0), (1, 1), (0, 1)]
    loads = [
        pltpu.make_async_copy(weight_hbm.at[k, j], weight_ref.at[k, j], weight_sems.at[n])
        for n, (k, j) in enumerate(places)
    ]
    for load in loads:
        load.start()
    order = order_ref[...]
    for block in range(8):
        rows = rows_ref[16 * block : 16 * block + 16, 0:16, :].reshape(256, CHANNELS)
        turned = dot(order, rows).astype(jnp.bfloat16)
        for q in range(16):
            kind, p, ri, j = q >> 3, (q >> 2) & 1, (q >> 1) & 1, q & 1
            piece = turned[16 * q : 16 * (q + 1), :]
            row = 128 * p + 16 * block
            lanes = slice(CHANNELS * ri, CHANNELS * (ri + 1))
            if kind == 0:
                high_ref[j, row : row + 16, lanes] = piece
            else:
                low_ref[j, row : row + 16, lanes] = piece
    place = lax.broadcasted_iota(jnp.int32, (256, 2 * CHANNELS), 0)
    base = 2 * (place & 127) + (place >> 7)
    product = dot_nt if back else dot
    saves = []
    for j in range(2):
        fold = 2 * rank_ref[0] + j
        both = low_ref[j].astype(jnp.float32)
        edge = jnp.concatenate(
            [edge_ref[2 * j : 2 * j + 1, :], edge_ref[2 * j + 1 : 2 * j + 2, :]], axis=1
        )
        high_ref[j, 256:512, :] = jnp.where(
            base > fold, both, jnp.where(base == fold, edge, 0.0)
        ).astype(jnp.bfloat16)
        low_ref[j] = jnp.where(base <= fold, both, 0.0).astype(jnp.bfloat16)
        pair = [
            pltpu.make_async_copy(high_ref.at[j], high_hbm.at[j], saved_sems.at[2 * j]),
            pltpu.make_async_copy(low_ref.at[j], low_hbm.at[j], saved_sems.at[2 * j + 1]),
        ]
        for save in pair:
            save.start()
        saves += pair
        loads[2 * j].wait()
        mixed[0, j] = product(high_ref[j, 0:256, :], weight_ref[1, j]).astype(jnp.bfloat16)
        high = product(high_ref[j, 256:512, :], weight_ref[1, j])
        loads[2 * j + 1].wait()
        low = product(low_ref[j], weight_ref[0, j])
        mixed[1, j] = jnp.where(base <= fold, low, high).astype(jnp.bfloat16)
        corner = jnp.sum(jnp.where(base == fold, high, 0.0), axis=0, keepdims=True)
        edge_out_ref[2 * j : 2 * j + 1, :] = corner[:, :CHANNELS]
        edge_out_ref[2 * j + 1 : 2 * j + 2, :] = corner[:, CHANNELS:]
    edge_out_ref[4:16, :] = jnp.zeros((12, CHANNELS), jnp.float32)
    for block in range(8):
        pieces = []
        for q in range(16):
            kind, p, ri, j = q >> 3, (q >> 2) & 1, (q >> 1) & 1, q & 1
            row = 128 * p + 16 * block
            pieces.append(mixed[kind, j, row : row + 16, CHANNELS * ri : CHANNELS * (ri + 1)])
        turned = dot(order, jnp.concatenate(pieces, axis=0))
        owners = slice(16 * block, 16 * (block + 1))
        out_ref[owners] = turned.astype(jnp.bfloat16).reshape(16, 16, CHANNELS)
        save = pltpu.make_async_copy(
            out_ref.at[owners], out_hbm.at[owners], out_sems.at[block]
        )
        save.start()
        saves.append(save)
    for save in saves:
        save.wait()


def mix(rank, rows, edge, weights, order, back):
    shape = jax.ShapeDtypeStruct
    vmem = pl.BlockSpec(memory_space=pltpu.VMEM)
    anywhere = pl.BlockSpec(memory_space=pl.ANY)
    flops = 2 * 1536 * 768 * 768 + 4 * 2048 * 256 * 384
    blocks = (DEVICES, 16, CHANNELS)
    high, low = (2, 512, 2 * CHANNELS), (2, 256, 2 * CHANNELS)
    return pl.pallas_call(
        functools.partial(mix_kernel, back=back),
        out_shape=(
            shape((16, CHANNELS), jnp.float32),
            shape(blocks, jnp.bfloat16),
            shape(high, jnp.bfloat16),
            shape(low, jnp.bfloat16),
        ),
        in_specs=[pl.BlockSpec(memory_space=pltpu.SMEM), vmem, vmem, vmem, anywhere],
        out_specs=(vmem, anywhere, anywhere, anywhere),
        scratch_shapes=[
            pltpu.VMEM((2, 2, 2 * CHANNELS, 2 * CHANNELS), jnp.bfloat16),
            pltpu.VMEM(blocks, jnp.bfloat16),
            pltpu.VMEM(high, jnp.bfloat16),
            pltpu.VMEM(low, jnp.bfloat16),
            pltpu.VMEM((2, 2, 256, 2 * CHANNELS), jnp.bfloat16),
            pltpu.SemaphoreType.DMA((4,)),
            pltpu.SemaphoreType.DMA((8,)),
            pltpu.SemaphoreType.DMA((4,)),
        ],
        compiler_params=pltpu.CompilerParams(vmem_limit_bytes=48 * 1024 * 1024),
        cost_estimate=pl.CostEstimate(flops=flops, bytes_accessed=12_000_000, transcendentals=0),
        name="mix_back" if back else "mix_modes",
    )(rank.reshape(1), rows, edge, order, weights)


def forward_kernel(table_ref, mine_ref, other_ref, out_ref):
    for part in range(4):
        rows = slice(128 * part, 128 * (part + 1))
        lines = []
        for a in range(2):
            sums = dot(table_ref[0, rows, :], mine_ref[a]) + dot(table_ref[1, rows, :], other_ref[a])
            lines.append(sums.reshape(16, 8, CHANNELS))
        out_ref[16 * part : 16 * (part + 1)] = jnp.concatenate(lines, axis=1).astype(jnp.bfloat16)


def inverse_rows(table_ref, mine, other, a):
    def pick(waves):
        return waves[:, 8 * a : 8 * (a + 1), :].reshape(512, CHANNELS).astype(jnp.bfloat16)

    sums = dot(table_ref[0], pick(mine)) + dot(table_ref[1], pick(other))
    return sums.astype(jnp.bfloat16).astype(jnp.float32)


def activate_kernel(table_ref, mine_ref, other_ref, local_ref, cotangent_ref, out_ref, grad_ref):
    mine = mine_ref[:, 0:16, :].astype(jnp.float32)
    other = other_ref[:, 0:16, :].astype(jnp.float32)
    scale = math.sqrt(2.0 / math.pi)
    for a in range(2):
        v = inverse_rows(table_ref, mine, other, a) + local_ref[a]
        square = v * v
        t = jnp.tanh(scale * (v + 0.044715 * (v * square)))
        half = 0.5 * (1.0 + t)
        out_ref[a] = (v * half).astype(jnp.bfloat16)
        slope = half + 0.5 * v * (1.0 - t * t) * (scale * (1.0 + 3 * 0.044715 * square))
        grad_ref[a] = (cotangent_ref[a].astype(jnp.float32) * slope).astype(jnp.bfloat16)


def finish_kernel(table_ref, mine_ref, other_ref, local_ref, out_ref):
    mine = mine_ref[:, 0:16, :].astype(jnp.float32)
    other = other_ref[:, 0:16, :].astype(jnp.float32)
    for a in range(2):
        total = inverse_rows(table_ref, mine, other, a) + local_ref[a]
        out_ref[a] = total.astype(jnp.bfloat16)


MARGIN = 8
CHUNK = 40


def stencil_kernel(
    weight_ref,
    corner_ref,
    above_ref,
    mine_ref,
    below_ref,
    left_ref,
    right_ref,
    out_ref,
    line,
    shifted,
    sums,
    *,
    sign,
):
    blocks = (above_ref, mine_ref, below_ref)
    for row in range(6):
        line[MARGIN : MARGIN + LON_DEV, :] = blocks[row // 2][row % 2].astype(jnp.float32)
        line[MARGIN - HALO_REACH : MARGIN, :] = left_ref[row]
        line[MARGIN + LON_DEV : MARGIN + LON_DEV + HALO_REACH, :] = right_ref[row]
        for shift in range(5):
            first = MARGIN - HALO_REACH + shift
            shifted[shift, row] = line[first : first + LON_DEV, :]

    def step(index, carry):
        first = pl.multiple_of(index * CHUNK, 8)
        for a in range(2):
            for lane in range(3):
                lanes = slice(128 * lane, 128 * (lane + 1))
                totals = [jnp.zeros((CHUNK, 128), jnp.float32)] * 4
                for n in range(9):
                    row = sign * corner_ref[n, 0] + HALO_REACH + a
                    column = sign * corner_ref[n, 1] + HALO_REACH
                    cells = shifted[column, row, pl.ds(first, CHUNK), lanes]
                    totals = [totals[k] + weight_ref[8 * n + 2 * k + a] * cells for k in range(4)]
                for k in range(4):
                    sums[k, a, pl.ds(first, CHUNK), lanes] = totals[k]
        return carry

    lax.fori_loop(0, LON_DEV // CHUNK, step, 0)
    for k in range(4):
        for a in range(2):
            out_ref[k, a] = sums[k, a].astype(jnp.bfloat16)


def outer_kernel(high_ref, high_grad_ref, low_ref, low_grad_ref, out_ref):
    c = CHANNELS
    for kind, (left_ref, right_ref) in enumerate(((low_ref, low_grad_ref), (high_ref, high_grad_ref))):
        for j in range(2):
            right = right_ref[j]
            across = (((0,), (0,)), ((), ()))
            first = lax.dot_general(
                left_ref[j, :, :c], right, across, preferred_element_type=jnp.float32
            )
            second = lax.dot_general(
                left_ref[j, :, c:], right, across, preferred_element_type=jnp.float32
            )
            out_ref[kind, j, 0] = first[:, :c] + second[:, c:]
            out_ref[kind, j, 1] = first[:, c:] - second[:, :c]


def on_device(kernel, shapes, operands, name, flops, scalars=0, scratch=()):
    vmem = pl.BlockSpec(memory_space=pltpu.VMEM)
    smem = pl.BlockSpec(memory_space=pltpu.SMEM)
    shapes = [jax.ShapeDtypeStruct(*s) for s in shapes]
    moved = sum(math.prod(v.shape) * v.dtype.itemsize for v in [*shapes, *operands])
    return pl.pallas_call(
        kernel,
        out_shape=tuple(shapes),
        in_specs=[smem] * scalars + [vmem] * (len(operands) - scalars),
        out_specs=(vmem,) * len(shapes),
        scratch_shapes=list(scratch),
        compiler_params=pltpu.CompilerParams(vmem_limit_bytes=48 * 1024 * 1024),
        cost_estimate=pl.CostEstimate(flops=flops, bytes_accessed=moved, transcendentals=0),
        name=name,
    )(*operands)


BLOCK = (2, LON_DEV, CHANNELS)
WAVE_FLOPS = 2 * 512 * 720 * 768


def swap_cores(values):
    return lax.ppermute(values, "core", SWAP)


def edges_kernel(above_ref, block_ref, below_ref, tail_ref, head_ref):
    for n, ref in enumerate((above_ref, block_ref, below_ref)):
        for a in range(2):
            cells = ref[a].astype(jnp.float32)
            tail_ref[2 * n + a] = cells[LON_DEV - HALO_REACH :]
            head_ref[2 * n + a] = cells[:HALO_REACH]


def to_wave_blocks(mine, other, table):
    shapes = [((64, 16, CHANNELS), jnp.bfloat16)]
    return on_device(forward_kernel, shapes, (table, mine, other), "to_waves", WAVE_FLOPS)[0]


def between_chips(blocks):
    return lax.all_to_all(blocks, CHIPS, split_axis=0, concat_axis=0, tiled=True)


def between_degrees(blocks):
    return lax.all_to_all(blocks, ALL, split_axis=0, concat_axis=0, tiled=True)


def coefficient_blocks(spectra, matrices, rider=None):
    matrix, flipped, edge, edge_flip = matrices
    operands = (matrix, edge, spectra.reshape(32, 2, 16, CHANNELS))
    operands += () if rider is None else (rider,)
    shapes = [
        ((DEVICES, 16 if rider is None else 24, CHANNELS), jnp.bfloat16),
        ((16, CHANNELS), jnp.float32),
    ]
    flops = 2 * 2048 * 512 * 512
    return on_device(to_coefficients_kernel, shapes, operands, "to_coefficients", flops)


def wave_blocks(rows, corner, matrices, rider=None):
    matrix, flipped, edge, edge_flip = matrices
    operands = (flipped, edge_flip, rows, corner)
    operands += () if rider is None else (rider,)
    shapes = [((32, 2, 16 if rider is None else 32, CHANNELS), jnp.bfloat16)]
    (out,) = on_device(to_waves_kernel, shapes, operands, "from_modes", 2 * 2048 * 512 * 512)
    return out.reshape(64, -1, CHANNELS)


def row_halo(block):
    above = lax.ppermute(block, "lat", [(i, i + 1) for i in range(31)])
    below = lax.ppermute(block, "lat", [(i + 1, i) for i in range(31)])
    return above, below


def column_halo(above, block, below):
    shapes = [((6, HALO_REACH, CHANNELS), jnp.float32)] * 2
    tails, heads = on_device(edges_kernel, shapes, (above, block, below), "edges", 0)
    lon = ("zhi", "core")
    left = lax.ppermute(tails, lon, [(i, (i + 1) % 4) for i in range(4)])
    right = lax.ppermute(heads, lon, [((i + 1) % 4, i) for i in range(4)])
    return left, right


def stencil(above, block, below, left, right, disco_kernel, offsets, lat_first, sign):
    row = lat_first + jnp.arange(2, dtype=jnp.int32)[None, :]
    row = row - offsets[:, :1] if sign < 0 else row + jnp.zeros_like(offsets[:, :1])
    chosen = row[:, :, None] == jnp.arange(64, dtype=jnp.int32)[None, None, :]
    weights = jnp.sum(
        jnp.where(chosen[:, None], disco_kernel[:, :, None, :], 0.0), axis=-1
    ).reshape(-1)
    operands = (weights, offsets, above, block, below, left, right)
    scratch = [
        pltpu.VMEM((LON_DEV + 2 * MARGIN, CHANNELS), jnp.float32),
        pltpu.VMEM((5, 6, LON_DEV, CHANNELS), jnp.float32),
        pltpu.VMEM((4, *BLOCK), jnp.float32),
    ]
    shapes = [((4, *BLOCK), jnp.bfloat16)]
    name = "stencil" if sign > 0 else "stencil_back"
    flops = 2 * 36 * math.prod(BLOCK) * 16
    kernel = functools.partial(stencil_kernel, sign=sign)
    return on_device(kernel, shapes, operands, name, flops, 2, scratch)[0]


def local(
    grid_field,
    cotangent,
    analysis_table,
    synthesis_table,
    spectral_weight,
    disco_weight,
    disco_kernel,
    neighbour_offsets,
    *,
    forward_all,
    backward_all,
    spread,
    order,
):
    lat, zhi, core = (lax.axis_index(name) for name in ALL)
    rank = lat * 4 + zhi * 2 + core
    lat_first = lat * 2
    forward_table = lax.dynamic_index_in_dim(jnp.asarray(forward_all), core, 0, keepdims=False)
    order = jnp.asarray(order)
    block_shapes = [(BLOCK, jnp.bfloat16)]

    grid_other = swap_cores(grid_field)
    above, below = row_halo(grid_field)
    blocks = to_wave_blocks(grid_field, grid_other, forward_table)
    blocks, analysis_table, spectral_weight, later = tie(
        blocks, analysis_table, spectral_weight, jnp.asarray(backward_all)
    )
    spectra = between_chips(blocks)
    analysis_parts = legendre_matrices(analysis_table, rank, spread)
    weights = complex_weights(spectral_weight)
    spectra, synthesis_table, above, below, *analysis_parts = tie(
        spectra, synthesis_table, above, below, *analysis_parts
    )
    rows, corner = coefficient_blocks(spectra, analysis_parts)
    rows, above, below = tie(rows, above, below)
    rows = between_degrees(rows)
    synthesis_parts = legendre_matrices(synthesis_table, rank, spread)
    left, right = column_halo(above, grid_field, below)
    rows, left, right, weights, *synthesis_parts = tie(rows, left, right, weights, *synthesis_parts)
    corner, mixed, modes_high, modes_low = mix(rank, rows, corner, weights, order, False)
    mixed, left, right = tie(mixed, left, right)
    mixed = between_degrees(mixed)
    inputs = stencil(
        above, grid_field, below, left, right, disco_kernel, neighbour_offsets, lat_first, 1
    )
    local_part = jnp.einsum(
        "kabc,kcd->abd", inputs, disco_weight, preferred_element_type=jnp.float32
    )
    mixed, local_part, inputs = tie(mixed, local_part, inputs)
    waves = wave_blocks(mixed, corner, synthesis_parts)
    waves, later, cotangent = tie(waves, later, cotangent)
    waves = between_chips(waves)
    backward_table = lax.dynamic_index_in_dim(later, core, 0, keepdims=False)
    block_output, hidden_grad = on_device(
        activate_kernel,
        block_shapes * 2,
        (backward_table, waves, swap_cores(waves), local_part, cotangent),
        "activate",
        WAVE_FLOPS,
    )

    blocks = to_wave_blocks(hidden_grad, swap_cores(hidden_grad), forward_table)
    blocks, hidden_grad, inputs = tie(blocks, hidden_grad, inputs)
    above, below = row_halo(hidden_grad)
    grad_spectra = between_chips(blocks)
    local_grad = jnp.einsum(
        "kabc,abd->kcd", inputs, hidden_grad, preferred_element_type=jnp.float32
    ) * (1.0 / math.sqrt(64 * LON_CELLS))
    halves = local_grad.reshape(2, 2 * CHANNELS, CHANNELS)
    kept = lax.dynamic_index_in_dim(halves, core, 0, keepdims=False)
    given = lax.dynamic_index_in_dim(halves, 1 - core, 0, keepdims=False)
    rider = (kept + swap_cores(given)).astype(jnp.bfloat16).reshape(96, 8, CHANNELS)
    grad_spectra, rider, above, below = tie(grad_spectra, rider, above, below)

    grad_rows, corner = coefficient_blocks(grad_spectra, synthesis_parts, rider)
    grad_rows, above, below = tie(grad_rows, above, below)
    grad_rows = between_degrees(grad_rows)
    left, right = column_halo(above, hidden_grad, below)
    grad_rows, left, right = tie(grad_rows, left, right)
    corner, back, grads_high, grads_low = mix(rank, grad_rows, corner, weights, order, True)
    back, left, right, grad_rows = tie(back, left, right, grad_rows)
    back = between_degrees(back)
    shares = grad_rows[:, 16:].reshape(64, 16, CHANNELS).astype(jnp.float32)
    owned = jnp.sum(shares, axis=0).astype(jnp.bfloat16)
    back_inputs = stencil(
        above, hidden_grad, below, left, right, disco_kernel, neighbour_offsets, lat_first, -1
    )
    local_back = jnp.einsum(
        "kabd,kcd->abc", back_inputs, disco_weight, preferred_element_type=jnp.float32
    )
    back, owned, local_back = tie(back, owned, local_back)
    waves_back = wave_blocks(back, corner, analysis_parts, owned)
    waves_back, grads_high, grads_low = tie(waves_back, grads_high, grads_low)
    waves_back = between_chips(waves_back)
    (spectral_grad,) = on_device(
        outer_kernel,
        [((2, 2, 2, CHANNELS, CHANNELS), jnp.float32)],
        (modes_high, grads_high, modes_low, grads_low),
        "outer",
        2 * 1536 * 768 * 768,
    )
    waves_back, spectral_grad = tie(waves_back, spectral_grad)
    waves_other = swap_cores(waves_back)
    (field_grad,) = on_device(
        finish_kernel,
        block_shapes,
        (backward_table, waves_back, waves_other, local_back),
        "finish",
        WAVE_FLOPS,
    )
    mine_sums = waves_back[:48, 16:].reshape(48, 2, 8, CHANNELS)
    other_sums = waves_other[:48, 16:].reshape(48, 2, 8, CHANNELS)
    first = jnp.where(core == 0, mine_sums, other_sums)
    second = jnp.where(core == 0, other_sums, mine_sums)
    disco_grad = (
        jnp.stack([first, second], axis=1)
        .transpose(2, 0, 1, 3, 4)
        .reshape(4, CHANNELS, CHANNELS)
        .astype(jnp.float32)
    )
    return (block_output, field_grad, spectral_grad, disco_grad)


def solution(mesh):
    forward_all, backward_all = wave_tables()
    place = np.arange(256)
    order = (place[:, None] == (place % 16 * 16 + place // 16)[None, :]).astype(ml_dtypes.bfloat16)
    split = Mesh(mesh.devices.reshape(32, 2, 2), ALL)
    lon = ("zhi", "core")
    return jax.shard_map(
        functools.partial(
            local,
            forward_all=forward_all,
            backward_all=backward_all,
            spread=spread_matrix(),
            order=order,
        ),
        mesh=split,
        in_specs=(
            P("lat", lon, None),
            P("lat", lon, None),
            P(None, ALL, None, None),
            P(None, ALL, None, None),
            P(None, ALL, None, None, None),
            P(),
            P(),
            P(),
        ),
        out_specs=(
            P("lat", lon, None),
            P("lat", lon, None),
            P(None, ALL, None, None, None),
            P(),
        ),
        check_vma=False,
    )
```

```python
import functools
import math

import jax
import jax.numpy as jnp
import ml_dtypes
import numpy as np
from jax import lax
from jax.experimental import pallas as pl
from jax.experimental.pallas import tpu as pltpu
from jax.sharding import Mesh
from jax.sharding import PartitionSpec as P

HALO_REACH = 2
LON_CELLS = 1440
LON_DEV = 360
CHANNELS = 384
DEGREES = 512
HALF = 256
DEVICES = 128
ALL = ("lat", "zhi", "core")
CHIPS = ("lat", "zhi")
SWAP = [(0, 1), (1, 0)]


def wave_tables():
    e, lh, p, ri = np.meshgrid(*map(np.arange, (64, 2, 2, 2)), indexing="ij")
    e, lh, p, ri = (v.reshape(-1) for v in (e, lh, p, ri))
    forward = np.zeros((2, 2, 512, LON_DEV), np.float32)
    backward = np.zeros((2, 2, LON_DEV, 512), np.float32)

    def basis(wave_core, cell_core):
        base = 4 * e + 2 * wave_core + p
        wave = np.where(lh == 0, base, DEGREES - 1 - base)
        column = np.arange(LON_DEV) + LON_DEV * cell_core
        angle = (wave[:, None] * column[None, :] % LON_CELLS) * (2.0 * math.pi / LON_CELLS)
        return np.where(ri[:, None] == 0, np.cos(angle), -np.sin(angle)) / math.sqrt(LON_CELLS)

    for core in range(2):
        for other in range(2):
            forward[core, other] = basis(core, core ^ other)
            backward[core, other] = basis(core ^ other, core).T
    return forward.astype(ml_dtypes.bfloat16), backward.astype(ml_dtypes.bfloat16)


def spread_matrix():
    row, lh, cp, cri = (
        v.reshape(-1) for v in np.meshgrid(*map(np.arange, (64, 2, 2, 2)), indexing="ij")
    )
    slh, sp, sa = (v.reshape(-1) for v in np.meshgrid(*map(np.arange, (2, 2, 64)), indexing="ij"))
    spread = (
        (slh[:, None] == lh[None, :]) & (sp[:, None] == cp[None, :]) & (sa[:, None] == row[None, :])
    )
    return spread.astype(np.float32).astype(ml_dtypes.bfloat16)


def tie(*values):
    return lax.optimization_barrier(values)


def dot(left, right):
    return jnp.dot(left, right, preferred_element_type=jnp.float32)


def dot_nt(left, right):
    return lax.dot_general(
        left, right, (((1,), (1,)), ((), ())), preferred_element_type=jnp.float32
    )


def one_hot(wanted, shape):
    degree = lax.broadcasted_iota(jnp.int32, shape, 1)
    return jnp.where(degree == wanted, 1.0, 0.0).astype(jnp.bfloat16)


def keep(rows, cols, values):
    return jnp.where(rows == cols, values, 0.0).astype(jnp.bfloat16)


def legendre_kernel(
    rank_ref,
    table_ref,
    spread_ref,
    turned_ref,
    matrix_hbm,
    flipped_hbm,
    edge_ref,
    edge_flip_ref,
    matrix_ref,
    flipped_ref,
    sems,
):
    rank = rank_ref[0]
    saves = []
    lower = table_ref[0].reshape(128, DEGREES)
    upper = table_ref[1].reshape(128, DEGREES)
    spread = spread_ref[...]
    turned = turned_ref[...]

    def attributes(place):
        p, kind = (place >> 2) & 1, (place >> 3) & 1
        fold = 2 * (place >> 4) + (place & 1)
        high = jnp.where(2 * rank + p > fold, kind, 0)
        return kind, fold, ((place >> 1) & 3) + 4 * high

    for block in range(8):
        rows = slice(256 * block, 256 * (block + 1))
        place = lax.broadcasted_iota(jnp.int32, (256, 1), 0) + 256 * block
        kind, fold, code = attributes(place)
        last = DEGREES - 1 - fold
        low = one_hot(jnp.where(kind == 0, last, fold), (256, DEGREES))
        high = one_hot(jnp.where(kind == 0, -1, last), (256, DEGREES))
        picked = jnp.concatenate([dot_nt(low, lower), dot_nt(high, upper)], axis=1)
        picked = picked.astype(jnp.bfloat16)
        column = lax.broadcasted_iota(jnp.int32, (1, 512), 1) & 7
        matrix_ref[rows, :] = keep(code, column, dot(picked, spread))
        _, _, across = attributes(lax.broadcasted_iota(jnp.int32, (1, 256), 1) + 256 * block)
        down = lax.broadcasted_iota(jnp.int32, (512, 1), 0) & 7
        flipped_ref[:, rows] = keep(down, across, dot_nt(turned, picked))
        saves.append(started(matrix_ref.at[rows], matrix_hbm.at[rows], sems.at[0, block]))
        saves.append(started(flipped_ref.at[:, rows], flipped_hbm.at[:, rows], sems.at[1, block]))
    place = lax.broadcasted_iota(jnp.int32, (16, 1), 0)
    wanted = jnp.where(place < 4, DEGREES - 1 - (2 * rank + (place >> 1)), -1)
    edge = dot_nt(one_hot(wanted, (16, DEGREES)), upper).astype(jnp.bfloat16)
    column = lax.broadcasted_iota(jnp.int32, (1, 512), 1) & 7
    edge_ref[...] = keep(place + 4, column, dot(edge, spread[128:]))
    across = lax.broadcasted_iota(jnp.int32, (1, 16), 1) + 4
    down = lax.broadcasted_iota(jnp.int32, (512, 1), 0) & 7
    edge_flip_ref[...] = keep(down, across, dot_nt(turned[:, 128:], edge))
    for save in saves:
        save.wait()


def chip_signs():
    line = lax.broadcasted_iota(jnp.int32, (1, 16, CHANNELS), 1)
    odd = ((line >> 2) ^ (line >> 1)) & 1
    return jnp.where(odd == 1, -1.0, 1.0)


def to_coefficients_kernel(
    matrix_hbm, edge_ref, spectra_ref, out_hbm, corner_ref, matrix_ref, out_ref, in_sems, out_sems
):
    parts = [slice(256 * block, 256 * (block + 1)) for block in range(8)]
    loads = [
        started(matrix_hbm.at[rows], matrix_ref.at[rows], in_sems.at[n])
        for n, rows in enumerate(parts)
    ]
    saves = []
    both = spectra_ref[...].astype(jnp.float32)
    spectra = (both[:, 0] + chip_signs() * both[:, 1]).reshape(512, CHANNELS).astype(jnp.bfloat16)
    for block, rows in enumerate(parts):
        loads[block].wait()
        sums = dot(matrix_ref[rows, :], spectra)
        places = slice(16 * block, 16 * (block + 1))
        out_ref[places] = sums.astype(jnp.bfloat16).reshape(16, 16, CHANNELS)
        saves.append(started(out_ref.at[places], out_hbm.at[places], out_sems.at[block]))
    corner = dot(edge_ref[...], spectra).astype(jnp.bfloat16)
    corner_ref[...] = corner.astype(jnp.float32)
    for save in saves:
        save.wait()


def from_modes_kernel(
    flipped_hbm,
    edge_flip_ref,
    rows_ref,
    corner_ref,
    out_hbm,
    flipped_ref,
    out_ref,
    in_sems,
    out_sems,
    *,
    rider,
):
    parts = [slice(128 * block, 128 * (block + 1)) for block in range(4)]
    loads = [
        started(flipped_hbm.at[lines], flipped_ref.at[lines], in_sems.at[n])
        for n, lines in enumerate(parts)
    ]
    saves = []
    rows = rows_ref[:, 0:16, :].reshape(2048, CHANNELS)
    corner = corner_ref[...].astype(jnp.bfloat16)
    if rider:
        shares = rows_ref[...].astype(jnp.float32).reshape(64, 2, 24, CHANNELS)[:, :, 16:24, :]
        owned = jnp.sum(shares, axis=0).reshape(16, CHANNELS).astype(jnp.bfloat16)
        out_ref[:, :, 16:32, :] = jnp.broadcast_to(owned[None, None], (32, 2, 16, CHANNELS))
    for block, lines in enumerate(parts):
        loads[block].wait()
        waves = dot(flipped_ref[lines, :], rows) + dot(edge_flip_ref[lines, :], corner)
        waves = waves.reshape(8, 16, CHANNELS)
        places = slice(8 * block, 8 * (block + 1))
        out_ref[places, 0, 0:16, :] = waves.astype(jnp.bfloat16)
        out_ref[places, 1, 0:16, :] = (waves * chip_signs()).astype(jnp.bfloat16)
        saves.append(started(out_ref.at[places], out_hbm.at[places], out_sems.at[block]))
    for save in saves:
        save.wait()


def legendre_matrices(table, rank, spread):
    shapes = [((2048, 512), jnp.bfloat16), ((512, 2048), jnp.bfloat16)]
    shapes += [((16, 512), jnp.bfloat16), ((512, 16), jnp.bfloat16)]
    operands = (rank.reshape(1), table, jnp.asarray(spread), jnp.asarray(spread.T))
    scratch = [
        pltpu.VMEM((2048, 512), jnp.bfloat16),
        pltpu.VMEM((512, 2048), jnp.bfloat16),
        pltpu.SemaphoreType.DMA((2, 8)),
    ]
    return on_device(
        legendre_kernel, shapes, operands, "legendre", 4_000_000_000, 1, scratch, (), (0, 1)
    )


def complex_weights(weight):
    real, imag = weight[:, :, 0], weight[:, :, 1]
    return jnp.concatenate(
        [jnp.concatenate([real, imag], axis=3), jnp.concatenate([-imag, real], axis=3)], axis=2
    )


def mix_kernel(
    rank_ref,
    rows_hbm,
    edge_ref,
    order_ref,
    weight_hbm,
    *refs,
    back,
):
    rider_ref, refs = (refs[0], refs[1:]) if back else (None, refs)
    (
        edge_out_ref,
        out_hbm,
        high_hbm,
        low_hbm,
        rows_ref,
        weight_ref,
        out_ref,
        high_ref,
        low_ref,
        mixed,
        row_sems,
        weight_sems,
        out_sems,
        saved_sems,
    ) = refs
    arrivals = []
    for block in range(8):
        sources = slice(16 * block, 16 * (block + 1))
        arrivals.append(started(rows_hbm.at[sources], rows_ref.at[sources], row_sems.at[block]))
    places = [(1, 0), (0, 0), (1, 1), (0, 1)]
    loads = [
        started(weight_hbm.at[k, j], weight_ref.at[k, j], weight_sems.at[n])
        for n, (k, j) in enumerate(places)
    ]
    order = order_ref[...]
    for block in range(8):
        arrivals[block].wait()
        rows = rows_ref[16 * block : 16 * block + 16, 0:16, :].reshape(256, CHANNELS)
        turned = dot(order, rows).astype(jnp.bfloat16)
        for q in range(16):
            kind, p, ri, j = q >> 3, (q >> 2) & 1, (q >> 1) & 1, q & 1
            piece = turned[16 * q : 16 * (q + 1), :]
            row = 128 * p + 16 * block
            lanes = slice(CHANNELS * ri, CHANNELS * (ri + 1))
            if kind == 0:
                high_ref[j, row : row + 16, lanes] = piece
            else:
                low_ref[j, row : row + 16, lanes] = piece
    place = lax.broadcasted_iota(jnp.int32, (256, 2 * CHANNELS), 0)
    base = 2 * (place & 127) + (place >> 7)
    product = dot_nt if back else dot
    saves = []
    for j in range(2):
        fold = 2 * rank_ref[0] + j
        both = low_ref[j].astype(jnp.float32)
        edge = jnp.concatenate(
            [edge_ref[2 * j : 2 * j + 1, :], edge_ref[2 * j + 1 : 2 * j + 2, :]], axis=1
        )
        high_ref[j, 256:512, :] = jnp.where(
            base > fold, both, jnp.where(base == fold, edge, 0.0)
        ).astype(jnp.bfloat16)
        low_ref[j] = jnp.where(base <= fold, both, 0.0).astype(jnp.bfloat16)
        saves.append(started(high_ref.at[j], high_hbm.at[j], saved_sems.at[2 * j]))
        saves.append(started(low_ref.at[j], low_hbm.at[j], saved_sems.at[2 * j + 1]))
        loads[2 * j].wait()
        mixed[0, j] = product(high_ref[j, 0:256, :], weight_ref[1, j]).astype(jnp.bfloat16)
        high = product(high_ref[j, 256:512, :], weight_ref[1, j])
        loads[2 * j + 1].wait()
        low = product(low_ref[j], weight_ref[0, j])
        mixed[1, j] = jnp.where(base <= fold, low, high).astype(jnp.bfloat16)
        corner = jnp.sum(jnp.where(base == fold, high, 0.0), axis=0, keepdims=True)
        edge_out_ref[2 * j : 2 * j + 1, :] = corner[:, :CHANNELS]
        edge_out_ref[2 * j + 1 : 2 * j + 2, :] = corner[:, CHANNELS:]
    edge_out_ref[4:16, :] = jnp.zeros((12, CHANNELS), jnp.float32)
    if rider_ref is not None:
        out_ref[0:96, 16:24, :] = rider_ref[...]
        out_ref[96:128, 16:24, :] = jnp.zeros((32, 8, CHANNELS), jnp.bfloat16)
    for block in range(8):
        pieces = []
        for q in range(16):
            kind, p, ri, j = q >> 3, (q >> 2) & 1, (q >> 1) & 1, q & 1
            row = 128 * p + 16 * block
            pieces.append(mixed[kind, j, row : row + 16, CHANNELS * ri : CHANNELS * (ri + 1)])
        turned = dot(order, jnp.concatenate(pieces, axis=0))
        owners = slice(16 * block, 16 * (block + 1))
        out_ref[owners, 0:16, :] = turned.astype(jnp.bfloat16).reshape(16, 16, CHANNELS)
        saves.append(started(out_ref.at[owners], out_hbm.at[owners], out_sems.at[block]))
    for save in saves:
        save.wait()


def mix(rank, rows, edge, weights, order, rider=None):
    back = rider is not None
    flops = 2 * 1536 * 768 * 768 + 4 * 2048 * 256 * 384
    blocks = (DEVICES, 24 if back else 16, CHANNELS)
    high, low = (2, 512, 2 * CHANNELS), (2, 256, 2 * CHANNELS)
    operands = (rank.reshape(1), rows, edge, order, weights) + ((rider,) if back else ())
    shapes = [
        ((16, CHANNELS), jnp.float32),
        (blocks, jnp.bfloat16),
        (high, jnp.bfloat16),
        (low, jnp.bfloat16),
    ]
    scratch = [
        pltpu.VMEM((DEVICES, 16, CHANNELS), jnp.bfloat16),
        pltpu.VMEM((2, 2, 2 * CHANNELS, 2 * CHANNELS), jnp.bfloat16),
        pltpu.VMEM(blocks, jnp.bfloat16),
        pltpu.VMEM(high, jnp.bfloat16),
        pltpu.VMEM(low, jnp.bfloat16),
        pltpu.VMEM((2, 2, 256, 2 * CHANNELS), jnp.bfloat16),
        pltpu.SemaphoreType.DMA((8,)),
        pltpu.SemaphoreType.DMA((4,)),
        pltpu.SemaphoreType.DMA((8,)),
        pltpu.SemaphoreType.DMA((4,)),
    ]
    return on_device(
        functools.partial(mix_kernel, back=back),
        shapes,
        operands,
        "mix_back" if back else "mix_modes",
        flops,
        1,
        scratch,
        (1, 4),
        (1, 2, 3),
    )


def forward_kernel(table_ref, mine_ref, other_ref, out_ref):
    for part in range(4):
        rows = slice(128 * part, 128 * (part + 1))
        lines = []
        for a in range(2):
            sums = dot(table_ref[0, rows, :], mine_ref[a]) + dot(table_ref[1, rows, :], other_ref[a])
            lines.append(sums.reshape(16, 8, CHANNELS))
        out_ref[16 * part : 16 * (part + 1)] = jnp.concatenate(lines, axis=1).astype(jnp.bfloat16)


def inverse_rows(table_ref, mine, other, a):
    def pick(waves):
        return waves[:, 8 * a : 8 * (a + 1), :].reshape(512, CHANNELS).astype(jnp.bfloat16)

    sums = dot(table_ref[0], pick(mine)) + dot(table_ref[1], pick(other))
    return sums.astype(jnp.bfloat16).astype(jnp.float32)


def activate_kernel(table_ref, mine_ref, other_ref, local_ref, cotangent_ref, out_ref, grad_ref):
    mine = mine_ref[:, 0:16, :].astype(jnp.float32)
    other = other_ref[:, 0:16, :].astype(jnp.float32)
    scale = math.sqrt(2.0 / math.pi)
    for a in range(2):
        v = inverse_rows(table_ref, mine, other, a) + local_ref[a]
        square = v * v
        t = jnp.tanh(scale * (v + 0.044715 * (v * square)))
        half = 0.5 * (1.0 + t)
        out_ref[a] = (v * half).astype(jnp.bfloat16)
        slope = half + 0.5 * v * (1.0 - t * t) * (scale * (1.0 + 3 * 0.044715 * square))
        grad_ref[a] = (cotangent_ref[a].astype(jnp.float32) * slope).astype(jnp.bfloat16)


def finish_kernel(
    core_ref, table_ref, mine_ref, other_ref, local_ref, out_ref, sums_hbm, sums_ref, sems
):
    mine = mine_ref[...].astype(jnp.float32)
    other = other_ref[...].astype(jnp.float32)
    saves = []
    for half in range(2):
        rows = slice(16 + 8 * half, 24 + 8 * half)
        pair = [mine[:48, rows, :], other[:48, rows, :]]
        for core in range(2):
            kept = jnp.where(core_ref[0] == core, pair[0], pair[1])
            sums_ref[half, :, core] = kept
        saves.append(started(sums_ref.at[half], sums_hbm.at[half], sems.at[half]))
    for a in range(2):
        total = inverse_rows(table_ref, mine[:, :16], other[:, :16], a) + local_ref[a]
        out_ref[a] = total.astype(jnp.bfloat16)
    for save in saves:
        save.wait()


MARGIN = 8
CHUNK = 40


def stencil_kernel(
    weight_ref,
    corner_ref,
    above_ref,
    mine_ref,
    below_ref,
    left_ref,
    right_ref,
    out_ref,
    line,
    shifted,
    sums,
    *,
    sign,
):
    blocks = (above_ref, mine_ref, below_ref)
    for row in range(6):
        line[MARGIN : MARGIN + LON_DEV, :] = blocks[row // 2][row % 2].astype(jnp.float32)
        line[MARGIN - HALO_REACH : MARGIN, :] = left_ref[row]
        line[MARGIN + LON_DEV : MARGIN + LON_DEV + HALO_REACH, :] = right_ref[row]
        for shift in range(5):
            first = MARGIN - HALO_REACH + shift
            shifted[shift, row] = line[first : first + LON_DEV, :]

    def step(index, carry):
        first = pl.multiple_of(index * CHUNK, 8)
        for a in range(2):
            for lane in range(3):
                lanes = slice(128 * lane, 128 * (lane + 1))
                totals = [jnp.zeros((CHUNK, 128), jnp.float32)] * 4
                for n in range(9):
                    row = sign * corner_ref[n, 0] + HALO_REACH + a
                    column = sign * corner_ref[n, 1] + HALO_REACH
                    cells = shifted[column, row, pl.ds(first, CHUNK), lanes]
                    totals = [totals[k] + weight_ref[8 * n + 2 * k + a] * cells for k in range(4)]
                for k in range(4):
                    sums[k, a, pl.ds(first, CHUNK), lanes] = totals[k]
        return carry

    lax.fori_loop(0, LON_DEV // CHUNK, step, 0)
    for k in range(4):
        for a in range(2):
            out_ref[k, a] = sums[k, a].astype(jnp.bfloat16)


def outer_kernel(high_ref, high_grad_ref, low_ref, low_grad_ref, out_ref):
    c = CHANNELS
    for kind, (left_ref, right_ref) in enumerate(((low_ref, low_grad_ref), (high_ref, high_grad_ref))):
        for j in range(2):
            right = right_ref[j]
            across = (((0,), (0,)), ((), ()))
            first = lax.dot_general(
                left_ref[j, :, :c], right, across, preferred_element_type=jnp.float32
            )
            second = lax.dot_general(
                left_ref[j, :, c:], right, across, preferred_element_type=jnp.float32
            )
            out_ref[kind, j, 0] = first[:, :c] + second[:, c:]
            out_ref[kind, j, 1] = first[:, c:] - second[:, :c]


def on_device(
    kernel, shapes, operands, name, flops, scalars=0, scratch=(), far_in=(), far_out=()
):
    vmem = pl.BlockSpec(memory_space=pltpu.VMEM)
    smem = pl.BlockSpec(memory_space=pltpu.SMEM)
    far = pl.BlockSpec(memory_space=pltpu.HBM)
    shapes = [jax.ShapeDtypeStruct(*s) for s in shapes]
    moved = sum(math.prod(v.shape) * v.dtype.itemsize for v in [*shapes, *operands])
    ins = [smem if n < scalars else far if n in far_in else vmem for n in range(len(operands))]
    return pl.pallas_call(
        kernel,
        out_shape=tuple(shapes),
        in_specs=ins,
        out_specs=tuple(far if n in far_out else vmem for n in range(len(shapes))),
        scratch_shapes=list(scratch),
        compiler_params=pltpu.CompilerParams(vmem_limit_bytes=48 * 1024 * 1024),
        cost_estimate=pl.CostEstimate(flops=flops, bytes_accessed=moved, transcendentals=0),
        name=name,
    )(*operands)


def started(source, target, sem):
    copy = pltpu.make_async_copy(source, target, sem)
    copy.start()
    return copy


BLOCK = (2, LON_DEV, CHANNELS)
WAVE_FLOPS = 2 * 512 * 720 * 768


def swap_cores(values):
    return lax.ppermute(values, "core", SWAP)


def edges_kernel(above_ref, block_ref, below_ref, tail_ref, head_ref):
    for n, ref in enumerate((above_ref, block_ref, below_ref)):
        for a in range(2):
            cells = ref[a].astype(jnp.float32)
            tail_ref[2 * n + a] = cells[LON_DEV - HALO_REACH :]
            head_ref[2 * n + a] = cells[:HALO_REACH]


def to_wave_blocks(mine, other, table):
    shapes = [((64, 16, CHANNELS), jnp.bfloat16)]
    return on_device(forward_kernel, shapes, (table, mine, other), "to_waves", WAVE_FLOPS)[0]


def between_chips(blocks):
    return lax.all_to_all(blocks, CHIPS, split_axis=0, concat_axis=0, tiled=True)


def between_degrees(blocks):
    return lax.all_to_all(blocks, ALL, split_axis=0, concat_axis=0, tiled=True)


def coefficient_blocks(spectra, matrices):
    matrix, flipped, edge, edge_flip = matrices
    operands = (matrix, edge, spectra.reshape(32, 2, 16, CHANNELS))
    blocks = (DEVICES, 16, CHANNELS)
    shapes = [(blocks, jnp.bfloat16), ((16, CHANNELS), jnp.float32)]
    scratch = [
        pltpu.VMEM((2048, 512), jnp.bfloat16),
        pltpu.VMEM(blocks, jnp.bfloat16),
        pltpu.SemaphoreType.DMA((8,)),
        pltpu.SemaphoreType.DMA((8,)),
    ]
    flops = 2 * 2048 * 512 * 512
    return on_device(
        to_coefficients_kernel, shapes, operands, "to_coefficients", flops, 0, scratch, (0,), (0,)
    )


def wave_blocks(rows, corner, matrices, rider):
    matrix, flipped, edge, edge_flip = matrices
    blocks = (32, 2, 32 if rider else 16, CHANNELS)
    scratch = [
        pltpu.VMEM((512, 2048), jnp.bfloat16),
        pltpu.VMEM(blocks, jnp.bfloat16),
        pltpu.SemaphoreType.DMA((4,)),
        pltpu.SemaphoreType.DMA((4,)),
    ]
    (out,) = on_device(
        functools.partial(from_modes_kernel, rider=rider),
        [(blocks, jnp.bfloat16)],
        (flipped, edge_flip, rows, corner),
        "from_modes",
        2 * 2048 * 512 * 512,
        0,
        scratch,
        (0,),
        (0,),
    )
    return out.reshape(64, -1, CHANNELS)


def row_halo(block):
    above = lax.ppermute(block, "lat", [(i, i + 1) for i in range(31)])
    below = lax.ppermute(block, "lat", [(i + 1, i) for i in range(31)])
    return above, below


def column_halo(above, block, below):
    shapes = [((6, HALO_REACH, CHANNELS), jnp.float32)] * 2
    tails, heads = on_device(edges_kernel, shapes, (above, block, below), "edges", 0)
    lon = ("zhi", "core")
    left = lax.ppermute(tails, lon, [(i, (i + 1) % 4) for i in range(4)])
    right = lax.ppermute(heads, lon, [((i + 1) % 4, i) for i in range(4)])
    return left, right


def stencil(above, block, below, left, right, disco_kernel, offsets, lat_first, sign):
    row = lat_first + jnp.arange(2, dtype=jnp.int32)[None, :]
    row = row - offsets[:, :1] if sign < 0 else row + jnp.zeros_like(offsets[:, :1])
    chosen = row[:, :, None] == jnp.arange(64, dtype=jnp.int32)[None, None, :]
    weights = jnp.sum(
        jnp.where(chosen[:, None], disco_kernel[:, :, None, :], 0.0), axis=-1
    ).reshape(-1)
    operands = (weights, offsets, above, block, below, left, right)
    scratch = [
        pltpu.VMEM((LON_DEV + 2 * MARGIN, CHANNELS), jnp.float32),
        pltpu.VMEM((5, 6, LON_DEV, CHANNELS), jnp.float32),
        pltpu.VMEM((4, *BLOCK), jnp.float32),
    ]
    shapes = [((4, *BLOCK), jnp.bfloat16)]
    name = "stencil" if sign > 0 else "stencil_back"
    flops = 2 * 36 * math.prod(BLOCK) * 16
    kernel = functools.partial(stencil_kernel, sign=sign)
    return on_device(kernel, shapes, operands, name, flops, 2, scratch)[0]


def local(
    grid_field,
    cotangent,
    analysis_table,
    synthesis_table,
    spectral_weight,
    disco_weight,
    disco_kernel,
    neighbour_offsets,
    *,
    forward_all,
    backward_all,
    spread,
    order,
):
    lat, zhi, core = (lax.axis_index(name) for name in ALL)
    rank = lat * 4 + zhi * 2 + core
    lat_first = lat * 2
    forward_table = lax.dynamic_index_in_dim(jnp.asarray(forward_all), core, 0, keepdims=False)
    order = jnp.asarray(order)
    block_shapes = [(BLOCK, jnp.bfloat16)]

    grid_other = swap_cores(grid_field)
    above, below = row_halo(grid_field)
    blocks = to_wave_blocks(grid_field, grid_other, forward_table)
    blocks, analysis_table, spectral_weight, later = tie(
        blocks, analysis_table, spectral_weight, jnp.asarray(backward_all)
    )
    spectra = between_chips(blocks)
    analysis_parts = legendre_matrices(analysis_table, rank, spread)
    weights = complex_weights(spectral_weight)
    spectra, synthesis_table, above, below, *analysis_parts = tie(
        spectra, synthesis_table, above, below, *analysis_parts
    )
    rows, corner = coefficient_blocks(spectra, analysis_parts)
    rows, above, below = tie(rows, above, below)
    rows = between_degrees(rows)
    synthesis_parts = legendre_matrices(synthesis_table, rank, spread)
    left, right = column_halo(above, grid_field, below)
    rows, left, right, weights, *synthesis_parts = tie(rows, left, right, weights, *synthesis_parts)
    corner, mixed, modes_high, modes_low = mix(rank, rows, corner, weights, order)
    mixed, left, right = tie(mixed, left, right)
    mixed = between_degrees(mixed)
    inputs = stencil(
        above, grid_field, below, left, right, disco_kernel, neighbour_offsets, lat_first, 1
    )
    local_part = jnp.einsum(
        "kabc,kcd->abd", inputs, disco_weight, preferred_element_type=jnp.float32
    )
    mixed, local_part, inputs = tie(mixed, local_part, inputs)
    waves = wave_blocks(mixed, corner, synthesis_parts, False)
    waves, later, cotangent = tie(waves, later, cotangent)
    waves = between_chips(waves)
    backward_table = lax.dynamic_index_in_dim(later, core, 0, keepdims=False)
    block_output, hidden_grad = on_device(
        activate_kernel,
        block_shapes * 2,
        (backward_table, waves, swap_cores(waves), local_part, cotangent),
        "activate",
        WAVE_FLOPS,
    )

    blocks = to_wave_blocks(hidden_grad, swap_cores(hidden_grad), forward_table)
    blocks, hidden_grad = tie(blocks, hidden_grad)
    above, below = row_halo(hidden_grad)
    grad_spectra = between_chips(blocks)
    grad_spectra, above, below, inputs = tie(grad_spectra, above, below, inputs)

    grad_rows, corner = coefficient_blocks(grad_spectra, synthesis_parts)
    grad_rows, above, below, inputs = tie(grad_rows, above, below, inputs)
    grad_rows = between_degrees(grad_rows)
    local_grad = jnp.einsum(
        "kabc,abd->kcd", inputs, hidden_grad, preferred_element_type=jnp.float32
    ) * (1.0 / math.sqrt(64 * LON_CELLS))
    halves = local_grad.reshape(2, 2 * CHANNELS, CHANNELS)
    kept = lax.dynamic_index_in_dim(halves, core, 0, keepdims=False)
    given = lax.dynamic_index_in_dim(halves, 1 - core, 0, keepdims=False)
    rider = (kept + swap_cores(given)).astype(jnp.bfloat16).reshape(96, 8, CHANNELS)
    left, right = column_halo(above, hidden_grad, below)
    grad_rows, left, right, rider = tie(grad_rows, left, right, rider)
    corner, back, grads_high, grads_low = mix(rank, grad_rows, corner, weights, order, rider)
    back, left, right = tie(back, left, right)
    back = between_degrees(back)
    back_inputs = stencil(
        above, hidden_grad, below, left, right, disco_kernel, neighbour_offsets, lat_first, -1
    )
    local_back = jnp.einsum(
        "kabd,kcd->abc", back_inputs, disco_weight, preferred_element_type=jnp.float32
    )
    back, local_back = tie(back, local_back)
    waves_back = wave_blocks(back, corner, analysis_parts, True)
    waves_back, grads_high, grads_low = tie(waves_back, grads_high, grads_low)
    waves_back = between_chips(waves_back)
    (spectral_grad,) = on_device(
        outer_kernel,
        [((2, 2, 2, CHANNELS, CHANNELS), jnp.float32)],
        (modes_high, grads_high, modes_low, grads_low),
        "outer",
        2 * 1536 * 768 * 768,
    )
    waves_back, spectral_grad = tie(waves_back, spectral_grad)
    sums = (2, 48, 2, 8, CHANNELS)
    field_grad, disco_grad = on_device(
        finish_kernel,
        [(BLOCK, jnp.bfloat16), (sums, jnp.float32)],
        (core.reshape(1), backward_table, waves_back, swap_cores(waves_back), local_back),
        "finish",
        WAVE_FLOPS,
        1,
        [pltpu.VMEM(sums, jnp.float32), pltpu.SemaphoreType.DMA((2,))],
        (),
        (1,),
    )
    return (
        block_output,
        field_grad,
        spectral_grad,
        disco_grad.reshape(4, CHANNELS, CHANNELS),
    )


def solution(mesh):
    forward_all, backward_all = wave_tables()
    place = np.arange(256)
    order = (place[:, None] == (place % 16 * 16 + place // 16)[None, :]).astype(ml_dtypes.bfloat16)
    split = Mesh(mesh.devices.reshape(32, 2, 2), ALL)
    lon = ("zhi", "core")
    return jax.shard_map(
        functools.partial(
            local,
            forward_all=forward_all,
            backward_all=backward_all,
            spread=spread_matrix(),
            order=order,
        ),
        mesh=split,
        in_specs=(
            P("lat", lon, None),
            P("lat", lon, None),
            P(None, ALL, None, None),
            P(None, ALL, None, None),
            P(None, ALL, None, None, None),
            P(),
            P(),
            P(),
        ),
        out_specs=(
            P("lat", lon, None),
            P("lat", lon, None),
            P(None, ALL, None, None, None),
            P(),
        ),
        check_vma=False,
    )
```

```python
import functools
import math

import jax
import jax.numpy as jnp
import ml_dtypes
import numpy as np
from jax import lax
from jax.experimental import pallas as pl
from jax.experimental.pallas import tpu as pltpu
from jax.sharding import Mesh
from jax.sharding import PartitionSpec as P

HALO_REACH = 2
LON_CELLS = 1440
LON_DEV = 360
CHANNELS = 384
DEGREES = 512
HALF = 256
DEVICES = 128
ALL = ("lat", "zhi", "core")
CHIPS = ("lat", "zhi")
SWAP = [(0, 1), (1, 0)]


def wave_tables():
    e, lh, p, ri = np.meshgrid(*map(np.arange, (64, 2, 2, 2)), indexing="ij")
    e, lh, p, ri = (v.reshape(-1) for v in (e, lh, p, ri))
    forward = np.zeros((2, 2, 512, LON_DEV), np.float32)
    backward = np.zeros((2, 2, LON_DEV, 512), np.float32)

    def basis(wave_core, cell_core):
        base = 4 * e + 2 * wave_core + p
        wave = np.where(lh == 0, base, DEGREES - 1 - base)
        column = np.arange(LON_DEV) + LON_DEV * cell_core
        angle = (wave[:, None] * column[None, :] % LON_CELLS) * (2.0 * math.pi / LON_CELLS)
        return np.where(ri[:, None] == 0, np.cos(angle), -np.sin(angle)) / math.sqrt(LON_CELLS)

    for core in range(2):
        for other in range(2):
            forward[core, other] = basis(core, core ^ other)
            backward[core, other] = basis(core ^ other, core).T
    return forward.astype(ml_dtypes.bfloat16), backward.astype(ml_dtypes.bfloat16)


def spread_matrix():
    row, lh, cp, cri = (
        v.reshape(-1) for v in np.meshgrid(*map(np.arange, (64, 2, 2, 2)), indexing="ij")
    )
    slh, sp, sa = (v.reshape(-1) for v in np.meshgrid(*map(np.arange, (2, 2, 64)), indexing="ij"))
    spread = (
        (slh[:, None] == lh[None, :]) & (sp[:, None] == cp[None, :]) & (sa[:, None] == row[None, :])
    )
    return spread.astype(np.float32).astype(ml_dtypes.bfloat16)


def tie(*values):
    return lax.optimization_barrier(values)


def dot(left, right):
    return jnp.dot(left, right, preferred_element_type=jnp.float32)


def dot_nt(left, right):
    return lax.dot_general(
        left, right, (((1,), (1,)), ((), ())), preferred_element_type=jnp.float32
    )


def one_hot(wanted, shape):
    degree = lax.broadcasted_iota(jnp.int32, shape, 1)
    return jnp.where(degree == wanted, 1.0, 0.0).astype(jnp.bfloat16)


def keep(rows, cols, values):
    return jnp.where(rows == cols, values, 0.0).astype(jnp.bfloat16)


def legendre_kernel(
    rank_ref,
    table_ref,
    spread_ref,
    turned_ref,
    matrix_hbm,
    flipped_hbm,
    matrix_ref,
    flipped_ref,
    sems,
):
    rank = rank_ref[0]
    saves = []
    lower = table_ref[0].reshape(128, DEGREES)
    upper = table_ref[1].reshape(128, DEGREES)
    spread = spread_ref[...]
    turned = turned_ref[...]

    def attributes(place):
        p, kind = (place >> 2) & 1, (place >> 3) & 1
        fold = 2 * (place >> 4) + (place & 1)
        high = jnp.where(2 * rank + p > fold, kind, 0)
        return kind, fold, ((place >> 1) & 3) + 4 * high

    for block in range(8):
        rows = slice(256 * block, 256 * (block + 1))
        place = lax.broadcasted_iota(jnp.int32, (256, 1), 0) + 256 * block
        kind, fold, code = attributes(place)
        last = DEGREES - 1 - fold
        low = one_hot(jnp.where(kind == 0, last, fold), (256, DEGREES))
        high = one_hot(jnp.where(kind == 0, -1, last), (256, DEGREES))
        picked = jnp.concatenate([dot_nt(low, lower), dot_nt(high, upper)], axis=1)
        picked = picked.astype(jnp.bfloat16)
        column = lax.broadcasted_iota(jnp.int32, (1, 512), 1) & 7
        matrix_ref[rows, :] = keep(code, column, dot(picked, spread))
        _, _, across = attributes(lax.broadcasted_iota(jnp.int32, (1, 256), 1) + 256 * block)
        down = lax.broadcasted_iota(jnp.int32, (512, 1), 0) & 7
        flipped_ref[:, rows] = keep(down, across, dot_nt(turned, picked))
        saves.append(started(matrix_ref.at[rows], matrix_hbm.at[rows], sems.at[0, block]))
        saves.append(started(flipped_ref.at[:, rows], flipped_hbm.at[:, rows], sems.at[1, block]))
    place = lax.broadcasted_iota(jnp.int32, (128, 1), 0)
    wanted = jnp.where(place < 4, DEGREES - 1 - (2 * rank + (place >> 1)), -1)
    edge = dot_nt(one_hot(wanted, (128, DEGREES)), upper).astype(jnp.bfloat16)
    column = lax.broadcasted_iota(jnp.int32, (1, 512), 1) & 7
    matrix_ref[2048:2064, :] = keep(place[:16] + 4, column, dot(edge[:16], spread[128:]))
    across = lax.broadcasted_iota(jnp.int32, (1, 128), 1) + 4
    down = lax.broadcasted_iota(jnp.int32, (512, 1), 0) & 7
    flipped_ref[:, 2048:2176] = keep(down, across, dot_nt(turned[:, 128:], edge))
    rows = slice(2048, 2064)
    saves.append(started(matrix_ref.at[rows], matrix_hbm.at[rows], sems.at[0, 8]))
    rows = slice(2048, 2176)
    saves.append(started(flipped_ref.at[:, rows], flipped_hbm.at[:, rows], sems.at[1, 8]))
    for save in saves:
        save.wait()


def chip_signs():
    line = lax.broadcasted_iota(jnp.int32, (1, 16, CHANNELS), 1)
    odd = ((line >> 2) ^ (line >> 1)) & 1
    return jnp.where(odd == 1, -1.0, 1.0)


def to_coefficients_kernel(
    matrix_hbm, spectra_ref, out_hbm, corner_ref, matrix_ref, out_ref, in_sems, out_sems
):
    parts = [slice(256 * block, 256 * (block + 1)) for block in range(8)] + [slice(2048, 2064)]
    loads = [
        started(matrix_hbm.at[rows], matrix_ref.at[rows], in_sems.at[n])
        for n, rows in enumerate(parts)
    ]
    saves = []
    both = spectra_ref[...].astype(jnp.float32)
    spectra = (both[:, 0] + chip_signs() * both[:, 1]).reshape(512, CHANNELS).astype(jnp.bfloat16)
    for block, rows in enumerate(parts[:8]):
        loads[block].wait()
        sums = dot(matrix_ref[rows, :], spectra)
        places = slice(16 * block, 16 * (block + 1))
        out_ref[places] = sums.astype(jnp.bfloat16).reshape(16, 16, CHANNELS)
        saves.append(started(out_ref.at[places], out_hbm.at[places], out_sems.at[block]))
    loads[8].wait()
    corner = dot(matrix_ref[parts[8], :], spectra).astype(jnp.bfloat16)
    corner_ref[...] = corner.astype(jnp.float32)
    for save in saves:
        save.wait()


def from_modes_kernel(
    flipped_hbm,
    rows_ref,
    corner_ref,
    out_hbm,
    flipped_ref,
    out_ref,
    in_sems,
    out_sems,
    *,
    rider,
):
    parts = [slice(128 * block, 128 * (block + 1)) for block in range(4)]
    loads = [
        started(flipped_hbm.at[lines], flipped_ref.at[lines], in_sems.at[n])
        for n, lines in enumerate(parts)
    ]
    saves = []
    rows = rows_ref[:, 0:16, :].reshape(2048, CHANNELS)
    corner = corner_ref[...].astype(jnp.bfloat16)
    if rider:
        shares = rows_ref[...].astype(jnp.float32).reshape(64, 2, 24, CHANNELS)[:, :, 16:24, :]
        owned = jnp.sum(shares, axis=0).reshape(16, CHANNELS).astype(jnp.bfloat16)
        out_ref[:, :, 16:32, :] = jnp.broadcast_to(owned[None, None], (32, 2, 16, CHANNELS))
    for block, lines in enumerate(parts):
        loads[block].wait()
        waves = dot(flipped_ref[lines, 0:2048], rows) + dot(flipped_ref[lines, 2048:2064], corner)
        waves = waves.reshape(8, 16, CHANNELS)
        places = slice(8 * block, 8 * (block + 1))
        out_ref[places, 0, 0:16, :] = waves.astype(jnp.bfloat16)
        out_ref[places, 1, 0:16, :] = (waves * chip_signs()).astype(jnp.bfloat16)
        saves.append(started(out_ref.at[places], out_hbm.at[places], out_sems.at[block]))
    for save in saves:
        save.wait()


def legendre_matrices(table, rank, spread):
    shapes = [((2064, 512), jnp.bfloat16), ((512, 2176), jnp.bfloat16)]
    operands = (rank.reshape(1), table, jnp.asarray(spread), jnp.asarray(spread.T))
    scratch = [
        pltpu.VMEM((2064, 512), jnp.bfloat16),
        pltpu.VMEM((512, 2176), jnp.bfloat16),
        pltpu.SemaphoreType.DMA((2, 9)),
    ]
    return on_device(
        legendre_kernel, shapes, operands, "legendre", 4_000_000_000, 1, scratch, (), (0, 1)
    )


def complex_weights(weight):
    real, imag = weight[:, :, 0], weight[:, :, 1]
    return jnp.concatenate(
        [jnp.concatenate([real, imag], axis=3), jnp.concatenate([-imag, real], axis=3)], axis=2
    )


def mix_kernel(
    rank_ref,
    rows_hbm,
    edge_ref,
    order_ref,
    weight_hbm,
    *refs,
    back,
):
    rider_ref, refs = (refs[0], refs[1:]) if back else (None, refs)
    (
        edge_out_ref,
        out_hbm,
        high_hbm,
        low_hbm,
        rows_ref,
        weight_ref,
        out_ref,
        high_ref,
        low_ref,
        mixed,
        row_sems,
        weight_sems,
        out_sems,
        saved_sems,
    ) = refs
    arrivals = []
    for block in range(8):
        sources = slice(16 * block, 16 * (block + 1))
        arrivals.append(started(rows_hbm.at[sources], rows_ref.at[sources], row_sems.at[block]))
    places = [(1, 0), (0, 0), (1, 1), (0, 1)]
    loads = [
        started(weight_hbm.at[k, j], weight_ref.at[k, j], weight_sems.at[n])
        for n, (k, j) in enumerate(places)
    ]
    order = order_ref[...]
    for block in range(8):
        arrivals[block].wait()
        rows = rows_ref[16 * block : 16 * block + 16, 0:16, :].reshape(256, CHANNELS)
        turned = dot(order, rows).astype(jnp.bfloat16)
        for q in range(16):
            kind, p, ri, j = q >> 3, (q >> 2) & 1, (q >> 1) & 1, q & 1
            piece = turned[16 * q : 16 * (q + 1), :]
            row = 128 * p + 16 * block
            lanes = slice(CHANNELS * ri, CHANNELS * (ri + 1))
            if kind == 0:
                high_ref[j, row : row + 16, lanes] = piece
            else:
                low_ref[j, row : row + 16, lanes] = piece
    place = lax.broadcasted_iota(jnp.int32, (256, 2 * CHANNELS), 0)
    base = 2 * (place & 127) + (place >> 7)
    product = dot_nt if back else dot
    saves = []
    for j in range(2):
        fold = 2 * rank_ref[0] + j
        both = low_ref[j].astype(jnp.float32)
        edge = jnp.concatenate(
            [edge_ref[2 * j : 2 * j + 1, :], edge_ref[2 * j + 1 : 2 * j + 2, :]], axis=1
        )
        high_ref[j, 256:512, :] = jnp.where(
            base > fold, both, jnp.where(base == fold, edge, 0.0)
        ).astype(jnp.bfloat16)
        low_ref[j] = jnp.where(base <= fold, both, 0.0).astype(jnp.bfloat16)
        saves.append(started(high_ref.at[j], high_hbm.at[j], saved_sems.at[2 * j]))
        saves.append(started(low_ref.at[j], low_hbm.at[j], saved_sems.at[2 * j + 1]))
        loads[2 * j].wait()
        mixed[0, j] = product(high_ref[j, 0:256, :], weight_ref[1, j]).astype(jnp.bfloat16)
        high = product(high_ref[j, 256:512, :], weight_ref[1, j])
        loads[2 * j + 1].wait()
        low = product(low_ref[j], weight_ref[0, j])
        mixed[1, j] = jnp.where(base <= fold, low, high).astype(jnp.bfloat16)
        corner = jnp.sum(jnp.where(base == fold, high, 0.0), axis=0, keepdims=True)
        edge_out_ref[2 * j : 2 * j + 1, :] = corner[:, :CHANNELS]
        edge_out_ref[2 * j + 1 : 2 * j + 2, :] = corner[:, CHANNELS:]
    edge_out_ref[4:16, :] = jnp.zeros((12, CHANNELS), jnp.float32)
    if rider_ref is not None:
        out_ref[0:96, 16:24, :] = rider_ref[...]
        out_ref[96:128, 16:24, :] = jnp.zeros((32, 8, CHANNELS), jnp.bfloat16)
    for block in range(8):
        pieces = []
        for q in range(16):
            kind, p, ri, j = q >> 3, (q >> 2) & 1, (q >> 1) & 1, q & 1
            row = 128 * p + 16 * block
            pieces.append(mixed[kind, j, row : row + 16, CHANNELS * ri : CHANNELS * (ri + 1)])
        turned = dot(order, jnp.concatenate(pieces, axis=0))
        owners = slice(16 * block, 16 * (block + 1))
        out_ref[owners, 0:16, :] = turned.astype(jnp.bfloat16).reshape(16, 16, CHANNELS)
        saves.append(started(out_ref.at[owners], out_hbm.at[owners], out_sems.at[block]))
    for save in saves:
        save.wait()


def mix(rank, rows, edge, weights, order, rider=None):
    back = rider is not None
    flops = 2 * 1536 * 768 * 768 + 4 * 2048 * 256 * 384
    blocks = (DEVICES, 24 if back else 16, CHANNELS)
    high, low = (2, 512, 2 * CHANNELS), (2, 256, 2 * CHANNELS)
    operands = (rank.reshape(1), rows, edge, order, weights) + ((rider,) if back else ())
    shapes = [
        ((16, CHANNELS), jnp.float32),
        (blocks, jnp.bfloat16),
        (high, jnp.bfloat16),
        (low, jnp.bfloat16),
    ]
    scratch = [
        pltpu.VMEM((DEVICES, 16, CHANNELS), jnp.bfloat16),
        pltpu.VMEM((2, 2, 2 * CHANNELS, 2 * CHANNELS), jnp.bfloat16),
        pltpu.VMEM(blocks, jnp.bfloat16),
        pltpu.VMEM(high, jnp.bfloat16),
        pltpu.VMEM(low, jnp.bfloat16),
        pltpu.VMEM((2, 2, 256, 2 * CHANNELS), jnp.bfloat16),
        pltpu.SemaphoreType.DMA((8,)),
        pltpu.SemaphoreType.DMA((4,)),
        pltpu.SemaphoreType.DMA((8,)),
        pltpu.SemaphoreType.DMA((4,)),
    ]
    return on_device(
        functools.partial(mix_kernel, back=back),
        shapes,
        operands,
        "mix_back" if back else "mix_modes",
        flops,
        1,
        scratch,
        (1, 4),
        (1, 2, 3),
    )


def forward_kernel(table_ref, mine_ref, other_ref, out_ref):
    for part in range(4):
        rows = slice(128 * part, 128 * (part + 1))
        lines = []
        for a in range(2):
            sums = dot(table_ref[0, rows, :], mine_ref[a]) + dot(table_ref[1, rows, :], other_ref[a])
            lines.append(sums.reshape(16, 8, CHANNELS))
        out_ref[16 * part : 16 * (part + 1)] = jnp.concatenate(lines, axis=1).astype(jnp.bfloat16)


def inverse_rows(table_ref, mine, other, a):
    def pick(waves):
        return waves[:, 8 * a : 8 * (a + 1), :].reshape(512, CHANNELS).astype(jnp.bfloat16)

    sums = dot(table_ref[0], pick(mine)) + dot(table_ref[1], pick(other))
    return sums.astype(jnp.bfloat16).astype(jnp.float32)


def activate_kernel(table_ref, mine_ref, other_ref, local_ref, cotangent_ref, out_ref, grad_ref):
    mine = mine_ref[:, 0:16, :].astype(jnp.float32)
    other = other_ref[:, 0:16, :].astype(jnp.float32)
    scale = math.sqrt(2.0 / math.pi)
    for a in range(2):
        v = inverse_rows(table_ref, mine, other, a) + local_ref[a]
        square = v * v
        t = jnp.tanh(scale * (v + 0.044715 * (v * square)))
        half = 0.5 * (1.0 + t)
        out_ref[a] = (v * half).astype(jnp.bfloat16)
        slope = half + 0.5 * v * (1.0 - t * t) * (scale * (1.0 + 3 * 0.044715 * square))
        grad_ref[a] = (cotangent_ref[a].astype(jnp.float32) * slope).astype(jnp.bfloat16)


def finish_kernel(
    core_ref, table_ref, mine_ref, other_ref, local_ref, out_ref, sums_hbm, sums_ref, sems
):
    mine = mine_ref[...].astype(jnp.float32)
    other = other_ref[...].astype(jnp.float32)
    saves = []
    for half in range(2):
        rows = slice(16 + 8 * half, 24 + 8 * half)
        pair = [mine[:48, rows, :], other[:48, rows, :]]
        for core in range(2):
            kept = jnp.where(core_ref[0] == core, pair[0], pair[1])
            sums_ref[half, :, core] = kept
        saves.append(started(sums_ref.at[half], sums_hbm.at[half], sems.at[half]))
    for a in range(2):
        total = inverse_rows(table_ref, mine[:, :16], other[:, :16], a) + local_ref[a]
        out_ref[a] = total.astype(jnp.bfloat16)
    for save in saves:
        save.wait()


MARGIN = 8
CHUNK = 40


def stencil_kernel(
    weight_ref,
    corner_ref,
    above_ref,
    mine_ref,
    below_ref,
    left_ref,
    right_ref,
    out_ref,
    line,
    shifted,
    sums,
    *,
    sign,
):
    blocks = (above_ref, mine_ref, below_ref)
    for row in range(6):
        line[MARGIN : MARGIN + LON_DEV, :] = blocks[row // 2][row % 2].astype(jnp.float32)
        line[MARGIN - HALO_REACH : MARGIN, :] = left_ref[row]
        line[MARGIN + LON_DEV : MARGIN + LON_DEV + HALO_REACH, :] = right_ref[row]
        for shift in range(5):
            first = MARGIN - HALO_REACH + shift
            shifted[shift, row] = line[first : first + LON_DEV, :]

    def step(index, carry):
        first = pl.multiple_of(index * CHUNK, 8)
        for a in range(2):
            for lane in range(3):
                lanes = slice(128 * lane, 128 * (lane + 1))
                totals = [jnp.zeros((CHUNK, 128), jnp.float32)] * 4
                for n in range(9):
                    row = sign * corner_ref[n, 0] + HALO_REACH + a
                    column = sign * corner_ref[n, 1] + HALO_REACH
                    cells = shifted[column, row, pl.ds(first, CHUNK), lanes]
                    totals = [totals[k] + weight_ref[8 * n + 2 * k + a] * cells for k in range(4)]
                for k in range(4):
                    sums[k, a, pl.ds(first, CHUNK), lanes] = totals[k]
        return carry

    lax.fori_loop(0, LON_DEV // CHUNK, step, 0)
    for k in range(4):
        for a in range(2):
            out_ref[k, a] = sums[k, a].astype(jnp.bfloat16)


def outer_kernel(high_ref, high_grad_ref, low_ref, low_grad_ref, out_ref):
    c = CHANNELS
    for kind, (left_ref, right_ref) in enumerate(((low_ref, low_grad_ref), (high_ref, high_grad_ref))):
        for j in range(2):
            right = right_ref[j]
            across = (((0,), (0,)), ((), ()))
            first = lax.dot_general(
                left_ref[j, :, :c], right, across, preferred_element_type=jnp.float32
            )
            second = lax.dot_general(
                left_ref[j, :, c:], right, across, preferred_element_type=jnp.float32
            )
            out_ref[kind, j, 0] = first[:, :c] + second[:, c:]
            out_ref[kind, j, 1] = first[:, c:] - second[:, :c]


def on_device(
    kernel, shapes, operands, name, flops, scalars=0, scratch=(), far_in=(), far_out=()
):
    vmem = pl.BlockSpec(memory_space=pltpu.VMEM)
    smem = pl.BlockSpec(memory_space=pltpu.SMEM)
    far = pl.BlockSpec(memory_space=pltpu.HBM)
    moved = sum(math.prod(v.shape) * v.dtype.itemsize for v in operands)
    moved += sum(math.prod(size) * jnp.dtype(kind).itemsize for size, kind in shapes)
    shapes = [
        pltpu.HBM(*s) if n in far_out else jax.ShapeDtypeStruct(*s) for n, s in enumerate(shapes)
    ]
    operands = [
        pltpu.with_memory_space_constraint(v, pltpu.HBM) if n in far_in else v
        for n, v in enumerate(operands)
    ]
    ins = [smem if n < scalars else far if n in far_in else vmem for n in range(len(operands))]
    return pl.pallas_call(
        kernel,
        out_shape=tuple(shapes),
        in_specs=ins,
        out_specs=tuple(far if n in far_out else vmem for n in range(len(shapes))),
        scratch_shapes=list(scratch),
        compiler_params=pltpu.CompilerParams(vmem_limit_bytes=48 * 1024 * 1024),
        cost_estimate=pl.CostEstimate(flops=flops, bytes_accessed=moved, transcendentals=0),
        name=name,
    )(*operands)


def started(source, target, sem):
    copy = pltpu.make_async_copy(source, target, sem)
    copy.start()
    return copy


BLOCK = (2, LON_DEV, CHANNELS)
WAVE_FLOPS = 2 * 512 * 720 * 768


def swap_cores(values):
    return lax.ppermute(values, "core", SWAP)


def edges_kernel(above_ref, block_ref, below_ref, tail_ref, head_ref):
    for n, ref in enumerate((above_ref, block_ref, below_ref)):
        for a in range(2):
            cells = ref[a].astype(jnp.float32)
            tail_ref[2 * n + a] = cells[LON_DEV - HALO_REACH :]
            head_ref[2 * n + a] = cells[:HALO_REACH]


def to_wave_blocks(mine, other, table):
    shapes = [((64, 16, CHANNELS), jnp.bfloat16)]
    return on_device(forward_kernel, shapes, (table, mine, other), "to_waves", WAVE_FLOPS)[0]


def between_chips(blocks):
    return lax.all_to_all(blocks, CHIPS, split_axis=0, concat_axis=0, tiled=True)


def between_degrees(blocks):
    return lax.all_to_all(blocks, ALL, split_axis=0, concat_axis=0, tiled=True)


def coefficient_blocks(spectra, matrices):
    matrix, flipped = matrices
    operands = (matrix, spectra.reshape(32, 2, 16, CHANNELS))
    blocks = (DEVICES, 16, CHANNELS)
    shapes = [(blocks, jnp.bfloat16), ((16, CHANNELS), jnp.float32)]
    scratch = [
        pltpu.VMEM((2064, 512), jnp.bfloat16),
        pltpu.VMEM(blocks, jnp.bfloat16),
        pltpu.SemaphoreType.DMA((9,)),
        pltpu.SemaphoreType.DMA((8,)),
    ]
    flops = 2 * 2048 * 512 * 512
    return on_device(
        to_coefficients_kernel, shapes, operands, "to_coefficients", flops, 0, scratch, (0,), (0,)
    )


def wave_blocks(rows, corner, matrices, rider):
    matrix, flipped = matrices
    blocks = (32, 2, 32 if rider else 16, CHANNELS)
    scratch = [
        pltpu.VMEM((512, 2176), jnp.bfloat16),
        pltpu.VMEM(blocks, jnp.bfloat16),
        pltpu.SemaphoreType.DMA((4,)),
        pltpu.SemaphoreType.DMA((4,)),
    ]
    (out,) = on_device(
        functools.partial(from_modes_kernel, rider=rider),
        [(blocks, jnp.bfloat16)],
        (flipped, rows, corner),
        "from_modes",
        2 * 2048 * 512 * 512,
        0,
        scratch,
        (0,),
        (0,),
    )
    return out.reshape(64, -1, CHANNELS)


def row_halo(block):
    above = lax.ppermute(block, "lat", [(i, i + 1) for i in range(31)])
    below = lax.ppermute(block, "lat", [(i + 1, i) for i in range(31)])
    return above, below


def column_halo(above, block, below):
    shapes = [((6, HALO_REACH, CHANNELS), jnp.float32)] * 2
    tails, heads = on_device(edges_kernel, shapes, (above, block, below), "edges", 0)
    lon = ("zhi", "core")
    left = lax.ppermute(tails, lon, [(i, (i + 1) % 4) for i in range(4)])
    right = lax.ppermute(heads, lon, [((i + 1) % 4, i) for i in range(4)])
    return left, right


def stencil(above, block, below, left, right, disco_kernel, offsets, lat_first, sign):
    row = lat_first + jnp.arange(2, dtype=jnp.int32)[None, :]
    row = row - offsets[:, :1] if sign < 0 else row + jnp.zeros_like(offsets[:, :1])
    chosen = row[:, :, None] == jnp.arange(64, dtype=jnp.int32)[None, None, :]
    weights = jnp.sum(
        jnp.where(chosen[:, None], disco_kernel[:, :, None, :], 0.0), axis=-1
    ).reshape(-1)
    operands = (weights, offsets, above, block, below, left, right)
    scratch = [
        pltpu.VMEM((LON_DEV + 2 * MARGIN, CHANNELS), jnp.float32),
        pltpu.VMEM((5, 6, LON_DEV, CHANNELS), jnp.float32),
        pltpu.VMEM((4, *BLOCK), jnp.float32),
    ]
    shapes = [((4, *BLOCK), jnp.bfloat16)]
    name = "stencil" if sign > 0 else "stencil_back"
    flops = 2 * 36 * math.prod(BLOCK) * 16
    kernel = functools.partial(stencil_kernel, sign=sign)
    return on_device(kernel, shapes, operands, name, flops, 2, scratch)[0]


def local(
    grid_field,
    cotangent,
    analysis_table,
    synthesis_table,
    spectral_weight,
    disco_weight,
    disco_kernel,
    neighbour_offsets,
    *,
    forward_all,
    backward_all,
    spread,
    order,
):
    lat, zhi, core = (lax.axis_index(name) for name in ALL)
    rank = lat * 4 + zhi * 2 + core
    lat_first = lat * 2
    forward_table = lax.dynamic_index_in_dim(jnp.asarray(forward_all), core, 0, keepdims=False)
    order = jnp.asarray(order)
    block_shapes = [(BLOCK, jnp.bfloat16)]

    grid_other = swap_cores(grid_field)
    above, below = row_halo(grid_field)
    blocks = to_wave_blocks(grid_field, grid_other, forward_table)
    blocks, analysis_table, spectral_weight, later = tie(
        blocks, analysis_table, spectral_weight, jnp.asarray(backward_all)
    )
    spectra = between_chips(blocks)
    analysis_parts = legendre_matrices(analysis_table, rank, spread)
    weights = complex_weights(spectral_weight)
    spectra, synthesis_table, above, below, *analysis_parts = tie(
        spectra, synthesis_table, above, below, *analysis_parts
    )
    rows, corner = coefficient_blocks(spectra, analysis_parts)
    rows, above, below = tie(rows, above, below)
    rows = between_degrees(rows)
    synthesis_parts = legendre_matrices(synthesis_table, rank, spread)
    left, right = column_halo(above, grid_field, below)
    rows, left, right, weights, *synthesis_parts = tie(rows, left, right, weights, *synthesis_parts)
    corner, mixed, modes_high, modes_low = mix(rank, rows, corner, weights, order)
    mixed, left, right = tie(mixed, left, right)
    mixed = between_degrees(mixed)
    inputs = stencil(
        above, grid_field, below, left, right, disco_kernel, neighbour_offsets, lat_first, 1
    )
    local_part = jnp.einsum(
        "kabc,kcd->abd", inputs, disco_weight, preferred_element_type=jnp.float32
    )
    mixed, local_part, inputs = tie(mixed, local_part, inputs)
    waves = wave_blocks(mixed, corner, synthesis_parts, False)
    waves, later, cotangent = tie(waves, later, cotangent)
    waves = between_chips(waves)
    backward_table = lax.dynamic_index_in_dim(later, core, 0, keepdims=False)
    block_output, hidden_grad = on_device(
        activate_kernel,
        block_shapes * 2,
        (backward_table, waves, swap_cores(waves), local_part, cotangent),
        "activate",
        WAVE_FLOPS,
    )

    blocks = to_wave_blocks(hidden_grad, swap_cores(hidden_grad), forward_table)
    blocks, hidden_grad = tie(blocks, hidden_grad)
    above, below = row_halo(hidden_grad)
    grad_spectra = between_chips(blocks)
    grad_spectra, above, below, inputs = tie(grad_spectra, above, below, inputs)

    grad_rows, corner = coefficient_blocks(grad_spectra, synthesis_parts)
    grad_rows, above, below, inputs = tie(grad_rows, above, below, inputs)
    grad_rows = between_degrees(grad_rows)
    local_grad = jnp.einsum(
        "kabc,abd->kcd", inputs, hidden_grad, preferred_element_type=jnp.float32
    ) * (1.0 / math.sqrt(64 * LON_CELLS))
    halves = local_grad.reshape(2, 2 * CHANNELS, CHANNELS)
    kept = lax.dynamic_index_in_dim(halves, core, 0, keepdims=False)
    given = lax.dynamic_index_in_dim(halves, 1 - core, 0, keepdims=False)
    rider = (kept + swap_cores(given)).astype(jnp.bfloat16).reshape(96, 8, CHANNELS)
    left, right = column_halo(above, hidden_grad, below)
    grad_rows, left, right, rider = tie(grad_rows, left, right, rider)
    corner, back, grads_high, grads_low = mix(rank, grad_rows, corner, weights, order, rider)
    back, left, right = tie(back, left, right)
    back = between_degrees(back)
    back_inputs = stencil(
        above, hidden_grad, below, left, right, disco_kernel, neighbour_offsets, lat_first, -1
    )
    local_back = jnp.einsum(
        "kabd,kcd->abc", back_inputs, disco_weight, preferred_element_type=jnp.float32
    )
    back, local_back = tie(back, local_back)
    waves_back = wave_blocks(back, corner, analysis_parts, True)
    waves_back, grads_high, grads_low = tie(waves_back, grads_high, grads_low)
    waves_back = between_chips(waves_back)
    (spectral_grad,) = on_device(
        outer_kernel,
        [((2, 2, 2, CHANNELS, CHANNELS), jnp.float32)],
        (modes_high, grads_high, modes_low, grads_low),
        "outer",
        2 * 1536 * 768 * 768,
    )
    waves_back, spectral_grad = tie(waves_back, spectral_grad)
    sums = (2, 48, 2, 8, CHANNELS)
    field_grad, disco_grad = on_device(
        finish_kernel,
        [(BLOCK, jnp.bfloat16), (sums, jnp.float32)],
        (core.reshape(1), backward_table, waves_back, swap_cores(waves_back), local_back),
        "finish",
        WAVE_FLOPS,
        1,
        [pltpu.VMEM(sums, jnp.float32), pltpu.SemaphoreType.DMA((2,))],
        (),
        (1,),
    )
    return (
        block_output,
        field_grad,
        spectral_grad,
        disco_grad.reshape(4, CHANNELS, CHANNELS),
    )


def solution(mesh):
    forward_all, backward_all = wave_tables()
    place = np.arange(256)
    order = (place[:, None] == (place % 16 * 16 + place // 16)[None, :]).astype(ml_dtypes.bfloat16)
    split = Mesh(mesh.devices.reshape(32, 2, 2), ALL)
    lon = ("zhi", "core")
    return jax.shard_map(
        functools.partial(
            local,
            forward_all=forward_all,
            backward_all=backward_all,
            spread=spread_matrix(),
            order=order,
        ),
        mesh=split,
        in_specs=(
            P("lat", lon, None),
            P("lat", lon, None),
            P(None, ALL, None, None),
            P(None, ALL, None, None),
            P(None, ALL, None, None, None),
            P(),
            P(),
            P(),
        ),
        out_specs=(
            P("lat", lon, None),
            P("lat", lon, None),
            P(None, ALL, None, None, None),
            P(),
        ),
        check_vma=False,
    )
```

```python
import functools
import math

import jax
import jax.numpy as jnp
import ml_dtypes
import numpy as np
from jax import lax
from jax.experimental import pallas as pl
from jax.experimental.pallas import tpu as pltpu
from jax.sharding import Mesh
from jax.sharding import PartitionSpec as P

HALO_REACH = 2
LON_CELLS = 1440
LON_DEV = 360
CHANNELS = 384
DEGREES = 512
HALF = 256
DEVICES = 128
ALL = ("lat", "zhi", "core")
CHIPS = ("lat", "zhi")
SWAP = [(0, 1), (1, 0)]


def wave_tables():
    e, lh, p, ri = np.meshgrid(*map(np.arange, (64, 2, 2, 2)), indexing="ij")
    e, lh, p, ri = (v.reshape(-1) for v in (e, lh, p, ri))
    forward = np.zeros((2, 2, 512, LON_DEV), np.float32)
    backward = np.zeros((2, 2, LON_DEV, 512), np.float32)

    def basis(wave_core, cell_core):
        base = 4 * e + 2 * wave_core + p
        wave = np.where(lh == 0, base, DEGREES - 1 - base)
        column = np.arange(LON_DEV) + LON_DEV * cell_core
        angle = (wave[:, None] * column[None, :] % LON_CELLS) * (2.0 * math.pi / LON_CELLS)
        return np.where(ri[:, None] == 0, np.cos(angle), -np.sin(angle)) / math.sqrt(LON_CELLS)

    for core in range(2):
        for other in range(2):
            forward[core, other] = basis(core, core ^ other)
            backward[core, other] = basis(core ^ other, core).T
    return forward.astype(ml_dtypes.bfloat16), backward.astype(ml_dtypes.bfloat16)


def spread_matrix():
    row, lh, cp, cri = (
        v.reshape(-1) for v in np.meshgrid(*map(np.arange, (64, 2, 2, 2)), indexing="ij")
    )
    slh, sp, sa = (v.reshape(-1) for v in np.meshgrid(*map(np.arange, (2, 2, 64)), indexing="ij"))
    spread = (
        (slh[:, None] == lh[None, :]) & (sp[:, None] == cp[None, :]) & (sa[:, None] == row[None, :])
    )
    return spread.astype(np.float32).astype(ml_dtypes.bfloat16)


def tie(*values):
    return lax.optimization_barrier(values)


def dot(left, right):
    return jnp.dot(left, right, preferred_element_type=jnp.float32)


def dot_nt(left, right):
    return lax.dot_general(
        left, right, (((1,), (1,)), ((), ())), preferred_element_type=jnp.float32
    )


def one_hot(wanted, shape):
    degree = lax.broadcasted_iota(jnp.int32, shape, 1)
    return jnp.where(degree == wanted, 1.0, 0.0).astype(jnp.bfloat16)


def keep(rows, cols, values):
    return jnp.where(rows == cols, values, 0.0).astype(jnp.bfloat16)


def legendre_kernel(
    rank_ref,
    table_ref,
    spread_ref,
    turned_ref,
    matrix_hbm,
    flipped_hbm,
    matrix_ref,
    flipped_ref,
    sems,
):
    rank = rank_ref[0]
    saves = []
    lower = table_ref[0].reshape(128, DEGREES)
    upper = table_ref[1].reshape(128, DEGREES)
    spread = spread_ref[...]
    turned = turned_ref[...]

    def attributes(place):
        p, kind = (place >> 2) & 1, (place >> 3) & 1
        fold = 2 * (place >> 4) + (place & 1)
        high = jnp.where(2 * rank + p > fold, kind, 0)
        return kind, fold, ((place >> 1) & 3) + 4 * high

    for block in range(8):
        rows = slice(256 * block, 256 * (block + 1))
        place = lax.broadcasted_iota(jnp.int32, (256, 1), 0) + 256 * block
        kind, fold, code = attributes(place)
        last = DEGREES - 1 - fold
        low = one_hot(jnp.where(kind == 0, last, fold), (256, DEGREES))
        high = one_hot(jnp.where(kind == 0, -1, last), (256, DEGREES))
        picked = jnp.concatenate([dot_nt(low, lower), dot_nt(high, upper)], axis=1)
        picked = picked.astype(jnp.bfloat16)
        column = lax.broadcasted_iota(jnp.int32, (1, 512), 1) & 7
        matrix_ref[rows, :] = keep(code, column, dot(picked, spread))
        _, _, across = attributes(lax.broadcasted_iota(jnp.int32, (1, 256), 1) + 256 * block)
        down = lax.broadcasted_iota(jnp.int32, (512, 1), 0) & 7
        flipped_ref[:, rows] = keep(down, across, dot_nt(turned, picked))
        saves.append(started(matrix_ref.at[rows], matrix_hbm.at[rows], sems.at[0, block]))
        saves.append(started(flipped_ref.at[:, rows], flipped_hbm.at[:, rows], sems.at[1, block]))
    place = lax.broadcasted_iota(jnp.int32, (128, 1), 0)
    wanted = jnp.where(place < 4, DEGREES - 1 - (2 * rank + (place >> 1)), -1)
    edge = dot_nt(one_hot(wanted, (128, DEGREES)), upper).astype(jnp.bfloat16)
    column = lax.broadcasted_iota(jnp.int32, (1, 512), 1) & 7
    matrix_ref[2048:2064, :] = keep(place[:16] + 4, column, dot(edge[:16], spread[128:]))
    across = lax.broadcasted_iota(jnp.int32, (1, 128), 1) + 4
    down = lax.broadcasted_iota(jnp.int32, (512, 1), 0) & 7
    flipped_ref[:, 2048:2176] = keep(down, across, dot_nt(turned[:, 128:], edge))
    rows = slice(2048, 2064)
    saves.append(started(matrix_ref.at[rows], matrix_hbm.at[rows], sems.at[0, 8]))
    rows = slice(2048, 2176)
    saves.append(started(flipped_ref.at[:, rows], flipped_hbm.at[:, rows], sems.at[1, 8]))
    for save in saves:
        save.wait()


def chip_signs():
    line = lax.broadcasted_iota(jnp.int32, (1, 16, CHANNELS), 1)
    odd = ((line >> 2) ^ (line >> 1)) & 1
    return jnp.where(odd == 1, -1.0, 1.0)


def to_coefficients_kernel(
    matrix_hbm, spectra_ref, out_hbm, corner_ref, matrix_ref, out_ref, in_sems, out_sems
):
    parts = [slice(256 * block, 256 * (block + 1)) for block in range(8)] + [slice(2048, 2064)]
    loads = [
        started(matrix_hbm.at[rows], matrix_ref.at[rows], in_sems.at[n])
        for n, rows in enumerate(parts)
    ]
    saves = []
    both = spectra_ref[...].astype(jnp.float32)
    spectra = (both[:, 0] + chip_signs() * both[:, 1]).reshape(512, CHANNELS).astype(jnp.bfloat16)
    for block, rows in enumerate(parts[:8]):
        loads[block].wait()
        sums = dot(matrix_ref[rows, :], spectra)
        places = slice(16 * block, 16 * (block + 1))
        out_ref[places] = sums.astype(jnp.bfloat16).reshape(16, 16, CHANNELS)
        saves.append(started(out_ref.at[places], out_hbm.at[places], out_sems.at[block]))
    loads[8].wait()
    corner = dot(matrix_ref[parts[8], :], spectra).astype(jnp.bfloat16)
    corner_ref[...] = corner.astype(jnp.float32)
    for save in saves:
        save.wait()


def from_modes_kernel(
    flipped_hbm,
    rows_ref,
    corner_ref,
    out_hbm,
    flipped_ref,
    out_ref,
    in_sems,
    out_sems,
    *,
    rider,
):
    parts = [slice(128 * block, 128 * (block + 1)) for block in range(4)]
    loads = [
        started(flipped_hbm.at[lines], flipped_ref.at[lines], in_sems.at[n])
        for n, lines in enumerate(parts)
    ]
    saves = []
    rows = rows_ref[:, 0:16, :].reshape(2048, CHANNELS)
    corner = corner_ref[...].astype(jnp.bfloat16)
    if rider:
        shares = rows_ref[...].astype(jnp.float32).reshape(64, 2, 24, CHANNELS)[:, :, 16:24, :]
        owned = jnp.sum(shares, axis=0).reshape(16, CHANNELS).astype(jnp.bfloat16)
        out_ref[:, :, 16:32, :] = jnp.broadcast_to(owned[None, None], (32, 2, 16, CHANNELS))
    for block, lines in enumerate(parts):
        loads[block].wait()
        waves = dot(flipped_ref[lines, 0:2048], rows) + dot(flipped_ref[lines, 2048:2064], corner)
        waves = waves.reshape(8, 16, CHANNELS)
        places = slice(8 * block, 8 * (block + 1))
        out_ref[places, 0, 0:16, :] = waves.astype(jnp.bfloat16)
        out_ref[places, 1, 0:16, :] = (waves * chip_signs()).astype(jnp.bfloat16)
        saves.append(started(out_ref.at[places], out_hbm.at[places], out_sems.at[block]))
    for save in saves:
        save.wait()


def legendre_matrices(table, rank, spread):
    shapes = [((2064, 512), jnp.bfloat16), ((512, 2176), jnp.bfloat16)]
    operands = (rank.reshape(1), table, jnp.asarray(spread), jnp.asarray(spread.T))
    scratch = [
        pltpu.VMEM((2064, 512), jnp.bfloat16),
        pltpu.VMEM((512, 2176), jnp.bfloat16),
        pltpu.SemaphoreType.DMA((2, 9)),
    ]
    return on_device(
        legendre_kernel, shapes, operands, "legendre", 4_000_000_000, 1, scratch, (), (0, 1)
    )


def unfold(rows_of, order, edge_ref, rank, high_ref, low_ref):
    for block in range(8):
        turned = dot(order, rows_of(block)).astype(jnp.bfloat16)
        for q in range(16):
            kind, p, ri, j = q >> 3, (q >> 2) & 1, (q >> 1) & 1, q & 1
            piece = turned[16 * q : 16 * (q + 1), :]
            row = 128 * p + 16 * block
            lanes = slice(CHANNELS * ri, CHANNELS * (ri + 1))
            if kind == 0:
                high_ref[j, row : row + 16, lanes] = piece
            else:
                low_ref[j, row : row + 16, lanes] = piece
    base = wave_places()
    for j in range(2):
        fold = 2 * rank + j
        both = low_ref[j].astype(jnp.float32)
        edge = jnp.concatenate(
            [edge_ref[2 * j : 2 * j + 1, :], edge_ref[2 * j + 1 : 2 * j + 2, :]], axis=1
        )
        high_ref[j, 256:512, :] = jnp.where(
            base > fold, both, jnp.where(base == fold, edge, 0.0)
        ).astype(jnp.bfloat16)
        low_ref[j] = jnp.where(base <= fold, both, 0.0).astype(jnp.bfloat16)


def wave_places():
    place = lax.broadcasted_iota(jnp.int32, (256, 2 * CHANNELS), 0)
    return 2 * (place & 127) + (place >> 7)


def complex_product(rows, weight, back):
    c = CHANNELS
    if back:
        turned = jnp.concatenate([rows[:, c:], -rows[:, :c]], axis=1)
        return jnp.concatenate([dot_nt(rows, weight), dot_nt(turned, weight)], axis=1)
    real, imag = dot(rows[:, :c], weight), dot(rows[:, c:], weight)
    return jnp.concatenate([real[:, :c] - imag[:, c:], real[:, c:] + imag[:, :c]], axis=1)


def mix_kernel(rank_ref, rows_hbm, edge_ref, order_ref, weight_hbm, *refs, back):
    rider_ref, refs = (refs[0], refs[1:]) if back else (None, refs)
    edge_out_ref, out_hbm, rows_ref, weight_ref, out_ref, high_ref, low_ref, mixed, *sems = refs
    row_sems, weight_sems, out_sems = sems
    arrivals = []
    for block in range(8):
        sources = slice(16 * block, 16 * (block + 1))
        arrivals.append(started(rows_hbm.at[sources], rows_ref.at[sources], row_sems.at[block]))
    loads = {}
    for n, (kind, j) in enumerate(((1, 0), (0, 0), (1, 1), (0, 1))):
        loads[kind, j] = [
            started(
                weight_hbm.at[kind, j, ri],
                weight_ref.at[kind, j, :, CHANNELS * ri : CHANNELS * (ri + 1)],
                weight_sems.at[n, ri],
            )
            for ri in range(2)
        ]
    order = order_ref[...]

    def rows_of(block):
        arrivals[block].wait()
        return rows_ref[16 * block : 16 * block + 16].reshape(256, CHANNELS)

    unfold(rows_of, order, edge_ref, rank_ref[0], high_ref, low_ref)
    base = wave_places()
    for j in range(2):
        fold = 2 * rank_ref[0] + j
        for load in loads[1, j]:
            load.wait()
        first = complex_product(high_ref[j, 0:256, :], weight_ref[1, j], back)
        mixed[0, j] = first.astype(jnp.bfloat16)
        high = complex_product(high_ref[j, 256:512, :], weight_ref[1, j], back)
        for load in loads[0, j]:
            load.wait()
        low = complex_product(low_ref[j], weight_ref[0, j], back)
        mixed[1, j] = jnp.where(base <= fold, low, high).astype(jnp.bfloat16)
        corner = jnp.sum(jnp.where(base == fold, high, 0.0), axis=0, keepdims=True)
        edge_out_ref[2 * j : 2 * j + 1, :] = corner[:, :CHANNELS]
        edge_out_ref[2 * j + 1 : 2 * j + 2, :] = corner[:, CHANNELS:]
    edge_out_ref[4:16, :] = jnp.zeros((12, CHANNELS), jnp.float32)
    if rider_ref is not None:
        out_ref[0:96, 16:24, :] = rider_ref[...]
        out_ref[96:128, 16:24, :] = jnp.zeros((32, 8, CHANNELS), jnp.bfloat16)
    saves = []
    for block in range(8):
        pieces = []
        for q in range(16):
            kind, p, ri, j = q >> 3, (q >> 2) & 1, (q >> 1) & 1, q & 1
            row = 128 * p + 16 * block
            pieces.append(mixed[kind, j, row : row + 16, CHANNELS * ri : CHANNELS * (ri + 1)])
        turned = dot(order, jnp.concatenate(pieces, axis=0))
        owners = slice(16 * block, 16 * (block + 1))
        out_ref[owners, 0:16, :] = turned.astype(jnp.bfloat16).reshape(16, 16, CHANNELS)
        saves.append(started(out_ref.at[owners], out_hbm.at[owners], out_sems.at[block]))
    for save in saves:
        save.wait()


UNFOLDED = ((2, 512, 2 * CHANNELS), (2, 256, 2 * CHANNELS))


def mix(rank, rows, edge, weights, order, rider=None):
    back = rider is not None
    flops = 2 * 1536 * 768 * 768 + 4 * 2048 * 256 * 384
    blocks = (DEVICES, 24 if back else 16, CHANNELS)
    operands = (rank.reshape(1), rows, edge, order, weights) + ((rider,) if back else ())
    shapes = [((16, CHANNELS), jnp.float32), (blocks, jnp.bfloat16)]
    scratch = [
        pltpu.VMEM((DEVICES, 16, CHANNELS), jnp.bfloat16),
        pltpu.VMEM((2, 2, CHANNELS, 2 * CHANNELS), jnp.bfloat16),
        pltpu.VMEM(blocks, jnp.bfloat16),
        pltpu.VMEM(UNFOLDED[0], jnp.bfloat16),
        pltpu.VMEM(UNFOLDED[1], jnp.bfloat16),
        pltpu.VMEM((2, 2, 256, 2 * CHANNELS), jnp.bfloat16),
        pltpu.SemaphoreType.DMA((8,)),
        pltpu.SemaphoreType.DMA((4, 2)),
        pltpu.SemaphoreType.DMA((8,)),
    ]
    return on_device(
        functools.partial(mix_kernel, back=back),
        shapes,
        operands,
        "mix_back" if back else "mix_modes",
        flops,
        1,
        scratch,
        (1, 4),
        (1,),
    )


def forward_kernel(table_ref, mine_ref, other_ref, out_ref):
    for part in range(4):
        rows = slice(128 * part, 128 * (part + 1))
        lines = []
        for a in range(2):
            sums = dot(table_ref[0, rows, :], mine_ref[a]) + dot(table_ref[1, rows, :], other_ref[a])
            lines.append(sums.reshape(16, 8, CHANNELS))
        out_ref[16 * part : 16 * (part + 1)] = jnp.concatenate(lines, axis=1).astype(jnp.bfloat16)


def fetch_table(core_ref, table_hbm, table_ref, sem):
    return started(table_hbm.at[core_ref[0]], table_ref, sem)


def inverse_rows(table_ref, mine, other, a):
    def pick(waves):
        return waves[:, 8 * a : 8 * (a + 1), :].reshape(512, CHANNELS).astype(jnp.bfloat16)

    sums = dot(table_ref[0], pick(mine)) + dot(table_ref[1], pick(other))
    return sums.astype(jnp.bfloat16).astype(jnp.float32)


def activate_kernel(
    core_ref,
    table_hbm,
    mine_hbm,
    other_ref,
    local_ref,
    cotangent_ref,
    out_ref,
    grad_ref,
    mine_ref,
    mine_sem,
    table_ref,
    sem,
):
    load = started(mine_hbm, mine_ref, mine_sem)
    fetch = fetch_table(core_ref, table_hbm, table_ref, sem)
    load.wait()
    mine = mine_ref[:, 0:16, :].astype(jnp.float32)
    other = other_ref[:, 0:16, :].astype(jnp.float32)
    scale = math.sqrt(2.0 / math.pi)
    fetch.wait()
    for a in range(2):
        v = inverse_rows(table_ref, mine, other, a) + local_ref[a]
        square = v * v
        t = jnp.tanh(scale * (v + 0.044715 * (v * square)))
        half = 0.5 * (1.0 + t)
        out_ref[a] = (v * half).astype(jnp.bfloat16)
        slope = half + 0.5 * v * (1.0 - t * t) * (scale * (1.0 + 3 * 0.044715 * square))
        grad_ref[a] = (cotangent_ref[a].astype(jnp.float32) * slope).astype(jnp.bfloat16)


def finish_kernel(
    core_ref,
    table_hbm,
    mine_ref,
    other_ref,
    local_ref,
    out_ref,
    sums_hbm,
    sums_ref,
    sems,
    table_ref,
    sem,
):
    fetch = fetch_table(core_ref, table_hbm, table_ref, sem)
    mine = mine_ref[...].astype(jnp.float32)
    other = other_ref[...].astype(jnp.float32)
    saves = []
    for half in range(2):
        rows = slice(16 + 8 * half, 24 + 8 * half)
        pair = [mine[:48, rows, :], other[:48, rows, :]]
        for core in range(2):
            kept = jnp.where(core_ref[0] == core, pair[0], pair[1])
            sums_ref[half, :, core] = kept
        saves.append(started(sums_ref.at[half], sums_hbm.at[half], sems.at[half]))
    fetch.wait()
    for a in range(2):
        total = inverse_rows(table_ref, mine[:, :16], other[:, :16], a) + local_ref[a]
        out_ref[a] = total.astype(jnp.bfloat16)
    for save in saves:
        save.wait()


MARGIN = 8
CHUNK = 40


def stencil_kernel(
    weight_ref,
    corner_ref,
    above_ref,
    mine_ref,
    below_ref,
    left_ref,
    right_ref,
    out_ref,
    line,
    shifted,
    sums,
    *,
    sign,
):
    blocks = (above_ref, mine_ref, below_ref)
    for row in range(6):
        line[MARGIN : MARGIN + LON_DEV, :] = blocks[row // 2][row % 2].astype(jnp.float32)
        line[MARGIN - HALO_REACH : MARGIN, :] = left_ref[row]
        line[MARGIN + LON_DEV : MARGIN + LON_DEV + HALO_REACH, :] = right_ref[row]
        for shift in range(5):
            first = MARGIN - HALO_REACH + shift
            shifted[shift, row] = line[first : first + LON_DEV, :]

    def step(index, carry):
        first = pl.multiple_of(index * CHUNK, 8)
        for a in range(2):
            for lane in range(3):
                lanes = slice(128 * lane, 128 * (lane + 1))
                totals = [jnp.zeros((CHUNK, 128), jnp.float32)] * 4
                for n in range(9):
                    row = sign * corner_ref[n, 0] + HALO_REACH + a
                    column = sign * corner_ref[n, 1] + HALO_REACH
                    cells = shifted[column, row, pl.ds(first, CHUNK), lanes]
                    totals = [totals[k] + weight_ref[8 * n + 2 * k + a] * cells for k in range(4)]
                for k in range(4):
                    sums[k, a, pl.ds(first, CHUNK), lanes] = totals[k]
        return carry

    lax.fori_loop(0, LON_DEV // CHUNK, step, 0)
    for k in range(4):
        for a in range(2):
            out_ref[k, a] = sums[k, a].astype(jnp.bfloat16)


def outer_kernel(
    rank_ref, rows_hbm, edge_ref, grad_rows_hbm, grad_edge_ref, order_ref, out_ref, *refs
):
    high_ref, low_ref, high_grad_ref, low_grad_ref, rows_ref, grad_rows_ref, sems = refs
    loads = [
        started(rows_hbm, rows_ref, sems.at[0]),
        started(grad_rows_hbm, grad_rows_ref, sems.at[1]),
    ]
    order = order_ref[...]
    for load in loads:
        load.wait()

    def taken(ref):
        return lambda block: ref[16 * block : 16 * block + 16].reshape(256, CHANNELS)

    unfold(taken(rows_ref), order, edge_ref, rank_ref[0], high_ref, low_ref)
    unfold(taken(grad_rows_ref), order, grad_edge_ref, rank_ref[0], high_grad_ref, low_grad_ref)
    c = CHANNELS
    for kind, (left_ref, right_ref) in enumerate(((low_ref, low_grad_ref), (high_ref, high_grad_ref))):
        for j in range(2):
            right = right_ref[j]
            across = (((0,), (0,)), ((), ()))
            first = lax.dot_general(
                left_ref[j, :, :c], right, across, preferred_element_type=jnp.float32
            )
            second = lax.dot_general(
                left_ref[j, :, c:], right, across, preferred_element_type=jnp.float32
            )
            out_ref[kind, j, 0] = first[:, :c] + second[:, c:]
            out_ref[kind, j, 1] = first[:, c:] - second[:, :c]


def on_device(
    kernel, shapes, operands, name, flops, scalars=0, scratch=(), far_in=(), far_out=()
):
    vmem = pl.BlockSpec(memory_space=pltpu.VMEM)
    smem = pl.BlockSpec(memory_space=pltpu.SMEM)
    far = pl.BlockSpec(memory_space=pltpu.HBM)
    moved = sum(math.prod(v.shape) * v.dtype.itemsize for v in operands)
    moved += sum(math.prod(size) * jnp.dtype(kind).itemsize for size, kind in shapes)
    shapes = [
        pltpu.HBM(*s) if n in far_out else jax.ShapeDtypeStruct(*s) for n, s in enumerate(shapes)
    ]
    operands = [
        pltpu.with_memory_space_constraint(v, pltpu.HBM) if n in far_in else v
        for n, v in enumerate(operands)
    ]
    ins = [smem if n < scalars else far if n in far_in else vmem for n in range(len(operands))]
    return pl.pallas_call(
        kernel,
        out_shape=tuple(shapes),
        in_specs=ins,
        out_specs=tuple(far if n in far_out else vmem for n in range(len(shapes))),
        scratch_shapes=list(scratch),
        compiler_params=pltpu.CompilerParams(vmem_limit_bytes=48 * 1024 * 1024),
        cost_estimate=pl.CostEstimate(flops=flops, bytes_accessed=moved, transcendentals=0),
        name=name,
    )(*operands)


def started(source, target, sem):
    copy = pltpu.make_async_copy(source, target, sem)
    copy.start()
    return copy


BLOCK = (2, LON_DEV, CHANNELS)
WAVE_FLOPS = 2 * 512 * 720 * 768


def swap_cores(values):
    return lax.ppermute(values, "core", SWAP)


def edges_kernel(above_ref, block_ref, below_ref, tail_ref, head_ref):
    for n, ref in enumerate((above_ref, block_ref, below_ref)):
        for a in range(2):
            cells = ref[a].astype(jnp.float32)
            tail_ref[2 * n + a] = cells[LON_DEV - HALO_REACH :]
            head_ref[2 * n + a] = cells[:HALO_REACH]


def to_wave_blocks(mine, other, table):
    shapes = [((64, 16, CHANNELS), jnp.bfloat16)]
    return on_device(forward_kernel, shapes, (table, mine, other), "to_waves", WAVE_FLOPS)[0]


def between_chips(blocks):
    return lax.all_to_all(blocks, CHIPS, split_axis=0, concat_axis=0, tiled=True)


def between_degrees(blocks):
    return lax.all_to_all(blocks, ALL, split_axis=0, concat_axis=0, tiled=True)


def coefficient_blocks(spectra, matrices):
    matrix, flipped = matrices
    operands = (matrix, spectra.reshape(32, 2, 16, CHANNELS))
    blocks = (DEVICES, 16, CHANNELS)
    shapes = [(blocks, jnp.bfloat16), ((16, CHANNELS), jnp.float32)]
    scratch = [
        pltpu.VMEM((2064, 512), jnp.bfloat16),
        pltpu.VMEM(blocks, jnp.bfloat16),
        pltpu.SemaphoreType.DMA((9,)),
        pltpu.SemaphoreType.DMA((8,)),
    ]
    flops = 2 * 2048 * 512 * 512
    return on_device(
        to_coefficients_kernel, shapes, operands, "to_coefficients", flops, 0, scratch, (0,), (0,)
    )


def wave_blocks(rows, corner, matrices, rider):
    matrix, flipped = matrices
    blocks = (32, 2, 32 if rider else 16, CHANNELS)
    scratch = [
        pltpu.VMEM((512, 2176), jnp.bfloat16),
        pltpu.VMEM(blocks, jnp.bfloat16),
        pltpu.SemaphoreType.DMA((4,)),
        pltpu.SemaphoreType.DMA((4,)),
    ]
    (out,) = on_device(
        functools.partial(from_modes_kernel, rider=rider),
        [(blocks, jnp.bfloat16)],
        (flipped, rows, corner),
        "from_modes",
        2 * 2048 * 512 * 512,
        0,
        scratch,
        (0,),
        (0,),
    )
    return out.reshape(64, -1, CHANNELS)


def row_halo(block):
    above = lax.ppermute(block, "lat", [(i, i + 1) for i in range(31)])
    below = lax.ppermute(block, "lat", [(i + 1, i) for i in range(31)])
    return above, below


def column_halo(above, block, below):
    shapes = [((6, HALO_REACH, CHANNELS), jnp.float32)] * 2
    tails, heads = on_device(edges_kernel, shapes, (above, block, below), "edges", 0)
    lon = ("zhi", "core")
    left = lax.ppermute(tails, lon, [(i, (i + 1) % 4) for i in range(4)])
    right = lax.ppermute(heads, lon, [((i + 1) % 4, i) for i in range(4)])
    return left, right


def stencil(above, block, below, left, right, disco_kernel, offsets, lat_first, sign):
    row = lat_first + jnp.arange(2, dtype=jnp.int32)[None, :]
    row = row - offsets[:, :1] if sign < 0 else row + jnp.zeros_like(offsets[:, :1])
    chosen = row[:, :, None] == jnp.arange(64, dtype=jnp.int32)[None, None, :]
    weights = jnp.sum(
        jnp.where(chosen[:, None], disco_kernel[:, :, None, :], 0.0), axis=-1
    ).reshape(-1)
    operands = (weights, offsets, above, block, below, left, right)
    scratch = [
        pltpu.VMEM((LON_DEV + 2 * MARGIN, CHANNELS), jnp.float32),
        pltpu.VMEM((5, 6, LON_DEV, CHANNELS), jnp.float32),
        pltpu.VMEM((4, *BLOCK), jnp.float32),
    ]
    shapes = [((4, *BLOCK), jnp.bfloat16)]
    name = "stencil" if sign > 0 else "stencil_back"
    flops = 2 * 36 * math.prod(BLOCK) * 16
    kernel = functools.partial(stencil_kernel, sign=sign)
    return on_device(kernel, shapes, operands, name, flops, 2, scratch)[0]


def local(
    grid_field,
    cotangent,
    analysis_table,
    synthesis_table,
    spectral_weight,
    disco_weight,
    disco_kernel,
    neighbour_offsets,
    *,
    forward_all,
    backward_all,
    spread,
    order,
):
    lat, zhi, core = (lax.axis_index(name) for name in ALL)
    rank = lat * 4 + zhi * 2 + core
    lat_first = lat * 2
    forward_table = lax.dynamic_index_in_dim(jnp.asarray(forward_all), core, 0, keepdims=False)
    order = jnp.asarray(order)
    block_shapes = [(BLOCK, jnp.bfloat16)]

    table_scratch = [
        pltpu.VMEM((2, LON_DEV, 512), jnp.bfloat16),
        pltpu.SemaphoreType.DMA(()),
    ]
    backward_tables = jnp.asarray(backward_all)

    grid_other = swap_cores(grid_field)
    above, below = row_halo(grid_field)
    blocks = to_wave_blocks(grid_field, grid_other, forward_table)
    blocks, analysis_table = tie(blocks, analysis_table)
    spectra = between_chips(blocks)
    analysis_parts = legendre_matrices(analysis_table, rank, spread)
    spectra, synthesis_table, above, *analysis_parts = tie(
        spectra, synthesis_table, above, *analysis_parts
    )
    rows, modes_corner = coefficient_blocks(spectra, analysis_parts)
    modes = between_degrees(rows)
    synthesis_parts = legendre_matrices(synthesis_table, rank, spread)
    modes, below, *synthesis_parts = tie(modes, below, *synthesis_parts)
    corner, mixed = mix(rank, modes, modes_corner, spectral_weight, order)
    mixed, above, below = tie(mixed, above, below)
    mixed = between_degrees(mixed)
    left, right = column_halo(above, grid_field, below)
    mixed, left, right = tie(mixed, left, right)
    wave_rows = wave_blocks(mixed, corner, synthesis_parts, False)
    wave_rows, left, right, above, below = tie(wave_rows, left, right, above, below)
    waves = between_chips(wave_rows)
    inputs = stencil(
        above, grid_field, below, left, right, disco_kernel, neighbour_offsets, lat_first, 1
    )
    local_part = jnp.einsum(
        "kabc,kcd->abd", inputs, disco_weight, preferred_element_type=jnp.float32
    )
    waves, local_part, inputs = tie(waves, local_part, inputs)
    block_output, hidden_grad = on_device(
        activate_kernel,
        block_shapes * 2,
        (core.reshape(1), backward_tables, waves, swap_cores(waves), local_part, cotangent),
        "activate",
        WAVE_FLOPS,
        1,
        [
            pltpu.VMEM((64, 16, CHANNELS), jnp.bfloat16),
            pltpu.SemaphoreType.DMA(()),
            *table_scratch,
        ],
        (1, 2),
    )

    blocks = to_wave_blocks(hidden_grad, swap_cores(hidden_grad), forward_table)
    above, below = row_halo(hidden_grad)
    grad_spectra = between_chips(blocks)
    grad_spectra, above, inputs = tie(grad_spectra, above, inputs)
    grad_rows, grad_corner = coefficient_blocks(grad_spectra, synthesis_parts)
    grad_rows, inputs = tie(grad_rows, inputs)
    grads = between_degrees(grad_rows)
    local_grad = jnp.einsum(
        "kabc,abd->kcd", inputs, hidden_grad, preferred_element_type=jnp.float32
    ) * (1.0 / math.sqrt(64 * LON_CELLS))
    halves = local_grad.reshape(2, 2 * CHANNELS, CHANNELS)
    kept = lax.dynamic_index_in_dim(halves, core, 0, keepdims=False)
    given = lax.dynamic_index_in_dim(halves, 1 - core, 0, keepdims=False)
    rider = (kept + swap_cores(given)).astype(jnp.bfloat16).reshape(96, 8, CHANNELS)
    grads, below, rider = tie(grads, below, rider)
    corner, back = mix(rank, grads, grad_corner, spectral_weight, order, rider)
    back, above, below = tie(back, above, below)
    back = between_degrees(back)
    left, right = column_halo(above, hidden_grad, below)
    back, left, right = tie(back, left, right)
    wave_rows = wave_blocks(back, corner, analysis_parts, True)
    wave_rows, left, right, above, below, grads = tie(
        wave_rows, left, right, above, below, grads
    )
    waves_back = between_chips(wave_rows)
    back_inputs = stencil(
        above, hidden_grad, below, left, right, disco_kernel, neighbour_offsets, lat_first, -1
    )
    local_back = jnp.einsum(
        "kabd,kcd->abc", back_inputs, disco_weight, preferred_element_type=jnp.float32
    )
    (spectral_grad,) = on_device(
        outer_kernel,
        [((2, 2, 2, CHANNELS, CHANNELS), jnp.float32)],
        (rank.reshape(1), modes, modes_corner, grads, grad_corner, order),
        "outer",
        2 * 1536 * 768 * 768,
        1,
        [
            *(pltpu.VMEM(size, jnp.bfloat16) for size in UNFOLDED * 2),
            *[pltpu.VMEM((DEVICES, 16, CHANNELS), jnp.bfloat16)] * 2,
            pltpu.SemaphoreType.DMA((2,)),
        ],
        (1, 3),
    )
    waves_back, local_back, spectral_grad = tie(waves_back, local_back, spectral_grad)
    sums = (2, 48, 2, 8, CHANNELS)
    field_grad, disco_grad = on_device(
        finish_kernel,
        [(BLOCK, jnp.bfloat16), (sums, jnp.float32)],
        (core.reshape(1), backward_tables, waves_back, swap_cores(waves_back), local_back),
        "finish",
        WAVE_FLOPS,
        1,
        [pltpu.VMEM(sums, jnp.float32), pltpu.SemaphoreType.DMA((2,)), *table_scratch],
        (1,),
        (1,),
    )
    return (
        block_output,
        field_grad,
        spectral_grad,
        disco_grad.reshape(4, CHANNELS, CHANNELS),
    )


def solution(mesh):
    forward_all, backward_all = wave_tables()
    place = np.arange(256)
    order = (place[:, None] == (place % 16 * 16 + place // 16)[None, :]).astype(ml_dtypes.bfloat16)
    split = Mesh(mesh.devices.reshape(32, 2, 2), ALL)
    lon = ("zhi", "core")
    return jax.shard_map(
        functools.partial(
            local,
            forward_all=forward_all,
            backward_all=backward_all,
            spread=spread_matrix(),
            order=order,
        ),
        mesh=split,
        in_specs=(
            P("lat", lon, None),
            P("lat", lon, None),
            P(None, ALL, None, None),
            P(None, ALL, None, None),
            P(None, ALL, None, None, None),
            P(),
            P(),
            P(),
        ),
        out_specs=(
            P("lat", lon, None),
            P("lat", lon, None),
            P(None, ALL, None, None, None),
            P(),
        ),
        check_vma=False,
    )
```

```python
import functools
import math

import jax
import jax.numpy as jnp
import ml_dtypes
import numpy as np
from jax import lax
from jax.experimental import pallas as pl
from jax.experimental.pallas import tpu as pltpu
from jax.sharding import Mesh
from jax.sharding import PartitionSpec as P

HALO_REACH = 2
LON_CELLS = 1440
LON_DEV = 360
CHANNELS = 384
DEGREES = 512
HALF = 256
DEVICES = 128
ALL = ("lat", "zhi", "core")
CHIPS = ("lat", "zhi")
SWAP = [(0, 1), (1, 0)]


def wave_tables():
    e, lh, p, ri = np.meshgrid(*map(np.arange, (64, 2, 2, 2)), indexing="ij")
    e, lh, p, ri = (v.reshape(-1) for v in (e, lh, p, ri))
    forward = np.zeros((2, 2, 512, LON_DEV), np.float32)
    backward = np.zeros((2, 2, LON_DEV, 512), np.float32)

    def basis(wave_core, cell_core):
        base = 4 * e + 2 * wave_core + p
        wave = np.where(lh == 0, base, DEGREES - 1 - base)
        column = np.arange(LON_DEV) + LON_DEV * cell_core
        angle = (wave[:, None] * column[None, :] % LON_CELLS) * (2.0 * math.pi / LON_CELLS)
        return np.where(ri[:, None] == 0, np.cos(angle), -np.sin(angle)) / math.sqrt(LON_CELLS)

    for core in range(2):
        for other in range(2):
            forward[core, other] = basis(core, core ^ other)
            backward[core, other] = basis(core ^ other, core).T
    return forward.astype(ml_dtypes.bfloat16), backward.astype(ml_dtypes.bfloat16)


def spread_matrix():
    row, lh, cp, cri = (
        v.reshape(-1) for v in np.meshgrid(*map(np.arange, (64, 2, 2, 2)), indexing="ij")
    )
    slh, sp, sa = (v.reshape(-1) for v in np.meshgrid(*map(np.arange, (2, 2, 64)), indexing="ij"))
    spread = (
        (slh[:, None] == lh[None, :]) & (sp[:, None] == cp[None, :]) & (sa[:, None] == row[None, :])
    )
    return spread.astype(np.float32).astype(ml_dtypes.bfloat16)


def tie(*values):
    return lax.optimization_barrier(values)


def dot(left, right):
    return jnp.dot(left, right, preferred_element_type=jnp.float32)


def dot_nt(left, right):
    return lax.dot_general(
        left, right, (((1,), (1,)), ((), ())), preferred_element_type=jnp.float32
    )


def one_hot(wanted, shape):
    degree = lax.broadcasted_iota(jnp.int32, shape, 1)
    return jnp.where(degree == wanted, 1.0, 0.0).astype(jnp.bfloat16)


def keep(rows, cols, values):
    return jnp.where(rows == cols, values, 0.0).astype(jnp.bfloat16)


def legendre_kernel(
    rank_ref,
    table_ref,
    spread_ref,
    turned_ref,
    matrix_hbm,
    flipped_hbm,
    matrix_ref,
    flipped_ref,
    sems,
):
    rank = rank_ref[0]
    saves = []
    lower = table_ref[0].reshape(128, DEGREES)
    upper = table_ref[1].reshape(128, DEGREES)
    spread = spread_ref[...]
    turned = turned_ref[...]

    def attributes(place):
        p, kind = (place >> 2) & 1, (place >> 3) & 1
        fold = 2 * (place >> 4) + (place & 1)
        high = jnp.where(2 * rank + p > fold, kind, 0)
        return kind, fold, ((place >> 1) & 3) + 4 * high

    for block in range(8):
        rows = slice(256 * block, 256 * (block + 1))
        place = lax.broadcasted_iota(jnp.int32, (256, 1), 0) + 256 * block
        kind, fold, code = attributes(place)
        last = DEGREES - 1 - fold
        low = one_hot(jnp.where(kind == 0, last, fold), (256, DEGREES))
        high = one_hot(jnp.where(kind == 0, -1, last), (256, DEGREES))
        picked = jnp.concatenate([dot_nt(low, lower), dot_nt(high, upper)], axis=1)
        picked = picked.astype(jnp.bfloat16)
        column = lax.broadcasted_iota(jnp.int32, (1, 512), 1) & 7
        matrix_ref[rows, :] = keep(code, column, dot(picked, spread))
        _, _, across = attributes(lax.broadcasted_iota(jnp.int32, (1, 256), 1) + 256 * block)
        down = lax.broadcasted_iota(jnp.int32, (512, 1), 0) & 7
        flipped_ref[:, rows] = keep(down, across, dot_nt(turned, picked))
        saves.append(started(matrix_ref.at[rows], matrix_hbm.at[rows], sems.at[0, block]))
        saves.append(started(flipped_ref.at[:, rows], flipped_hbm.at[:, rows], sems.at[1, block]))
    place = lax.broadcasted_iota(jnp.int32, (128, 1), 0)
    wanted = jnp.where(place < 4, DEGREES - 1 - (2 * rank + (place >> 1)), -1)
    edge = dot_nt(one_hot(wanted, (128, DEGREES)), upper).astype(jnp.bfloat16)
    column = lax.broadcasted_iota(jnp.int32, (1, 512), 1) & 7
    matrix_ref[2048:2064, :] = keep(place[:16] + 4, column, dot(edge[:16], spread[128:]))
    across = lax.broadcasted_iota(jnp.int32, (1, 128), 1) + 4
    down = lax.broadcasted_iota(jnp.int32, (512, 1), 0) & 7
    flipped_ref[:, 2048:2176] = keep(down, across, dot_nt(turned[:, 128:], edge))
    rows = slice(2048, 2064)
    saves.append(started(matrix_ref.at[rows], matrix_hbm.at[rows], sems.at[0, 8]))
    rows = slice(2048, 2176)
    saves.append(started(flipped_ref.at[:, rows], flipped_hbm.at[:, rows], sems.at[1, 8]))
    for save in saves:
        save.wait()


def chip_signs():
    line = lax.broadcasted_iota(jnp.int32, (1, 16, CHANNELS), 1)
    odd = ((line >> 2) ^ (line >> 1)) & 1
    return jnp.where(odd == 1, -1.0, 1.0)


def to_coefficients_kernel(
    matrix_hbm,
    spectra_hbm,
    out_hbm,
    corner_ref,
    matrix_ref,
    out_ref,
    in_sems,
    out_sems,
    spectra_ref,
    spectra_sem,
):
    arrival = started(spectra_hbm, spectra_ref, spectra_sem)
    parts = [slice(256 * block, 256 * (block + 1)) for block in range(8)] + [slice(2048, 2064)]
    loads = [
        started(matrix_hbm.at[rows], matrix_ref.at[rows], in_sems.at[n])
        for n, rows in enumerate(parts)
    ]
    saves = []
    arrival.wait()
    both = spectra_ref[...].astype(jnp.float32)
    spectra = (both[:, 0] + chip_signs() * both[:, 1]).reshape(512, CHANNELS).astype(jnp.bfloat16)
    for block, rows in enumerate(parts[:8]):
        loads[block].wait()
        sums = dot(matrix_ref[rows, :], spectra)
        places = slice(16 * block, 16 * (block + 1))
        out_ref[places] = sums.astype(jnp.bfloat16).reshape(16, 16, CHANNELS)
        saves.append(started(out_ref.at[places], out_hbm.at[places], out_sems.at[block]))
    loads[8].wait()
    corner = dot(matrix_ref[parts[8], :], spectra).astype(jnp.bfloat16)
    corner_ref[...] = corner.astype(jnp.float32)
    for save in saves:
        save.wait()


def from_modes_kernel(
    flipped_hbm,
    rows_ref,
    corner_ref,
    out_hbm,
    flipped_ref,
    out_ref,
    in_sems,
    out_sems,
    *,
    rider,
):
    parts = [slice(128 * block, 128 * (block + 1)) for block in range(4)]
    loads = [
        started(flipped_hbm.at[lines], flipped_ref.at[lines], in_sems.at[n])
        for n, lines in enumerate(parts)
    ]
    saves = []
    rows = rows_ref[:, 0:16, :].reshape(2048, CHANNELS)
    corner = corner_ref[...].astype(jnp.bfloat16)
    if rider:
        shares = rows_ref[...].astype(jnp.float32).reshape(64, 2, 24, CHANNELS)[:, :, 16:24, :]
        owned = jnp.sum(shares, axis=0).reshape(16, CHANNELS).astype(jnp.bfloat16)
        out_ref[:, :, 16:32, :] = jnp.broadcast_to(owned[None, None], (32, 2, 16, CHANNELS))
    for block, lines in enumerate(parts):
        loads[block].wait()
        waves = dot(flipped_ref[lines, 0:2048], rows) + dot(flipped_ref[lines, 2048:2064], corner)
        waves = waves.reshape(8, 16, CHANNELS)
        places = slice(8 * block, 8 * (block + 1))
        out_ref[places, 0, 0:16, :] = waves.astype(jnp.bfloat16)
        out_ref[places, 1, 0:16, :] = (waves * chip_signs()).astype(jnp.bfloat16)
        saves.append(started(out_ref.at[places], out_hbm.at[places], out_sems.at[block]))
    for save in saves:
        save.wait()


def legendre_matrices(table, rank, spread):
    shapes = [((2064, 512), jnp.bfloat16), ((512, 2176), jnp.bfloat16)]
    operands = (rank.reshape(1), table, jnp.asarray(spread), jnp.asarray(spread.T))
    scratch = [
        pltpu.VMEM((2064, 512), jnp.bfloat16),
        pltpu.VMEM((512, 2176), jnp.bfloat16),
        pltpu.SemaphoreType.DMA((2, 9)),
    ]
    return on_device(
        legendre_kernel, shapes, operands, "legendre", 4_000_000_000, 1, scratch, (), (0, 1)
    )


def complex_weights(weight):
    real, imag = weight[:, :, 0], weight[:, :, 1]
    return jnp.concatenate(
        [jnp.concatenate([real, imag], axis=3), jnp.concatenate([-imag, real], axis=3)], axis=2
    )


def mix_kernel(
    rank_ref,
    rows_hbm,
    edge_ref,
    order_ref,
    weight_hbm,
    *refs,
    back,
):
    rider_ref, refs = (refs[0], refs[1:]) if back else (None, refs)
    (
        edge_out_ref,
        out_hbm,
        high_hbm,
        low_hbm,
        rows_ref,
        weight_ref,
        out_ref,
        high_ref,
        low_ref,
        mixed,
        row_sems,
        weight_sems,
        out_sems,
        saved_sems,
    ) = refs
    arrivals = []
    for block in range(8):
        sources = slice(16 * block, 16 * (block + 1))
        arrivals.append(started(rows_hbm.at[sources], rows_ref.at[sources], row_sems.at[block]))
    places = [(1, 0), (0, 0), (1, 1), (0, 1)]
    loads = [
        started(weight_hbm.at[k, j], weight_ref.at[k, j], weight_sems.at[n])
        for n, (k, j) in enumerate(places)
    ]
    order = order_ref[...]
    for block in range(8):
        arrivals[block].wait()
        rows = rows_ref[16 * block : 16 * block + 16, 0:16, :].reshape(256, CHANNELS)
        turned = dot(order, rows).astype(jnp.bfloat16)
        for q in range(16):
            kind, p, ri, j = q >> 3, (q >> 2) & 1, (q >> 1) & 1, q & 1
            piece = turned[16 * q : 16 * (q + 1), :]
            row = 128 * p + 16 * block
            lanes = slice(CHANNELS * ri, CHANNELS * (ri + 1))
            if kind == 0:
                high_ref[j, row : row + 16, lanes] = piece
            else:
                low_ref[j, row : row + 16, lanes] = piece
    place = lax.broadcasted_iota(jnp.int32, (256, 2 * CHANNELS), 0)
    base = 2 * (place & 127) + (place >> 7)
    product = dot_nt if back else dot
    saves = []
    for j in range(2):
        fold = 2 * rank_ref[0] + j
        both = low_ref[j].astype(jnp.float32)
        edge = jnp.concatenate(
            [edge_ref[2 * j : 2 * j + 1, :], edge_ref[2 * j + 1 : 2 * j + 2, :]], axis=1
        )
        high_ref[j, 256:512, :] = jnp.where(
            base > fold, both, jnp.where(base == fold, edge, 0.0)
        ).astype(jnp.bfloat16)
        low_ref[j] = jnp.where(base <= fold, both, 0.0).astype(jnp.bfloat16)
        saves.append(started(high_ref.at[j], high_hbm.at[j], saved_sems.at[2 * j]))
        saves.append(started(low_ref.at[j], low_hbm.at[j], saved_sems.at[2 * j + 1]))
        loads[2 * j].wait()
        shared = product(high_ref[j], weight_ref[1, j])
        mixed[0, j] = shared[:256].astype(jnp.bfloat16)
        high = shared[256:]
        loads[2 * j + 1].wait()
        low = product(low_ref[j], weight_ref[0, j])
        mixed[1, j] = jnp.where(base <= fold, low, high).astype(jnp.bfloat16)
        corner = jnp.sum(jnp.where(base == fold, high, 0.0), axis=0, keepdims=True)
        edge_out_ref[2 * j : 2 * j + 1, :] = corner[:, :CHANNELS]
        edge_out_ref[2 * j + 1 : 2 * j + 2, :] = corner[:, CHANNELS:]
    edge_out_ref[4:16, :] = jnp.zeros((12, CHANNELS), jnp.float32)
    if rider_ref is not None:
        out_ref[0:96, 16:24, :] = rider_ref[...]
        out_ref[96:128, 16:24, :] = jnp.zeros((32, 8, CHANNELS), jnp.bfloat16)
    for block in range(8):
        pieces = []
        for q in range(16):
            kind, p, ri, j = q >> 3, (q >> 2) & 1, (q >> 1) & 1, q & 1
            row = 128 * p + 16 * block
            pieces.append(mixed[kind, j, row : row + 16, CHANNELS * ri : CHANNELS * (ri + 1)])
        turned = dot(order, jnp.concatenate(pieces, axis=0))
        owners = slice(16 * block, 16 * (block + 1))
        out_ref[owners, 0:16, :] = turned.astype(jnp.bfloat16).reshape(16, 16, CHANNELS)
        saves.append(started(out_ref.at[owners], out_hbm.at[owners], out_sems.at[block]))
    for save in saves:
        save.wait()


def mix(rank, rows, edge, weights, order, rider=None):
    back = rider is not None
    flops = 2 * 1536 * 768 * 768 + 4 * 2048 * 256 * 384
    blocks = (DEVICES, 24 if back else 16, CHANNELS)
    high, low = (2, 512, 2 * CHANNELS), (2, 256, 2 * CHANNELS)
    operands = (rank.reshape(1), rows, edge, order, weights) + ((rider,) if back else ())
    shapes = [
        ((16, CHANNELS), jnp.float32),
        (blocks, jnp.bfloat16),
        (high, jnp.bfloat16),
        (low, jnp.bfloat16),
    ]
    scratch = [
        pltpu.VMEM((DEVICES, 16, CHANNELS), jnp.bfloat16),
        pltpu.VMEM((2, 2, 2 * CHANNELS, 2 * CHANNELS), jnp.bfloat16),
        pltpu.VMEM(blocks, jnp.bfloat16),
        pltpu.VMEM(high, jnp.bfloat16),
        pltpu.VMEM(low, jnp.bfloat16),
        pltpu.VMEM((2, 2, 256, 2 * CHANNELS), jnp.bfloat16),
        pltpu.SemaphoreType.DMA((8,)),
        pltpu.SemaphoreType.DMA((4,)),
        pltpu.SemaphoreType.DMA((8,)),
        pltpu.SemaphoreType.DMA((4,)),
    ]
    return on_device(
        functools.partial(mix_kernel, back=back),
        shapes,
        operands,
        "mix_back" if back else "mix_modes",
        flops,
        1,
        scratch,
        (1, 4),
        (1, 2, 3),
    )


def forward_kernel(table_ref, mine_ref, other_ref, out_ref):
    for part in range(4):
        rows = slice(128 * part, 128 * (part + 1))
        lines = []
        for a in range(2):
            sums = dot(table_ref[0, rows, :], mine_ref[a]) + dot(table_ref[1, rows, :], other_ref[a])
            lines.append(sums.reshape(16, 8, CHANNELS))
        out_ref[16 * part : 16 * (part + 1)] = jnp.concatenate(lines, axis=1).astype(jnp.bfloat16)


def fetch(core_ref, table_hbm, table_ref, local_hbm, local_ref, sems):
    return [
        started(table_hbm.at[core_ref[0]], table_ref, sems.at[0]),
        started(local_hbm, local_ref, sems.at[1]),
    ]


def inverse_rows(table_ref, mine, other, a):
    def pick(waves):
        return waves[:, 8 * a : 8 * (a + 1), :].reshape(512, CHANNELS).astype(jnp.bfloat16)

    sums = dot(table_ref[0], pick(mine)) + dot(table_ref[1], pick(other))
    return sums.astype(jnp.bfloat16).astype(jnp.float32)


def activate_kernel(
    core_ref,
    table_hbm,
    mine_ref,
    other_ref,
    local_hbm,
    cotangent_ref,
    out_ref,
    grad_ref,
    table_ref,
    local_ref,
    fetch_sems,
):
    loads = fetch(core_ref, table_hbm, table_ref, local_hbm, local_ref, fetch_sems)
    mine = mine_ref[:, 0:16, :].astype(jnp.float32)
    other = other_ref[:, 0:16, :].astype(jnp.float32)
    scale = math.sqrt(2.0 / math.pi)
    for load in loads:
        load.wait()
    for a in range(2):
        v = inverse_rows(table_ref, mine, other, a) + local_ref[a]
        square = v * v
        t = jnp.tanh(scale * (v + 0.044715 * (v * square)))
        half = 0.5 * (1.0 + t)
        out_ref[a] = (v * half).astype(jnp.bfloat16)
        slope = half + 0.5 * v * (1.0 - t * t) * (scale * (1.0 + 3 * 0.044715 * square))
        grad_ref[a] = (cotangent_ref[a].astype(jnp.float32) * slope).astype(jnp.bfloat16)


def finish_kernel(
    core_ref,
    table_hbm,
    mine_ref,
    other_ref,
    local_hbm,
    out_ref,
    sums_hbm,
    sums_ref,
    sems,
    table_ref,
    local_ref,
    fetch_sems,
):
    loads = fetch(core_ref, table_hbm, table_ref, local_hbm, local_ref, fetch_sems)
    mine = mine_ref[...].astype(jnp.float32)
    other = other_ref[...].astype(jnp.float32)
    saves = []
    for half in range(2):
        rows = slice(16 + 8 * half, 24 + 8 * half)
        pair = [mine[:48, rows, :], other[:48, rows, :]]
        for core in range(2):
            kept = jnp.where(core_ref[0] == core, pair[0], pair[1])
            sums_ref[half, :, core] = kept
        saves.append(started(sums_ref.at[half], sums_hbm.at[half], sems.at[half]))
    for load in loads:
        load.wait()
    for a in range(2):
        total = inverse_rows(table_ref, mine[:, :16], other[:, :16], a) + local_ref[a]
        out_ref[a] = total.astype(jnp.bfloat16)
    for save in saves:
        save.wait()


MARGIN = 8
CHUNK = 40


def stencil_kernel(
    weight_ref,
    corner_ref,
    above_ref,
    mine_ref,
    below_ref,
    left_ref,
    right_ref,
    out_ref,
    line,
    shifted,
    sums,
    *,
    sign,
):
    blocks = (above_ref, mine_ref, below_ref)
    for row in range(6):
        line[MARGIN : MARGIN + LON_DEV, :] = blocks[row // 2][row % 2].astype(jnp.float32)
        line[MARGIN - HALO_REACH : MARGIN, :] = left_ref[row]
        line[MARGIN + LON_DEV : MARGIN + LON_DEV + HALO_REACH, :] = right_ref[row]
        for shift in range(5):
            first = MARGIN - HALO_REACH + shift
            shifted[shift, row] = line[first : first + LON_DEV, :]

    def step(index, carry):
        first = pl.multiple_of(index * CHUNK, 8)
        for a in range(2):
            for lane in range(3):
                lanes = slice(128 * lane, 128 * (lane + 1))
                totals = [jnp.zeros((CHUNK, 128), jnp.float32)] * 4
                for n in range(9):
                    row = sign * corner_ref[n, 0] + HALO_REACH + a
                    column = sign * corner_ref[n, 1] + HALO_REACH
                    cells = shifted[column, row, pl.ds(first, CHUNK), lanes]
                    totals = [totals[k] + weight_ref[8 * n + 2 * k + a] * cells for k in range(4)]
                for k in range(4):
                    sums[k, a, pl.ds(first, CHUNK), lanes] = totals[k]
        return carry

    lax.fori_loop(0, LON_DEV // CHUNK, step, 0)
    for k in range(4):
        for a in range(2):
            out_ref[k, a] = sums[k, a].astype(jnp.bfloat16)


def outer_kernel(high_ref, high_grad_ref, low_ref, low_grad_ref, out_ref):
    c = CHANNELS
    for kind, (left_ref, right_ref) in enumerate(((low_ref, low_grad_ref), (high_ref, high_grad_ref))):
        for j in range(2):
            right = right_ref[j]
            across = (((0,), (0,)), ((), ()))
            first = lax.dot_general(
                left_ref[j, :, :c], right, across, preferred_element_type=jnp.float32
            )
            second = lax.dot_general(
                left_ref[j, :, c:], right, across, preferred_element_type=jnp.float32
            )
            out_ref[kind, j, 0] = first[:, :c] + second[:, c:]
            out_ref[kind, j, 1] = first[:, c:] - second[:, :c]


def on_device(
    kernel, shapes, operands, name, flops, scalars=0, scratch=(), far_in=(), far_out=()
):
    vmem = pl.BlockSpec(memory_space=pltpu.VMEM)
    smem = pl.BlockSpec(memory_space=pltpu.SMEM)
    far = pl.BlockSpec(memory_space=pltpu.HBM)
    moved = sum(math.prod(v.shape) * v.dtype.itemsize for v in operands)
    moved += sum(math.prod(size) * jnp.dtype(kind).itemsize for size, kind in shapes)
    shapes = [
        pltpu.HBM(*s) if n in far_out else jax.ShapeDtypeStruct(*s) for n, s in enumerate(shapes)
    ]
    operands = [
        pltpu.with_memory_space_constraint(v, pltpu.HBM) if n in far_in else v
        for n, v in enumerate(operands)
    ]
    ins = [smem if n < scalars else far if n in far_in else vmem for n in range(len(operands))]
    return pl.pallas_call(
        kernel,
        out_shape=tuple(shapes),
        in_specs=ins,
        out_specs=tuple(far if n in far_out else vmem for n in range(len(shapes))),
        scratch_shapes=list(scratch),
        compiler_params=pltpu.CompilerParams(vmem_limit_bytes=48 * 1024 * 1024),
        cost_estimate=pl.CostEstimate(flops=flops, bytes_accessed=moved, transcendentals=0),
        name=name,
    )(*operands)


def started(source, target, sem):
    copy = pltpu.make_async_copy(source, target, sem)
    copy.start()
    return copy


BLOCK = (2, LON_DEV, CHANNELS)
WAVE_FLOPS = 2 * 512 * 720 * 768


def swap_cores(values):
    return lax.ppermute(values, "core", SWAP)


def edges_kernel(above_ref, block_ref, below_ref, tail_ref, head_ref):
    for n, ref in enumerate((above_ref, block_ref, below_ref)):
        for a in range(2):
            cells = ref[a].astype(jnp.float32)
            tail_ref[2 * n + a] = cells[LON_DEV - HALO_REACH :]
            head_ref[2 * n + a] = cells[:HALO_REACH]


def to_wave_blocks(mine, other, table):
    shapes = [((64, 16, CHANNELS), jnp.bfloat16)]
    return on_device(forward_kernel, shapes, (table, mine, other), "to_waves", WAVE_FLOPS)[0]


def between_chips(blocks):
    return lax.all_to_all(blocks, CHIPS, split_axis=0, concat_axis=0, tiled=True)


def between_degrees(blocks):
    return lax.all_to_all(blocks, ALL, split_axis=0, concat_axis=0, tiled=True)


def coefficient_blocks(spectra, matrices):
    matrix, flipped = matrices
    operands = (matrix, spectra.reshape(32, 2, 16, CHANNELS))
    blocks = (DEVICES, 16, CHANNELS)
    shapes = [(blocks, jnp.bfloat16), ((16, CHANNELS), jnp.float32)]
    scratch = [
        pltpu.VMEM((2064, 512), jnp.bfloat16),
        pltpu.VMEM(blocks, jnp.bfloat16),
        pltpu.SemaphoreType.DMA((9,)),
        pltpu.SemaphoreType.DMA((8,)),
        pltpu.VMEM((32, 2, 16, CHANNELS), jnp.bfloat16),
        pltpu.SemaphoreType.DMA(()),
    ]
    flops = 2 * 2048 * 512 * 512
    return on_device(
        to_coefficients_kernel, shapes, operands, "to_coefficients", flops, 0, scratch, (0, 1), (0,)
    )


def wave_blocks(rows, corner, matrices, rider):
    matrix, flipped = matrices
    blocks = (32, 2, 32 if rider else 16, CHANNELS)
    scratch = [
        pltpu.VMEM((512, 2176), jnp.bfloat16),
        pltpu.VMEM(blocks, jnp.bfloat16),
        pltpu.SemaphoreType.DMA((4,)),
        pltpu.SemaphoreType.DMA((4,)),
    ]
    (out,) = on_device(
        functools.partial(from_modes_kernel, rider=rider),
        [(blocks, jnp.bfloat16)],
        (flipped, rows, corner),
        "from_modes",
        2 * 2048 * 512 * 512,
        0,
        scratch,
        (0,),
        (0,),
    )
    return out.reshape(64, -1, CHANNELS)


def row_halo(block):
    above = lax.ppermute(block, "lat", [(i, i + 1) for i in range(31)])
    below = lax.ppermute(block, "lat", [(i + 1, i) for i in range(31)])
    return above, below


def column_halo(above, block, below):
    shapes = [((6, HALO_REACH, CHANNELS), jnp.float32)] * 2
    tails, heads = on_device(edges_kernel, shapes, (above, block, below), "edges", 0)
    lon = ("zhi", "core")
    left = lax.ppermute(tails, lon, [(i, (i + 1) % 4) for i in range(4)])
    right = lax.ppermute(heads, lon, [((i + 1) % 4, i) for i in range(4)])
    return left, right


def stencil(above, block, below, left, right, disco_kernel, offsets, lat_first, sign):
    row = lat_first + jnp.arange(2, dtype=jnp.int32)[None, :]
    row = row - offsets[:, :1] if sign < 0 else row + jnp.zeros_like(offsets[:, :1])
    chosen = row[:, :, None] == jnp.arange(64, dtype=jnp.int32)[None, None, :]
    weights = jnp.sum(
        jnp.where(chosen[:, None], disco_kernel[:, :, None, :], 0.0), axis=-1
    ).reshape(-1)
    operands = (weights, offsets, above, block, below, left, right)
    scratch = [
        pltpu.VMEM((LON_DEV + 2 * MARGIN, CHANNELS), jnp.float32),
        pltpu.VMEM((5, 6, LON_DEV, CHANNELS), jnp.float32),
        pltpu.VMEM((4, *BLOCK), jnp.float32),
    ]
    shapes = [((4, *BLOCK), jnp.bfloat16)]
    name = "stencil" if sign > 0 else "stencil_back"
    flops = 2 * 36 * math.prod(BLOCK) * 16
    kernel = functools.partial(stencil_kernel, sign=sign)
    return on_device(kernel, shapes, operands, name, flops, 2, scratch)[0]


def local(
    grid_field,
    cotangent,
    analysis_table,
    synthesis_table,
    spectral_weight,
    disco_weight,
    disco_kernel,
    neighbour_offsets,
    *,
    forward_all,
    backward_all,
    spread,
    order,
):
    lat, zhi, core = (lax.axis_index(name) for name in ALL)
    rank = lat * 4 + zhi * 2 + core
    lat_first = lat * 2
    forward_table = lax.dynamic_index_in_dim(jnp.asarray(forward_all), core, 0, keepdims=False)
    order = jnp.asarray(order)
    block_shapes = [(BLOCK, jnp.bfloat16)]

    grid_other = swap_cores(grid_field)
    above, below = row_halo(grid_field)
    blocks = to_wave_blocks(grid_field, grid_other, forward_table)
    blocks, analysis_table, spectral_weight = tie(blocks, analysis_table, spectral_weight)
    backward_tables = jnp.asarray(backward_all)
    spectra = between_chips(blocks)
    analysis_parts = legendre_matrices(analysis_table, rank, spread)
    weights = complex_weights(spectral_weight)
    spectra, synthesis_table, above, below, *analysis_parts = tie(
        spectra, synthesis_table, above, below, *analysis_parts
    )
    rows, corner = coefficient_blocks(spectra, analysis_parts)
    rows, above, below = tie(rows, above, below)
    rows = between_degrees(rows)
    synthesis_parts = legendre_matrices(synthesis_table, rank, spread)
    left, right = column_halo(above, grid_field, below)
    rows, left, right, weights, *synthesis_parts = tie(rows, left, right, weights, *synthesis_parts)
    corner, mixed, modes_high, modes_low = mix(rank, rows, corner, weights, order)
    mixed, left, right = tie(mixed, left, right)
    mixed = between_degrees(mixed)
    inputs = stencil(
        above, grid_field, below, left, right, disco_kernel, neighbour_offsets, lat_first, 1
    )
    local_part = jnp.einsum(
        "kabc,kcd->abd", inputs, disco_weight, preferred_element_type=jnp.float32
    )
    mixed, local_part, inputs = tie(mixed, local_part, inputs)
    waves = wave_blocks(mixed, corner, synthesis_parts, False)
    waves, cotangent = tie(waves, cotangent)
    waves = between_chips(waves)
    fetched = [
        pltpu.VMEM((2, LON_DEV, 512), jnp.bfloat16),
        pltpu.VMEM(BLOCK, jnp.float32),
        pltpu.SemaphoreType.DMA((2,)),
    ]
    block_output, hidden_grad = on_device(
        activate_kernel,
        block_shapes * 2,
        (core.reshape(1), backward_tables, waves, swap_cores(waves), local_part, cotangent),
        "activate",
        WAVE_FLOPS,
        1,
        fetched,
        (1, 4),
    )

    blocks = to_wave_blocks(hidden_grad, swap_cores(hidden_grad), forward_table)
    blocks, hidden_grad = tie(blocks, hidden_grad)
    above, below = row_halo(hidden_grad)
    grad_spectra = between_chips(blocks)
    grad_rows, corner = coefficient_blocks(grad_spectra, synthesis_parts)
    grad_rows, inputs = tie(grad_rows, inputs)
    grad_rows = between_degrees(grad_rows)
    inputs, above, below = tie(inputs, above, below)
    local_grad = jnp.einsum(
        "kabc,abd->kcd", inputs, hidden_grad, preferred_element_type=jnp.float32
    ) * (1.0 / math.sqrt(64 * LON_CELLS))
    halves = local_grad.reshape(2, 2 * CHANNELS, CHANNELS)
    kept = lax.dynamic_index_in_dim(halves, core, 0, keepdims=False)
    given = lax.dynamic_index_in_dim(halves, 1 - core, 0, keepdims=False)
    rider = (kept + swap_cores(given)).astype(jnp.bfloat16).reshape(96, 8, CHANNELS)
    left, right = column_halo(above, hidden_grad, below)
    grad_rows, left, right, rider = tie(grad_rows, left, right, rider)
    corner, back, grads_high, grads_low = mix(rank, grad_rows, corner, weights, order, rider)
    back, left, right = tie(back, left, right)
    back = between_degrees(back)
    back_inputs = stencil(
        above, hidden_grad, below, left, right, disco_kernel, neighbour_offsets, lat_first, -1
    )
    local_back = jnp.einsum(
        "kabd,kcd->abc", back_inputs, disco_weight, preferred_element_type=jnp.float32
    )
    back, local_back = tie(back, local_back)
    waves_back = wave_blocks(back, corner, analysis_parts, True)
    waves_back, grads_high, grads_low = tie(waves_back, grads_high, grads_low)
    waves_back = between_chips(waves_back)
    (spectral_grad,) = on_device(
        outer_kernel,
        [((2, 2, 2, CHANNELS, CHANNELS), jnp.float32)],
        (modes_high, grads_high, modes_low, grads_low),
        "outer",
        2 * 1536 * 768 * 768,
    )
    waves_back, spectral_grad = tie(waves_back, spectral_grad)
    waves_other = swap_cores(waves_back)
    sums = (2, 48, 2, 8, CHANNELS)
    field_grad, disco_grad = on_device(
        finish_kernel,
        [(BLOCK, jnp.bfloat16), (sums, jnp.float32)],
        (core.reshape(1), backward_tables, waves_back, waves_other, local_back),
        "finish",
        WAVE_FLOPS,
        1,
        [pltpu.VMEM(sums, jnp.float32), pltpu.SemaphoreType.DMA((2,)), *fetched],
        (1, 4),
        (1,),
    )
    return (
        block_output,
        field_grad,
        spectral_grad,
        disco_grad.reshape(4, CHANNELS, CHANNELS),
    )


def solution(mesh):
    forward_all, backward_all = wave_tables()
    place = np.arange(256)
    order = (place[:, None] == (place % 16 * 16 + place // 16)[None, :]).astype(ml_dtypes.bfloat16)
    split = Mesh(mesh.devices.reshape(32, 2, 2), ALL)
    lon = ("zhi", "core")
    return jax.shard_map(
        functools.partial(
            local,
            forward_all=forward_all,
            backward_all=backward_all,
            spread=spread_matrix(),
            order=order,
        ),
        mesh=split,
        in_specs=(
            P("lat", lon, None),
            P("lat", lon, None),
            P(None, ALL, None, None),
            P(None, ALL, None, None),
            P(None, ALL, None, None, None),
            P(),
            P(),
            P(),
        ),
        out_specs=(
            P("lat", lon, None),
            P("lat", lon, None),
            P(None, ALL, None, None, None),
            P(),
        ),
        check_vma=False,
    )
```

```python
import functools
import math

import jax
import jax.numpy as jnp
import ml_dtypes
import numpy as np
from jax import lax
from jax.experimental import pallas as pl
from jax.experimental.pallas import tpu as pltpu
from jax.sharding import Mesh
from jax.sharding import PartitionSpec as P

HALO_REACH = 2
LON_CELLS = 1440
LON_DEV = 360
CHANNELS = 384
DEGREES = 512
HALF = 256
DEVICES = 128
ALL = ("lat", "zhi", "core")
CHIPS = ("lat", "zhi")
SWAP = [(0, 1), (1, 0)]


def wave_tables():
    e, lh, p, ri = np.meshgrid(*map(np.arange, (64, 2, 2, 2)), indexing="ij")
    e, lh, p, ri = (v.reshape(-1) for v in (e, lh, p, ri))
    forward = np.zeros((2, 2, 512, LON_DEV), np.float32)
    backward = np.zeros((2, 2, LON_DEV, 512), np.float32)

    def basis(wave_core, cell_core):
        base = 4 * e + 2 * wave_core + p
        wave = np.where(lh == 0, base, DEGREES - 1 - base)
        column = np.arange(LON_DEV) + LON_DEV * cell_core
        angle = (wave[:, None] * column[None, :] % LON_CELLS) * (2.0 * math.pi / LON_CELLS)
        return np.where(ri[:, None] == 0, np.cos(angle), -np.sin(angle)) / math.sqrt(LON_CELLS)

    for core in range(2):
        for other in range(2):
            forward[core, other] = basis(core, core ^ other)
            backward[core, other] = basis(core ^ other, core).T
    return forward.astype(ml_dtypes.bfloat16), backward.astype(ml_dtypes.bfloat16)


def spread_matrix():
    row, lh, cp, cri = (
        v.reshape(-1) for v in np.meshgrid(*map(np.arange, (64, 2, 2, 2)), indexing="ij")
    )
    slh, sp, sa = (v.reshape(-1) for v in np.meshgrid(*map(np.arange, (2, 2, 64)), indexing="ij"))
    spread = (
        (slh[:, None] == lh[None, :]) & (sp[:, None] == cp[None, :]) & (sa[:, None] == row[None, :])
    )
    return spread.astype(np.float32).astype(ml_dtypes.bfloat16)


def tie(*values):
    return lax.optimization_barrier(values)


def dot(left, right):
    return jnp.dot(left, right, preferred_element_type=jnp.float32)


def dot_nt(left, right):
    return lax.dot_general(
        left, right, (((1,), (1,)), ((), ())), preferred_element_type=jnp.float32
    )


def one_hot(wanted, shape):
    degree = lax.broadcasted_iota(jnp.int32, shape, 1)
    return jnp.where(degree == wanted, 1.0, 0.0).astype(jnp.bfloat16)


def keep(rows, cols, values):
    return jnp.where(rows == cols, values, 0.0).astype(jnp.bfloat16)


def legendre_kernel(
    rank_ref,
    table_ref,
    spread_ref,
    turned_ref,
    matrix_hbm,
    flipped_hbm,
    matrix_ref,
    flipped_ref,
    sems,
):
    rank = rank_ref[0]
    saves = []
    lower = table_ref[0].reshape(128, DEGREES)
    upper = table_ref[1].reshape(128, DEGREES)
    spread = spread_ref[...]
    turned = turned_ref[...]

    def attributes(place):
        p, kind = (place >> 2) & 1, (place >> 3) & 1
        fold = 2 * (place >> 4) + (place & 1)
        high = jnp.where(2 * rank + p > fold, kind, 0)
        return kind, fold, ((place >> 1) & 3) + 4 * high

    for block in range(8):
        rows = slice(256 * block, 256 * (block + 1))
        place = lax.broadcasted_iota(jnp.int32, (256, 1), 0) + 256 * block
        kind, fold, code = attributes(place)
        last = DEGREES - 1 - fold
        low = one_hot(jnp.where(kind == 0, last, fold), (256, DEGREES))
        high = one_hot(jnp.where(kind == 0, -1, last), (256, DEGREES))
        picked = jnp.concatenate([dot_nt(low, lower), dot_nt(high, upper)], axis=1)
        picked = picked.astype(jnp.bfloat16)
        column = lax.broadcasted_iota(jnp.int32, (1, 512), 1) & 7
        matrix_ref[rows, :] = keep(code, column, dot(picked, spread))
        _, _, across = attributes(lax.broadcasted_iota(jnp.int32, (1, 256), 1) + 256 * block)
        down = lax.broadcasted_iota(jnp.int32, (512, 1), 0) & 7
        flipped_ref[:, rows] = keep(down, across, dot_nt(turned, picked))
        saves.append(started(matrix_ref.at[rows], matrix_hbm.at[rows], sems.at[0, block]))
        saves.append(started(flipped_ref.at[:, rows], flipped_hbm.at[:, rows], sems.at[1, block]))
    place = lax.broadcasted_iota(jnp.int32, (128, 1), 0)
    wanted = jnp.where(place < 4, DEGREES - 1 - (2 * rank + (place >> 1)), -1)
    edge = dot_nt(one_hot(wanted, (128, DEGREES)), upper).astype(jnp.bfloat16)
    column = lax.broadcasted_iota(jnp.int32, (1, 512), 1) & 7
    matrix_ref[2048:2064, :] = keep(place[:16] + 4, column, dot(edge[:16], spread[128:]))
    across = lax.broadcasted_iota(jnp.int32, (1, 128), 1) + 4
    down = lax.broadcasted_iota(jnp.int32, (512, 1), 0) & 7
    flipped_ref[:, 2048:2176] = keep(down, across, dot_nt(turned[:, 128:], edge))
    rows = slice(2048, 2064)
    saves.append(started(matrix_ref.at[rows], matrix_hbm.at[rows], sems.at[0, 8]))
    rows = slice(2048, 2176)
    saves.append(started(flipped_ref.at[:, rows], flipped_hbm.at[:, rows], sems.at[1, 8]))
    for save in saves:
        save.wait()


def chip_signs():
    line = lax.broadcasted_iota(jnp.int32, (1, 16, CHANNELS), 1)
    odd = ((line >> 2) ^ (line >> 1)) & 1
    return jnp.where(odd == 1, -1.0, 1.0)


def to_coefficients_kernel(
    matrix_hbm,
    spectra_hbm,
    out_hbm,
    corner_ref,
    matrix_ref,
    out_ref,
    in_sems,
    out_sems,
    spectra_ref,
    spectra_sem,
):
    arrival = started(spectra_hbm, spectra_ref, spectra_sem)
    parts = [slice(256 * block, 256 * (block + 1)) for block in range(8)] + [slice(2048, 2064)]
    loads = [
        started(matrix_hbm.at[rows], matrix_ref.at[rows], in_sems.at[n])
        for n, rows in enumerate(parts)
    ]
    saves = []
    arrival.wait()
    both = spectra_ref[...].astype(jnp.float32)
    spectra = (both[:, 0] + chip_signs() * both[:, 1]).reshape(512, CHANNELS).astype(jnp.bfloat16)
    for block, rows in enumerate(parts[:8]):
        loads[block].wait()
        sums = dot(matrix_ref[rows, :], spectra)
        places = slice(16 * block, 16 * (block + 1))
        out_ref[places] = sums.astype(jnp.bfloat16).reshape(16, 16, CHANNELS)
        saves.append(started(out_ref.at[places], out_hbm.at[places], out_sems.at[block]))
    loads[8].wait()
    corner = dot(matrix_ref[parts[8], :], spectra).astype(jnp.bfloat16)
    corner_ref[...] = corner.astype(jnp.float32)
    for save in saves:
        save.wait()


def from_modes_kernel(
    flipped_hbm,
    rows_ref,
    corner_ref,
    out_hbm,
    flipped_ref,
    out_ref,
    in_sems,
    out_sems,
    *,
    rider,
):
    parts = [slice(128 * block, 128 * (block + 1)) for block in range(4)]
    loads = [
        started(flipped_hbm.at[lines], flipped_ref.at[lines], in_sems.at[n])
        for n, lines in enumerate(parts)
    ]
    saves = []
    rows = rows_ref[:, 0:16, :].reshape(2048, CHANNELS)
    corner = corner_ref[...].astype(jnp.bfloat16)
    if rider:
        shares = rows_ref[...].astype(jnp.float32).reshape(64, 2, 24, CHANNELS)[:, :, 16:24, :]
        owned = jnp.sum(shares, axis=0).reshape(16, CHANNELS).astype(jnp.bfloat16)
        out_ref[:, :, 16:32, :] = jnp.broadcast_to(owned[None, None], (32, 2, 16, CHANNELS))
    for block, lines in enumerate(parts):
        loads[block].wait()
        waves = dot(flipped_ref[lines, 0:2048], rows) + dot(flipped_ref[lines, 2048:2064], corner)
        waves = waves.reshape(8, 16, CHANNELS)
        places = slice(8 * block, 8 * (block + 1))
        out_ref[places, 0, 0:16, :] = waves.astype(jnp.bfloat16)
        out_ref[places, 1, 0:16, :] = (waves * chip_signs()).astype(jnp.bfloat16)
        saves.append(started(out_ref.at[places], out_hbm.at[places], out_sems.at[block]))
    for save in saves:
        save.wait()


def legendre_matrices(table, rank, spread, flops):
    shapes = [((2064, 512), jnp.bfloat16), ((512, 2176), jnp.bfloat16)]
    operands = (rank.reshape(1), table, jnp.asarray(spread), jnp.asarray(spread.T))
    scratch = [
        pltpu.VMEM((2064, 512), jnp.bfloat16),
        pltpu.VMEM((512, 2176), jnp.bfloat16),
        pltpu.SemaphoreType.DMA((2, 9)),
    ]
    return on_device(
        legendre_kernel, shapes, operands, "legendre", flops, 1, scratch, (), (0, 1)
    )


def unfold(rows_of, order, edge_ref, rank, high_ref, low_ref):
    for block in range(8):
        turned = dot(order, rows_of(block)).astype(jnp.bfloat16)
        for q in range(16):
            kind, p, ri, j = q >> 3, (q >> 2) & 1, (q >> 1) & 1, q & 1
            piece = turned[16 * q : 16 * (q + 1), :]
            row = 128 * p + 16 * block
            lanes = slice(CHANNELS * ri, CHANNELS * (ri + 1))
            if kind == 0:
                high_ref[j, row : row + 16, lanes] = piece
            else:
                low_ref[j, row : row + 16, lanes] = piece
    base = wave_places()
    for j in range(2):
        fold = 2 * rank + j
        both = low_ref[j].astype(jnp.float32)
        edge = jnp.concatenate(
            [edge_ref[2 * j : 2 * j + 1, :], edge_ref[2 * j + 1 : 2 * j + 2, :]], axis=1
        )
        high_ref[j, 256:512, :] = jnp.where(
            base > fold, both, jnp.where(base == fold, edge, 0.0)
        ).astype(jnp.bfloat16)
        low_ref[j] = jnp.where(base <= fold, both, 0.0).astype(jnp.bfloat16)


def wave_places():
    place = lax.broadcasted_iota(jnp.int32, (256, 2 * CHANNELS), 0)
    return 2 * (place & 127) + (place >> 7)


def complete(weight_ref, loads):
    c = CHANNELS
    for load in loads:
        load.wait()
    weight_ref[c:, c:] = weight_ref[:c, :c]
    weight_ref[c:, :c] = -weight_ref[:c, c:]


def mix_kernel(rank_ref, rows_hbm, edge_ref, order_ref, weight_hbm, *refs, back):
    rider_ref, refs = (refs[0], refs[1:]) if back else (None, refs)
    edge_out_ref, out_hbm, rows_ref, weight_ref, out_ref, high_ref, low_ref, mixed, *sems = refs
    row_sems, weight_sems, out_sems = sems
    arrivals = []
    for block in range(8):
        sources = slice(16 * block, 16 * (block + 1))
        arrivals.append(started(rows_hbm.at[sources], rows_ref.at[sources], row_sems.at[block]))
    loads = {}
    for n, (kind, j) in enumerate(((1, 0), (0, 0), (1, 1), (0, 1))):
        loads[kind, j] = [
            started(
                weight_hbm.at[kind, j, ri],
                weight_ref.at[kind, j, 0:CHANNELS, CHANNELS * ri : CHANNELS * (ri + 1)],
                weight_sems.at[n, ri],
            )
            for ri in range(2)
        ]
    order = order_ref[...]

    def rows_of(block):
        arrivals[block].wait()
        return rows_ref[16 * block : 16 * block + 16].reshape(256, CHANNELS)

    unfold(rows_of, order, edge_ref, rank_ref[0], high_ref, low_ref)
    base = wave_places()
    product = dot_nt if back else dot
    for j in range(2):
        fold = 2 * rank_ref[0] + j
        complete(weight_ref.at[1, j], loads[1, j])
        shared = product(high_ref[j], weight_ref[1, j])
        mixed[0, j] = shared[:256].astype(jnp.bfloat16)
        high = shared[256:]
        complete(weight_ref.at[0, j], loads[0, j])
        low = product(low_ref[j], weight_ref[0, j])
        mixed[1, j] = jnp.where(base <= fold, low, high).astype(jnp.bfloat16)
        corner = jnp.sum(jnp.where(base == fold, high, 0.0), axis=0, keepdims=True)
        edge_out_ref[2 * j : 2 * j + 1, :] = corner[:, :CHANNELS]
        edge_out_ref[2 * j + 1 : 2 * j + 2, :] = corner[:, CHANNELS:]
    edge_out_ref[4:16, :] = jnp.zeros((12, CHANNELS), jnp.float32)
    if rider_ref is not None:
        out_ref[0:96, 16:24, :] = rider_ref[...]
        out_ref[96:128, 16:24, :] = jnp.zeros((32, 8, CHANNELS), jnp.bfloat16)
    saves = []
    for block in range(8):
        pieces = []
        for q in range(16):
            kind, p, ri, j = q >> 3, (q >> 2) & 1, (q >> 1) & 1, q & 1
            row = 128 * p + 16 * block
            pieces.append(mixed[kind, j, row : row + 16, CHANNELS * ri : CHANNELS * (ri + 1)])
        turned = dot(order, jnp.concatenate(pieces, axis=0))
        owners = slice(16 * block, 16 * (block + 1))
        out_ref[owners, 0:16, :] = turned.astype(jnp.bfloat16).reshape(16, 16, CHANNELS)
        saves.append(started(out_ref.at[owners], out_hbm.at[owners], out_sems.at[block]))
    for save in saves:
        save.wait()


UNFOLDED = ((2, 512, 2 * CHANNELS), (2, 256, 2 * CHANNELS))


def mix(rank, rows, edge, weights, order, rider=None):
    back = rider is not None
    flops = 2 * 1536 * 768 * 768 + 4 * 2048 * 256 * 384
    blocks = (DEVICES, 24 if back else 16, CHANNELS)
    operands = (rank.reshape(1), rows, edge, order, weights) + ((rider,) if back else ())
    shapes = [((16, CHANNELS), jnp.float32), (blocks, jnp.bfloat16)]
    scratch = [
        pltpu.VMEM((DEVICES, 16, CHANNELS), jnp.bfloat16),
        pltpu.VMEM((2, 2, 2 * CHANNELS, 2 * CHANNELS), jnp.bfloat16),
        pltpu.VMEM(blocks, jnp.bfloat16),
        pltpu.VMEM(UNFOLDED[0], jnp.bfloat16),
        pltpu.VMEM(UNFOLDED[1], jnp.bfloat16),
        pltpu.VMEM((2, 2, 256, 2 * CHANNELS), jnp.bfloat16),
        pltpu.SemaphoreType.DMA((8,)),
        pltpu.SemaphoreType.DMA((4, 2)),
        pltpu.SemaphoreType.DMA((8,)),
    ]
    return on_device(
        functools.partial(mix_kernel, back=back),
        shapes,
        operands,
        "mix_back" if back else "mix_modes",
        flops,
        1,
        scratch,
        (1, 4),
        (1,),
    )


def forward_kernel(table_ref, mine_ref, other_ref, out_ref):
    for part in range(4):
        rows = slice(128 * part, 128 * (part + 1))
        lines = []
        for a in range(2):
            sums = dot(table_ref[0, rows, :], mine_ref[a]) + dot(table_ref[1, rows, :], other_ref[a])
            lines.append(sums.reshape(16, 8, CHANNELS))
        out_ref[16 * part : 16 * (part + 1)] = jnp.concatenate(lines, axis=1).astype(jnp.bfloat16)


def fetch(core_ref, table_hbm, table_ref, local_hbm, local_ref, sems):
    return [
        started(table_hbm.at[core_ref[0]], table_ref, sems.at[0]),
        started(local_hbm, local_ref, sems.at[1]),
    ]


def inverse_rows(table_ref, mine, other, a):
    def pick(waves):
        return waves[:, 8 * a : 8 * (a + 1), :].reshape(512, CHANNELS).astype(jnp.bfloat16)

    sums = dot(table_ref[0], pick(mine)) + dot(table_ref[1], pick(other))
    return sums.astype(jnp.bfloat16).astype(jnp.float32)


def activate_kernel(
    core_ref,
    table_hbm,
    mine_ref,
    other_ref,
    local_hbm,
    cotangent_ref,
    out_ref,
    grad_ref,
    table_ref,
    local_ref,
    fetch_sems,
):
    loads = fetch(core_ref, table_hbm, table_ref, local_hbm, local_ref, fetch_sems)
    mine = mine_ref[:, 0:16, :].astype(jnp.float32)
    other = other_ref[:, 0:16, :].astype(jnp.float32)
    scale = math.sqrt(2.0 / math.pi)
    for load in loads:
        load.wait()
    for a in range(2):
        v = inverse_rows(table_ref, mine, other, a) + local_ref[a]
        square = v * v
        t = jnp.tanh(scale * (v + 0.044715 * (v * square)))
        half = 0.5 * (1.0 + t)
        out_ref[a] = (v * half).astype(jnp.bfloat16)
        slope = half + 0.5 * v * (1.0 - t * t) * (scale * (1.0 + 3 * 0.044715 * square))
        grad_ref[a] = (cotangent_ref[a].astype(jnp.float32) * slope).astype(jnp.bfloat16)


def finish_kernel(
    core_ref,
    table_hbm,
    mine_ref,
    other_ref,
    local_hbm,
    out_ref,
    sums_hbm,
    sums_ref,
    sems,
    table_ref,
    local_ref,
    fetch_sems,
):
    loads = fetch(core_ref, table_hbm, table_ref, local_hbm, local_ref, fetch_sems)
    mine = mine_ref[...].astype(jnp.float32)
    other = other_ref[...].astype(jnp.float32)
    saves = []
    for half in range(2):
        rows = slice(16 + 8 * half, 24 + 8 * half)
        pair = [mine[:48, rows, :], other[:48, rows, :]]
        for core in range(2):
            kept = jnp.where(core_ref[0] == core, pair[0], pair[1])
            sums_ref[half, :, core] = kept
        saves.append(started(sums_ref.at[half], sums_hbm.at[half], sems.at[half]))
    for load in loads:
        load.wait()
    for a in range(2):
        total = inverse_rows(table_ref, mine[:, :16], other[:, :16], a) + local_ref[a]
        out_ref[a] = total.astype(jnp.bfloat16)
    for save in saves:
        save.wait()


MARGIN = 8
CHUNK = 40


def stencil_kernel(
    weight_ref,
    corner_ref,
    above_ref,
    mine_ref,
    below_ref,
    left_ref,
    right_ref,
    out_ref,
    line,
    shifted,
    sums,
    *,
    sign,
):
    blocks = (above_ref, mine_ref, below_ref)
    for row in range(6):
        line[MARGIN : MARGIN + LON_DEV, :] = blocks[row // 2][row % 2].astype(jnp.float32)
        line[MARGIN - HALO_REACH : MARGIN, :] = left_ref[row]
        line[MARGIN + LON_DEV : MARGIN + LON_DEV + HALO_REACH, :] = right_ref[row]
        for shift in range(5):
            first = MARGIN - HALO_REACH + shift
            shifted[shift, row] = line[first : first + LON_DEV, :]

    def step(index, carry):
        first = pl.multiple_of(index * CHUNK, 8)
        for a in range(2):
            for lane in range(3):
                lanes = slice(128 * lane, 128 * (lane + 1))
                totals = [jnp.zeros((CHUNK, 128), jnp.float32)] * 4
                for n in range(9):
                    row = sign * corner_ref[n, 0] + HALO_REACH + a
                    column = sign * corner_ref[n, 1] + HALO_REACH
                    cells = shifted[column, row, pl.ds(first, CHUNK), lanes]
                    totals = [totals[k] + weight_ref[8 * n + 2 * k + a] * cells for k in range(4)]
                for k in range(4):
                    sums[k, a, pl.ds(first, CHUNK), lanes] = totals[k]
        return carry

    lax.fori_loop(0, LON_DEV // CHUNK, step, 0)
    for k in range(4):
        for a in range(2):
            out_ref[k, a] = sums[k, a].astype(jnp.bfloat16)


def outer_kernel(
    rank_ref, rows_hbm, edge_ref, grad_rows_hbm, grad_edge_ref, order_ref, out_ref, *refs
):
    high_ref, low_ref, high_grad_ref, low_grad_ref, rows_ref, grad_rows_ref, sems = refs
    loads = [
        started(rows_hbm, rows_ref, sems.at[0]),
        started(grad_rows_hbm, grad_rows_ref, sems.at[1]),
    ]
    order = order_ref[...]
    for load in loads:
        load.wait()

    def taken(ref):
        return lambda block: ref[16 * block : 16 * block + 16].reshape(256, CHANNELS)

    unfold(taken(rows_ref), order, edge_ref, rank_ref[0], high_ref, low_ref)
    unfold(taken(grad_rows_ref), order, grad_edge_ref, rank_ref[0], high_grad_ref, low_grad_ref)
    c = CHANNELS
    for kind, (left_ref, right_ref) in enumerate(((low_ref, low_grad_ref), (high_ref, high_grad_ref))):
        for j in range(2):
            right = right_ref[j]
            across = (((0,), (0,)), ((), ()))
            first = lax.dot_general(
                left_ref[j, :, :c], right, across, preferred_element_type=jnp.float32
            )
            second = lax.dot_general(
                left_ref[j, :, c:], right, across, preferred_element_type=jnp.float32
            )
            out_ref[kind, j, 0] = first[:, :c] + second[:, c:]
            out_ref[kind, j, 1] = first[:, c:] - second[:, :c]


def on_device(
    kernel, shapes, operands, name, flops, scalars=0, scratch=(), far_in=(), far_out=()
):
    vmem = pl.BlockSpec(memory_space=pltpu.VMEM)
    smem = pl.BlockSpec(memory_space=pltpu.SMEM)
    far = pl.BlockSpec(memory_space=pltpu.HBM)
    moved = sum(math.prod(v.shape) * v.dtype.itemsize for v in operands)
    moved += sum(math.prod(size) * jnp.dtype(kind).itemsize for size, kind in shapes)
    shapes = [
        pltpu.HBM(*s) if n in far_out else jax.ShapeDtypeStruct(*s) for n, s in enumerate(shapes)
    ]
    operands = [
        pltpu.with_memory_space_constraint(v, pltpu.HBM) if n in far_in else v
        for n, v in enumerate(operands)
    ]
    ins = [smem if n < scalars else far if n in far_in else vmem for n in range(len(operands))]
    return pl.pallas_call(
        kernel,
        out_shape=tuple(shapes),
        in_specs=ins,
        out_specs=tuple(far if n in far_out else vmem for n in range(len(shapes))),
        scratch_shapes=list(scratch),
        compiler_params=pltpu.CompilerParams(vmem_limit_bytes=48 * 1024 * 1024),
        cost_estimate=pl.CostEstimate(flops=flops, bytes_accessed=moved, transcendentals=0),
        name=name,
    )(*operands)


def started(source, target, sem):
    copy = pltpu.make_async_copy(source, target, sem)
    copy.start()
    return copy


BLOCK = (2, LON_DEV, CHANNELS)
WAVE_FLOPS = 2 * 512 * 720 * 768


def swap_cores(values):
    return lax.ppermute(values, "core", SWAP)


def edges_kernel(above_ref, block_ref, below_ref, tail_ref, head_ref):
    for n, ref in enumerate((above_ref, block_ref, below_ref)):
        for a in range(2):
            cells = ref[a].astype(jnp.float32)
            tail_ref[2 * n + a] = cells[LON_DEV - HALO_REACH :]
            head_ref[2 * n + a] = cells[:HALO_REACH]


def to_wave_blocks(mine, other, table):
    shapes = [((64, 16, CHANNELS), jnp.bfloat16)]
    return on_device(forward_kernel, shapes, (table, mine, other), "to_waves", WAVE_FLOPS)[0]


def between_chips(blocks):
    return lax.all_to_all(blocks, CHIPS, split_axis=0, concat_axis=0, tiled=True)


def between_degrees(blocks):
    return lax.all_to_all(blocks, ALL, split_axis=0, concat_axis=0, tiled=True)


def coefficient_blocks(spectra, matrices):
    matrix, flipped = matrices
    operands = (matrix, spectra.reshape(32, 2, 16, CHANNELS))
    blocks = (DEVICES, 16, CHANNELS)
    shapes = [(blocks, jnp.bfloat16), ((16, CHANNELS), jnp.float32)]
    scratch = [
        pltpu.VMEM((2064, 512), jnp.bfloat16),
        pltpu.VMEM(blocks, jnp.bfloat16),
        pltpu.SemaphoreType.DMA((9,)),
        pltpu.SemaphoreType.DMA((8,)),
        pltpu.VMEM((32, 2, 16, CHANNELS), jnp.bfloat16),
        pltpu.SemaphoreType.DMA(()),
    ]
    flops = 2 * 2048 * 512 * 512
    return on_device(
        to_coefficients_kernel, shapes, operands, "to_coefficients", flops, 0, scratch, (0, 1), (0,)
    )


def wave_blocks(rows, corner, matrices, rider):
    matrix, flipped = matrices
    blocks = (32, 2, 32 if rider else 16, CHANNELS)
    scratch = [
        pltpu.VMEM((512, 2176), jnp.bfloat16),
        pltpu.VMEM(blocks, jnp.bfloat16),
        pltpu.SemaphoreType.DMA((4,)),
        pltpu.SemaphoreType.DMA((4,)),
    ]
    (out,) = on_device(
        functools.partial(from_modes_kernel, rider=rider),
        [(blocks, jnp.bfloat16)],
        (flipped, rows, corner),
        "from_modes",
        2 * 2048 * 512 * 512,
        0,
        scratch,
        (0,),
        (0,),
    )
    return out.reshape(64, -1, CHANNELS)


def row_halo(block):
    above = lax.ppermute(block, "lat", [(i, i + 1) for i in range(31)])
    below = lax.ppermute(block, "lat", [(i + 1, i) for i in range(31)])
    return above, below


def column_halo(above, block, below):
    shapes = [((6, HALO_REACH, CHANNELS), jnp.float32)] * 2
    tails, heads = on_device(edges_kernel, shapes, (above, block, below), "edges", 0)
    lon = ("zhi", "core")
    left = lax.ppermute(tails, lon, [(i, (i + 1) % 4) for i in range(4)])
    right = lax.ppermute(heads, lon, [((i + 1) % 4, i) for i in range(4)])
    return left, right


def stencil(above, block, below, left, right, disco_kernel, offsets, lat_first, sign):
    row = lat_first + jnp.arange(2, dtype=jnp.int32)[None, :]
    row = row - offsets[:, :1] if sign < 0 else row + jnp.zeros_like(offsets[:, :1])
    chosen = row[:, :, None] == jnp.arange(64, dtype=jnp.int32)[None, None, :]
    weights = jnp.sum(
        jnp.where(chosen[:, None], disco_kernel[:, :, None, :], 0.0), axis=-1
    ).reshape(-1)
    operands = (weights, offsets, above, block, below, left, right)
    scratch = [
        pltpu.VMEM((LON_DEV + 2 * MARGIN, CHANNELS), jnp.float32),
        pltpu.VMEM((5, 6, LON_DEV, CHANNELS), jnp.float32),
        pltpu.VMEM((4, *BLOCK), jnp.float32),
    ]
    shapes = [((4, *BLOCK), jnp.bfloat16)]
    name = "stencil" if sign > 0 else "stencil_back"
    flops = 2 * 36 * math.prod(BLOCK) * 16
    kernel = functools.partial(stencil_kernel, sign=sign)
    return on_device(kernel, shapes, operands, name, flops, 2, scratch)[0]


def local(
    grid_field,
    cotangent,
    analysis_table,
    synthesis_table,
    spectral_weight,
    disco_weight,
    disco_kernel,
    neighbour_offsets,
    *,
    forward_all,
    backward_all,
    spread,
    order,
):
    lat, zhi, core = (lax.axis_index(name) for name in ALL)
    rank = lat * 4 + zhi * 2 + core
    lat_first = lat * 2
    forward_table = lax.dynamic_index_in_dim(jnp.asarray(forward_all), core, 0, keepdims=False)
    order = jnp.asarray(order)
    block_shapes = [(BLOCK, jnp.bfloat16)]

    grid_other = swap_cores(grid_field)
    above, below = row_halo(grid_field)
    blocks = to_wave_blocks(grid_field, grid_other, forward_table)
    blocks, analysis_table = tie(blocks, analysis_table)
    backward_tables = jnp.asarray(backward_all)
    spectra = between_chips(blocks)
    analysis_parts = legendre_matrices(analysis_table, rank, spread, 0)
    spectra, synthesis_table, *analysis_parts = tie(spectra, synthesis_table, *analysis_parts)
    synthesis_table, above, below = tie(synthesis_table, above, below)
    rows, modes_corner = coefficient_blocks(spectra, analysis_parts)
    modes = between_degrees(rows)
    synthesis_parts = legendre_matrices(synthesis_table, rank, spread, 16_000_000_000)
    left, right = column_halo(above, grid_field, below)
    modes, left, right, *synthesis_parts = tie(modes, left, right, *synthesis_parts)
    corner, mixed = mix(rank, modes, modes_corner, spectral_weight, order)
    mixed, left, right = tie(mixed, left, right)
    mixed = between_degrees(mixed)
    inputs = stencil(
        above, grid_field, below, left, right, disco_kernel, neighbour_offsets, lat_first, 1
    )
    local_part = jnp.einsum(
        "kabc,kcd->abd", inputs, disco_weight, preferred_element_type=jnp.float32
    )
    mixed, local_part, inputs = tie(mixed, local_part, inputs)
    waves = wave_blocks(mixed, corner, synthesis_parts, False)
    waves, cotangent = tie(waves, cotangent)
    waves = between_chips(waves)
    fetched = [
        pltpu.VMEM((2, LON_DEV, 512), jnp.bfloat16),
        pltpu.VMEM(BLOCK, jnp.float32),
        pltpu.SemaphoreType.DMA((2,)),
    ]
    block_output, hidden_grad = on_device(
        activate_kernel,
        block_shapes * 2,
        (core.reshape(1), backward_tables, waves, swap_cores(waves), local_part, cotangent),
        "activate",
        WAVE_FLOPS,
        1,
        fetched,
        (1, 4),
    )

    blocks = to_wave_blocks(hidden_grad, swap_cores(hidden_grad), forward_table)
    blocks, hidden_grad = tie(blocks, hidden_grad)
    above, below = row_halo(hidden_grad)
    grad_spectra = between_chips(blocks)
    grad_rows, grad_corner = coefficient_blocks(grad_spectra, synthesis_parts)
    grad_rows, inputs = tie(grad_rows, inputs)
    grad_rows = between_degrees(grad_rows)
    inputs, above, below = tie(inputs, above, below)
    local_grad = jnp.einsum(
        "kabc,abd->kcd", inputs, hidden_grad, preferred_element_type=jnp.float32
    ) * (1.0 / math.sqrt(64 * LON_CELLS))
    halves = local_grad.reshape(2, 2 * CHANNELS, CHANNELS)
    kept = lax.dynamic_index_in_dim(halves, core, 0, keepdims=False)
    given = lax.dynamic_index_in_dim(halves, 1 - core, 0, keepdims=False)
    rider = (kept + swap_cores(given)).astype(jnp.bfloat16).reshape(96, 8, CHANNELS)
    left, right = column_halo(above, hidden_grad, below)
    grad_rows, left, right, rider = tie(grad_rows, left, right, rider)
    corner, back = mix(rank, grad_rows, grad_corner, spectral_weight, order, rider)
    back, left, right = tie(back, left, right)
    back = between_degrees(back)
    back_inputs = stencil(
        above, hidden_grad, below, left, right, disco_kernel, neighbour_offsets, lat_first, -1
    )
    local_back = jnp.einsum(
        "kabd,kcd->abc", back_inputs, disco_weight, preferred_element_type=jnp.float32
    )
    back, local_back = tie(back, local_back)
    waves_back = wave_blocks(back, corner, analysis_parts, True)
    waves_back, grad_rows = tie(waves_back, grad_rows)
    waves_back = between_chips(waves_back)
    (spectral_grad,) = on_device(
        outer_kernel,
        [((2, 2, 2, CHANNELS, CHANNELS), jnp.float32)],
        (rank.reshape(1), modes, modes_corner, grad_rows, grad_corner, order),
        "outer",
        2 * 1536 * 768 * 768,
        1,
        [
            *(pltpu.VMEM(size, jnp.bfloat16) for size in UNFOLDED * 2),
            *[pltpu.VMEM((DEVICES, 16, CHANNELS), jnp.bfloat16)] * 2,
            pltpu.SemaphoreType.DMA((2,)),
        ],
        (1, 3),
    )
    waves_back, spectral_grad = tie(waves_back, spectral_grad)
    waves_other = swap_cores(waves_back)
    sums = (2, 48, 2, 8, CHANNELS)
    field_grad, disco_grad = on_device(
        finish_kernel,
        [(BLOCK, jnp.bfloat16), (sums, jnp.float32)],
        (core.reshape(1), backward_tables, waves_back, waves_other, local_back),
        "finish",
        WAVE_FLOPS,
        1,
        [pltpu.VMEM(sums, jnp.float32), pltpu.SemaphoreType.DMA((2,)), *fetched],
        (1, 4),
        (1,),
    )
    return (
        block_output,
        field_grad,
        spectral_grad,
        disco_grad.reshape(4, CHANNELS, CHANNELS),
    )


def solution(mesh):
    forward_all, backward_all = wave_tables()
    place = np.arange(256)
    order = (place[:, None] == (place % 16 * 16 + place // 16)[None, :]).astype(ml_dtypes.bfloat16)
    split = Mesh(mesh.devices.reshape(32, 2, 2), ALL)
    lon = ("zhi", "core")
    return jax.shard_map(
        functools.partial(
            local,
            forward_all=forward_all,
            backward_all=backward_all,
            spread=spread_matrix(),
            order=order,
        ),
        mesh=split,
        in_specs=(
            P("lat", lon, None),
            P("lat", lon, None),
            P(None, ALL, None, None),
            P(None, ALL, None, None),
            P(None, ALL, None, None, None),
            P(),
            P(),
            P(),
        ),
        out_specs=(
            P("lat", lon, None),
            P("lat", lon, None),
            P(None, ALL, None, None, None),
            P(),
        ),
        check_vma=False,
    )
```

```python
import functools
import math

import jax
import jax.numpy as jnp
import ml_dtypes
import numpy as np
from jax import lax
from jax.experimental import pallas as pl
from jax.experimental.pallas import tpu as pltpu
from jax.sharding import Mesh
from jax.sharding import PartitionSpec as P

HALO_REACH = 2
LON_CELLS = 1440
LON_DEV = 360
CHANNELS = 384
DEGREES = 512
HALF = 256
DEVICES = 128
ALL = ("lat", "zhi", "core")
CHIPS = ("lat", "zhi")
SWAP = [(0, 1), (1, 0)]


def wave_tables():
    e, lh, p, ri = np.meshgrid(*map(np.arange, (64, 2, 2, 2)), indexing="ij")
    e, lh, p, ri = (v.reshape(-1) for v in (e, lh, p, ri))
    forward = np.zeros((2, 2, 512, LON_DEV), np.float32)
    backward = np.zeros((2, 2, LON_DEV, 512), np.float32)

    def basis(wave_core, cell_core):
        base = 4 * e + 2 * wave_core + p
        wave = np.where(lh == 0, base, DEGREES - 1 - base)
        column = np.arange(LON_DEV) + LON_DEV * cell_core
        angle = (wave[:, None] * column[None, :] % LON_CELLS) * (2.0 * math.pi / LON_CELLS)
        return np.where(ri[:, None] == 0, np.cos(angle), -np.sin(angle)) / math.sqrt(LON_CELLS)

    for core in range(2):
        for other in range(2):
            forward[core, other] = basis(core, core ^ other)
            backward[core, other] = basis(core ^ other, core).T
    return forward.astype(ml_dtypes.bfloat16), backward.astype(ml_dtypes.bfloat16)


def spread_matrix():
    row, lh, cp, cri = (
        v.reshape(-1) for v in np.meshgrid(*map(np.arange, (64, 2, 2, 2)), indexing="ij")
    )
    slh, sp, sa = (v.reshape(-1) for v in np.meshgrid(*map(np.arange, (2, 2, 64)), indexing="ij"))
    spread = (
        (slh[:, None] == lh[None, :]) & (sp[:, None] == cp[None, :]) & (sa[:, None] == row[None, :])
    )
    return spread.astype(np.float32).astype(ml_dtypes.bfloat16)


def tie(*values):
    return lax.optimization_barrier(values)


def dot(left, right):
    return jnp.dot(left, right, preferred_element_type=jnp.float32)


def dot_nt(left, right):
    return lax.dot_general(
        left, right, (((1,), (1,)), ((), ())), preferred_element_type=jnp.float32
    )


def one_hot(wanted, shape):
    degree = lax.broadcasted_iota(jnp.int32, shape, 1)
    return jnp.where(degree == wanted, 1.0, 0.0).astype(jnp.bfloat16)


def keep(rows, cols, values):
    return jnp.where(rows == cols, values, 0.0).astype(jnp.bfloat16)


def legendre_kernel(
    rank_ref,
    table_ref,
    spread_ref,
    turned_ref,
    matrix_hbm,
    flipped_hbm,
    matrix_ref,
    flipped_ref,
    sems,
):
    rank = rank_ref[0]
    saves = []
    lower = table_ref[0].reshape(128, DEGREES)
    upper = table_ref[1].reshape(128, DEGREES)
    spread = spread_ref[...]
    turned = turned_ref[...]

    def attributes(place):
        p, kind = (place >> 2) & 1, (place >> 3) & 1
        fold = 2 * (place >> 4) + (place & 1)
        high = jnp.where(2 * rank + p > fold, kind, 0)
        return kind, fold, ((place >> 1) & 3) + 4 * high

    for block in range(8):
        rows = slice(256 * block, 256 * (block + 1))
        place = lax.broadcasted_iota(jnp.int32, (256, 1), 0) + 256 * block
        kind, fold, code = attributes(place)
        last = DEGREES - 1 - fold
        low = one_hot(jnp.where(kind == 0, last, fold), (256, DEGREES))
        high = one_hot(jnp.where(kind == 0, -1, last), (256, DEGREES))
        picked = jnp.concatenate([dot_nt(low, lower), dot_nt(high, upper)], axis=1)
        picked = picked.astype(jnp.bfloat16)
        column = lax.broadcasted_iota(jnp.int32, (1, 512), 1) & 7
        matrix_ref[rows, :] = keep(code, column, dot(picked, spread))
        _, _, across = attributes(lax.broadcasted_iota(jnp.int32, (1, 256), 1) + 256 * block)
        down = lax.broadcasted_iota(jnp.int32, (512, 1), 0) & 7
        flipped_ref[:, rows] = keep(down, across, dot_nt(turned, picked))
        saves.append(started(matrix_ref.at[rows], matrix_hbm.at[rows], sems.at[0, block]))
        saves.append(started(flipped_ref.at[:, rows], flipped_hbm.at[:, rows], sems.at[1, block]))
    place = lax.broadcasted_iota(jnp.int32, (128, 1), 0)
    wanted = jnp.where(place < 4, DEGREES - 1 - (2 * rank + (place >> 1)), -1)
    edge = dot_nt(one_hot(wanted, (128, DEGREES)), upper).astype(jnp.bfloat16)
    column = lax.broadcasted_iota(jnp.int32, (1, 512), 1) & 7
    matrix_ref[2048:2064, :] = keep(place[:16] + 4, column, dot(edge[:16], spread[128:]))
    across = lax.broadcasted_iota(jnp.int32, (1, 128), 1) + 4
    down = lax.broadcasted_iota(jnp.int32, (512, 1), 0) & 7
    flipped_ref[:, 2048:2176] = keep(down, across, dot_nt(turned[:, 128:], edge))
    rows = slice(2048, 2064)
    saves.append(started(matrix_ref.at[rows], matrix_hbm.at[rows], sems.at[0, 8]))
    rows = slice(2048, 2176)
    saves.append(started(flipped_ref.at[:, rows], flipped_hbm.at[:, rows], sems.at[1, 8]))
    for save in saves:
        save.wait()


def chip_signs():
    line = lax.broadcasted_iota(jnp.int32, (1, 16, CHANNELS), 1)
    odd = ((line >> 2) ^ (line >> 1)) & 1
    return jnp.where(odd == 1, -1.0, 1.0)


def to_coefficients_kernel(
    matrix_hbm,
    spectra_hbm,
    out_hbm,
    corner_ref,
    matrix_ref,
    out_ref,
    in_sems,
    out_sems,
    spectra_ref,
    spectra_sem,
):
    arrival = started(spectra_hbm, spectra_ref, spectra_sem)
    parts = [slice(512 * block, 512 * (block + 1)) for block in range(3)] + [slice(1536, 2064)]
    loads = [
        started(matrix_hbm.at[rows], matrix_ref.at[rows], in_sems.at[n])
        for n, rows in enumerate(parts)
    ]
    saves = []
    arrival.wait()
    both = spectra_ref[...].astype(jnp.float32)
    spectra = (both[:, 0] + chip_signs() * both[:, 1]).reshape(512, CHANNELS).astype(jnp.bfloat16)
    for block, rows in enumerate(parts):
        loads[block].wait()
        sums = dot(matrix_ref[rows, :], spectra).astype(jnp.bfloat16)
        places = slice(32 * block, 32 * (block + 1))
        out_ref[places] = sums[:512].reshape(32, 16, CHANNELS)
        saves.append(started(out_ref.at[places], out_hbm.at[places], out_sems.at[block]))
    corner = sums[512:]
    corner_ref[...] = corner.astype(jnp.float32)
    for save in saves:
        save.wait()


def from_modes_kernel(
    flipped_hbm,
    rows_ref,
    corner_ref,
    out_hbm,
    flipped_ref,
    out_ref,
    in_sems,
    out_sems,
    *,
    rider,
):
    parts = [slice(256 * block, 256 * (block + 1)) for block in range(2)]
    loads = [
        started(flipped_hbm.at[lines], flipped_ref.at[lines], in_sems.at[n])
        for n, lines in enumerate(parts)
    ]
    saves = []
    rows = rows_ref[:, 0:16, :].reshape(2048, CHANNELS)
    corner = corner_ref[...].astype(jnp.bfloat16)
    if rider:
        shares = rows_ref[...].astype(jnp.float32).reshape(64, 2, 24, CHANNELS)[:, :, 16:24, :]
        owned = jnp.sum(shares, axis=0).reshape(16, CHANNELS).astype(jnp.bfloat16)
        out_ref[:, :, 16:32, :] = jnp.broadcast_to(owned[None, None], (32, 2, 16, CHANNELS))
    for block, lines in enumerate(parts):
        loads[block].wait()
        waves = dot(flipped_ref[lines, 0:2048], rows) + dot(flipped_ref[lines, 2048:2064], corner)
        waves = waves.reshape(16, 16, CHANNELS)
        places = slice(16 * block, 16 * (block + 1))
        out_ref[places, 0, 0:16, :] = waves.astype(jnp.bfloat16)
        out_ref[places, 1, 0:16, :] = (waves * chip_signs()).astype(jnp.bfloat16)
        saves.append(started(out_ref.at[places], out_hbm.at[places], out_sems.at[block]))
    for save in saves:
        save.wait()


def legendre_matrices(table, rank, spread, flops):
    shapes = [((2064, 512), jnp.bfloat16), ((512, 2176), jnp.bfloat16)]
    operands = (rank.reshape(1), table, jnp.asarray(spread), jnp.asarray(spread.T))
    scratch = [
        pltpu.VMEM((2064, 512), jnp.bfloat16),
        pltpu.VMEM((512, 2176), jnp.bfloat16),
        pltpu.SemaphoreType.DMA((2, 9)),
    ]
    return on_device(
        legendre_kernel, shapes, operands, "legendre", flops, 1, scratch, (), (0, 1)
    )


def unfold(rows_of, order, edge_ref, rank, high_ref, low_ref):
    for block in range(8):
        turned = dot(order, rows_of(block)).astype(jnp.bfloat16)
        for q in range(16):
            kind, p, ri, j = q >> 3, (q >> 2) & 1, (q >> 1) & 1, q & 1
            piece = turned[16 * q : 16 * (q + 1), :]
            row = 128 * p + 16 * block
            lanes = slice(CHANNELS * ri, CHANNELS * (ri + 1))
            if kind == 0:
                high_ref[j, row : row + 16, lanes] = piece
            else:
                low_ref[j, row : row + 16, lanes] = piece
    base = wave_places()
    for j in range(2):
        fold = 2 * rank + j
        both = low_ref[j].astype(jnp.float32)
        edge = jnp.concatenate(
            [edge_ref[2 * j : 2 * j + 1, :], edge_ref[2 * j + 1 : 2 * j + 2, :]], axis=1
        )
        high_ref[j, 256:512, :] = jnp.where(
            base > fold, both, jnp.where(base == fold, edge, 0.0)
        ).astype(jnp.bfloat16)
        low_ref[j] = jnp.where(base <= fold, both, 0.0).astype(jnp.bfloat16)


def wave_places():
    place = lax.broadcasted_iota(jnp.int32, (256, 2 * CHANNELS), 0)
    return 2 * (place & 127) + (place >> 7)


def complete(weight_ref, loads):
    c = CHANNELS
    for load in loads:
        load.wait()
    weight_ref[c:, c:] = weight_ref[:c, :c]
    weight_ref[c:, :c] = -weight_ref[:c, c:]


def mix_kernel(rank_ref, rows_hbm, edge_ref, order_ref, weight_hbm, *refs, back):
    rider_ref, refs = (refs[0], refs[1:]) if back else (None, refs)
    edge_out_ref, out_hbm, rows_ref, weight_ref, out_ref, high_ref, low_ref, mixed, *sems = refs
    row_sems, weight_sems, out_sems = sems
    arrivals = []
    for block in range(4):
        sources = slice(32 * block, 32 * (block + 1))
        arrivals.append(started(rows_hbm.at[sources], rows_ref.at[sources], row_sems.at[block]))
    loads = {}
    for n, (kind, j) in enumerate(((1, 0), (0, 0), (1, 1), (0, 1))):
        loads[kind, j] = [
            started(
                weight_hbm.at[kind, j, ri],
                weight_ref.at[kind, j, 0:CHANNELS, CHANNELS * ri : CHANNELS * (ri + 1)],
                weight_sems.at[n, ri],
            )
            for ri in range(2)
        ]
    order = order_ref[...]

    def rows_of(block):
        if block % 2 == 0:
            arrivals[block // 2].wait()
        return rows_ref[16 * block : 16 * block + 16].reshape(256, CHANNELS)

    unfold(rows_of, order, edge_ref, rank_ref[0], high_ref, low_ref)
    base = wave_places()
    product = dot_nt if back else dot
    for j in range(2):
        fold = 2 * rank_ref[0] + j
        complete(weight_ref.at[1, j], loads[1, j])
        shared = product(high_ref[j], weight_ref[1, j])
        mixed[0, j] = shared[:256].astype(jnp.bfloat16)
        high = shared[256:]
        complete(weight_ref.at[0, j], loads[0, j])
        low = product(low_ref[j], weight_ref[0, j])
        mixed[1, j] = jnp.where(base <= fold, low, high).astype(jnp.bfloat16)
        corner = jnp.sum(jnp.where(base == fold, high, 0.0), axis=0, keepdims=True)
        edge_out_ref[2 * j : 2 * j + 1, :] = corner[:, :CHANNELS]
        edge_out_ref[2 * j + 1 : 2 * j + 2, :] = corner[:, CHANNELS:]
    edge_out_ref[4:16, :] = jnp.zeros((12, CHANNELS), jnp.float32)
    if rider_ref is not None:
        out_ref[0:96, 16:24, :] = rider_ref[...]
        out_ref[96:128, 16:24, :] = jnp.zeros((32, 8, CHANNELS), jnp.bfloat16)
    saves = []
    for block in range(8):
        pieces = []
        for q in range(16):
            kind, p, ri, j = q >> 3, (q >> 2) & 1, (q >> 1) & 1, q & 1
            row = 128 * p + 16 * block
            pieces.append(mixed[kind, j, row : row + 16, CHANNELS * ri : CHANNELS * (ri + 1)])
        turned = dot(order, jnp.concatenate(pieces, axis=0))
        owners = slice(16 * block, 16 * (block + 1))
        out_ref[owners, 0:16, :] = turned.astype(jnp.bfloat16).reshape(16, 16, CHANNELS)
        if block % 2 == 1:
            pair = slice(16 * (block - 1), 16 * (block + 1))
            saves.append(started(out_ref.at[pair], out_hbm.at[pair], out_sems.at[block // 2]))
    for save in saves:
        save.wait()


UNFOLDED = ((2, 512, 2 * CHANNELS), (2, 256, 2 * CHANNELS))


def mix(rank, rows, edge, weights, order, rider=None):
    back = rider is not None
    flops = 2 * 1536 * 768 * 768 + 4 * 2048 * 256 * 384
    blocks = (DEVICES, 24 if back else 16, CHANNELS)
    operands = (rank.reshape(1), rows, edge, order, weights) + ((rider,) if back else ())
    shapes = [((16, CHANNELS), jnp.float32), (blocks, jnp.bfloat16)]
    scratch = [
        pltpu.VMEM((DEVICES, 16, CHANNELS), jnp.bfloat16),
        pltpu.VMEM((2, 2, 2 * CHANNELS, 2 * CHANNELS), jnp.bfloat16),
        pltpu.VMEM(blocks, jnp.bfloat16),
        pltpu.VMEM(UNFOLDED[0], jnp.bfloat16),
        pltpu.VMEM(UNFOLDED[1], jnp.bfloat16),
        pltpu.VMEM((2, 2, 256, 2 * CHANNELS), jnp.bfloat16),
        pltpu.SemaphoreType.DMA((4,)),
        pltpu.SemaphoreType.DMA((4, 2)),
        pltpu.SemaphoreType.DMA((4,)),
    ]
    return on_device(
        functools.partial(mix_kernel, back=back),
        shapes,
        operands,
        "mix_back" if back else "mix_modes",
        flops,
        1,
        scratch,
        (1, 4),
        (1,),
    )


def forward_kernel(table_ref, mine_ref, other_ref, out_ref):
    for part in range(4):
        rows = slice(128 * part, 128 * (part + 1))
        lines = []
        for a in range(2):
            sums = dot(table_ref[0, rows, :], mine_ref[a]) + dot(table_ref[1, rows, :], other_ref[a])
            lines.append(sums.reshape(16, 8, CHANNELS))
        out_ref[16 * part : 16 * (part + 1)] = jnp.concatenate(lines, axis=1).astype(jnp.bfloat16)


def fetch(core_ref, table_hbm, table_ref, local_hbm, local_ref, sems):
    return [
        started(table_hbm.at[core_ref[0]], table_ref, sems.at[0]),
        started(local_hbm, local_ref, sems.at[1]),
    ]


def inverse_rows(table_ref, mine, other, a):
    def pick(waves):
        return waves[:, 8 * a : 8 * (a + 1), :].reshape(512, CHANNELS).astype(jnp.bfloat16)

    sums = dot(table_ref[0], pick(mine)) + dot(table_ref[1], pick(other))
    return sums.astype(jnp.bfloat16).astype(jnp.float32)


def activate_kernel(
    core_ref,
    table_hbm,
    mine_ref,
    other_ref,
    local_hbm,
    cotangent_ref,
    out_ref,
    grad_ref,
    table_ref,
    local_ref,
    fetch_sems,
):
    loads = fetch(core_ref, table_hbm, table_ref, local_hbm, local_ref, fetch_sems)
    mine = mine_ref[:, 0:16, :].astype(jnp.float32)
    other = other_ref[:, 0:16, :].astype(jnp.float32)
    scale = math.sqrt(2.0 / math.pi)
    for load in loads:
        load.wait()
    for a in range(2):
        v = inverse_rows(table_ref, mine, other, a) + local_ref[a]
        square = v * v
        t = jnp.tanh(scale * (v + 0.044715 * (v * square)))
        half = 0.5 * (1.0 + t)
        out_ref[a] = (v * half).astype(jnp.bfloat16)
        slope = half + 0.5 * v * (1.0 - t * t) * (scale * (1.0 + 3 * 0.044715 * square))
        grad_ref[a] = (cotangent_ref[a].astype(jnp.float32) * slope).astype(jnp.bfloat16)


def finish_kernel(
    core_ref,
    table_hbm,
    mine_ref,
    other_ref,
    local_hbm,
    out_ref,
    sums_hbm,
    sums_ref,
    sems,
    table_ref,
    local_ref,
    fetch_sems,
):
    loads = fetch(core_ref, table_hbm, table_ref, local_hbm, local_ref, fetch_sems)
    mine = mine_ref[...].astype(jnp.float32)
    other = other_ref[...].astype(jnp.float32)
    saves = []
    for half in range(2):
        rows = slice(16 + 8 * half, 24 + 8 * half)
        pair = [mine[:48, rows, :], other[:48, rows, :]]
        for core in range(2):
            kept = jnp.where(core_ref[0] == core, pair[0], pair[1])
            sums_ref[half, :, core] = kept
        saves.append(started(sums_ref.at[half], sums_hbm.at[half], sems.at[half]))
    for load in loads:
        load.wait()
    for a in range(2):
        total = inverse_rows(table_ref, mine[:, :16], other[:, :16], a) + local_ref[a]
        out_ref[a] = total.astype(jnp.bfloat16)
    for save in saves:
        save.wait()


MARGIN = 8
CHUNK = 40


def stencil_kernel(
    weight_ref,
    corner_ref,
    above_ref,
    mine_ref,
    below_ref,
    left_ref,
    right_ref,
    out_ref,
    line,
    shifted,
    sums,
    *,
    sign,
):
    blocks = (above_ref, mine_ref, below_ref)
    for row in range(6):
        line[MARGIN : MARGIN + LON_DEV, :] = blocks[row // 2][row % 2].astype(jnp.float32)
        line[MARGIN - HALO_REACH : MARGIN, :] = left_ref[row]
        line[MARGIN + LON_DEV : MARGIN + LON_DEV + HALO_REACH, :] = right_ref[row]
        for shift in range(5):
            first = MARGIN - HALO_REACH + shift
            shifted[shift, row] = line[first : first + LON_DEV, :]

    def step(index, carry):
        first = pl.multiple_of(index * CHUNK, 8)
        for a in range(2):
            for lane in range(3):
                lanes = slice(128 * lane, 128 * (lane + 1))
                totals = [jnp.zeros((CHUNK, 128), jnp.float32)] * 4
                for n in range(9):
                    row = sign * corner_ref[n, 0] + HALO_REACH + a
                    column = sign * corner_ref[n, 1] + HALO_REACH
                    cells = shifted[column, row, pl.ds(first, CHUNK), lanes]
                    totals = [totals[k] + weight_ref[8 * n + 2 * k + a] * cells for k in range(4)]
                for k in range(4):
                    sums[k, a, pl.ds(first, CHUNK), lanes] = totals[k]
        return carry

    lax.fori_loop(0, LON_DEV // CHUNK, step, 0)
    for k in range(4):
        for a in range(2):
            out_ref[k, a] = sums[k, a].astype(jnp.bfloat16)


def outer_kernel(
    rank_ref, rows_hbm, edge_ref, grad_rows_hbm, grad_edge_ref, order_ref, out_ref, *refs
):
    high_ref, low_ref, high_grad_ref, low_grad_ref, rows_ref, grad_rows_ref, sems = refs
    loads = [
        started(rows_hbm, rows_ref, sems.at[0]),
        started(grad_rows_hbm, grad_rows_ref, sems.at[1]),
    ]
    order = order_ref[...]
    for load in loads:
        load.wait()

    def taken(ref):
        return lambda block: ref[16 * block : 16 * block + 16].reshape(256, CHANNELS)

    unfold(taken(rows_ref), order, edge_ref, rank_ref[0], high_ref, low_ref)
    unfold(taken(grad_rows_ref), order, grad_edge_ref, rank_ref[0], high_grad_ref, low_grad_ref)
    c = CHANNELS
    for kind, (left_ref, right_ref) in enumerate(((low_ref, low_grad_ref), (high_ref, high_grad_ref))):
        for j in range(2):
            right = right_ref[j]
            across = (((0,), (0,)), ((), ()))
            first = lax.dot_general(
                left_ref[j, :, :c], right, across, preferred_element_type=jnp.float32
            )
            second = lax.dot_general(
                left_ref[j, :, c:], right, across, preferred_element_type=jnp.float32
            )
            out_ref[kind, j, 0] = first[:, :c] + second[:, c:]
            out_ref[kind, j, 1] = first[:, c:] - second[:, :c]


def on_device(
    kernel, shapes, operands, name, flops, scalars=0, scratch=(), far_in=(), far_out=()
):
    vmem = pl.BlockSpec(memory_space=pltpu.VMEM)
    smem = pl.BlockSpec(memory_space=pltpu.SMEM)
    far = pl.BlockSpec(memory_space=pltpu.HBM)
    moved = sum(math.prod(v.shape) * v.dtype.itemsize for v in operands)
    moved += sum(math.prod(size) * jnp.dtype(kind).itemsize for size, kind in shapes)
    shapes = [
        pltpu.HBM(*s) if n in far_out else jax.ShapeDtypeStruct(*s) for n, s in enumerate(shapes)
    ]
    operands = [
        pltpu.with_memory_space_constraint(v, pltpu.HBM) if n in far_in else v
        for n, v in enumerate(operands)
    ]
    ins = [smem if n < scalars else far if n in far_in else vmem for n in range(len(operands))]
    return pl.pallas_call(
        kernel,
        out_shape=tuple(shapes),
        in_specs=ins,
        out_specs=tuple(far if n in far_out else vmem for n in range(len(shapes))),
        scratch_shapes=list(scratch),
        compiler_params=pltpu.CompilerParams(vmem_limit_bytes=48 * 1024 * 1024),
        cost_estimate=pl.CostEstimate(flops=flops, bytes_accessed=moved, transcendentals=0),
        name=name,
    )(*operands)


def started(source, target, sem):
    copy = pltpu.make_async_copy(source, target, sem)
    copy.start()
    return copy


BLOCK = (2, LON_DEV, CHANNELS)
WAVE_FLOPS = 2 * 512 * 720 * 768


def swap_cores(values):
    return lax.ppermute(values, "core", SWAP)


def edges_kernel(above_ref, block_ref, below_ref, tail_ref, head_ref):
    for n, ref in enumerate((above_ref, block_ref, below_ref)):
        for a in range(2):
            cells = ref[a].astype(jnp.float32)
            tail_ref[2 * n + a] = cells[LON_DEV - HALO_REACH :]
            head_ref[2 * n + a] = cells[:HALO_REACH]


def to_wave_blocks(mine, other, table):
    shapes = [((64, 16, CHANNELS), jnp.bfloat16)]
    return on_device(forward_kernel, shapes, (table, mine, other), "to_waves", WAVE_FLOPS)[0]


def between_chips(blocks):
    return lax.all_to_all(blocks, CHIPS, split_axis=0, concat_axis=0, tiled=True)


def between_degrees(blocks):
    return lax.all_to_all(blocks, ALL, split_axis=0, concat_axis=0, tiled=True)


def coefficient_blocks(spectra, matrices):
    matrix, flipped = matrices
    operands = (matrix, spectra.reshape(32, 2, 16, CHANNELS))
    blocks = (DEVICES, 16, CHANNELS)
    shapes = [(blocks, jnp.bfloat16), ((16, CHANNELS), jnp.float32)]
    scratch = [
        pltpu.VMEM((2064, 512), jnp.bfloat16),
        pltpu.VMEM(blocks, jnp.bfloat16),
        pltpu.SemaphoreType.DMA((4,)),
        pltpu.SemaphoreType.DMA((4,)),
        pltpu.VMEM((32, 2, 16, CHANNELS), jnp.bfloat16),
        pltpu.SemaphoreType.DMA(()),
    ]
    flops = 2 * 2048 * 512 * 512
    return on_device(
        to_coefficients_kernel, shapes, operands, "to_coefficients", flops, 0, scratch, (0, 1), (0,)
    )


def wave_blocks(rows, corner, matrices, rider):
    matrix, flipped = matrices
    blocks = (32, 2, 32 if rider else 16, CHANNELS)
    scratch = [
        pltpu.VMEM((512, 2176), jnp.bfloat16),
        pltpu.VMEM(blocks, jnp.bfloat16),
        pltpu.SemaphoreType.DMA((2,)),
        pltpu.SemaphoreType.DMA((2,)),
    ]
    (out,) = on_device(
        functools.partial(from_modes_kernel, rider=rider),
        [(blocks, jnp.bfloat16)],
        (flipped, rows, corner),
        "from_modes",
        2 * 2048 * 512 * 512,
        0,
        scratch,
        (0,),
        (0,),
    )
    return out.reshape(64, -1, CHANNELS)


def row_halo(block):
    above = lax.ppermute(block, "lat", [(i, i + 1) for i in range(31)])
    below = lax.ppermute(block, "lat", [(i + 1, i) for i in range(31)])
    return above, below


def column_halo(above, block, below):
    shapes = [((6, HALO_REACH, CHANNELS), jnp.float32)] * 2
    tails, heads = on_device(edges_kernel, shapes, (above, block, below), "edges", 0)
    lon = ("zhi", "core")
    left = lax.ppermute(tails, lon, [(i, (i + 1) % 4) for i in range(4)])
    right = lax.ppermute(heads, lon, [((i + 1) % 4, i) for i in range(4)])
    return left, right


def stencil(above, block, below, left, right, disco_kernel, offsets, lat_first, sign):
    row = lat_first + jnp.arange(2, dtype=jnp.int32)[None, :]
    row = row - offsets[:, :1] if sign < 0 else row + jnp.zeros_like(offsets[:, :1])
    chosen = row[:, :, None] == jnp.arange(64, dtype=jnp.int32)[None, None, :]
    weights = jnp.sum(
        jnp.where(chosen[:, None], disco_kernel[:, :, None, :], 0.0), axis=-1
    ).reshape(-1)
    operands = (weights, offsets, above, block, below, left, right)
    scratch = [
        pltpu.VMEM((LON_DEV + 2 * MARGIN, CHANNELS), jnp.float32),
        pltpu.VMEM((5, 6, LON_DEV, CHANNELS), jnp.float32),
        pltpu.VMEM((4, *BLOCK), jnp.float32),
    ]
    shapes = [((4, *BLOCK), jnp.bfloat16)]
    name = "stencil" if sign > 0 else "stencil_back"
    flops = 2 * 36 * math.prod(BLOCK) * 16
    kernel = functools.partial(stencil_kernel, sign=sign)
    return on_device(kernel, shapes, operands, name, flops, 2, scratch)[0]


def local(
    grid_field,
    cotangent,
    analysis_table,
    synthesis_table,
    spectral_weight,
    disco_weight,
    disco_kernel,
    neighbour_offsets,
    *,
    forward_all,
    backward_all,
    spread,
    order,
):
    lat, zhi, core = (lax.axis_index(name) for name in ALL)
    rank = lat * 4 + zhi * 2 + core
    lat_first = lat * 2
    forward_table = lax.dynamic_index_in_dim(jnp.asarray(forward_all), core, 0, keepdims=False)
    order = jnp.asarray(order)
    block_shapes = [(BLOCK, jnp.bfloat16)]

    grid_other = swap_cores(grid_field)
    above, below = row_halo(grid_field)
    blocks = to_wave_blocks(grid_field, grid_other, forward_table)
    blocks, analysis_table = tie(blocks, analysis_table)
    backward_tables = jnp.asarray(backward_all)
    spectra = between_chips(blocks)
    analysis_parts = legendre_matrices(analysis_table, rank, spread, 0)
    spectra, synthesis_table, *analysis_parts = tie(spectra, synthesis_table, *analysis_parts)
    synthesis_table, above, below = tie(synthesis_table, above, below)
    rows, modes_corner = coefficient_blocks(spectra, analysis_parts)
    modes = between_degrees(rows)
    synthesis_parts = legendre_matrices(synthesis_table, rank, spread, 16_000_000_000)
    left, right = column_halo(above, grid_field, below)
    modes, left, right, *synthesis_parts = tie(modes, left, right, *synthesis_parts)
    corner, mixed = mix(rank, modes, modes_corner, spectral_weight, order)
    mixed, left, right = tie(mixed, left, right)
    mixed = between_degrees(mixed)
    inputs = stencil(
        above, grid_field, below, left, right, disco_kernel, neighbour_offsets, lat_first, 1
    )
    local_part = jnp.einsum(
        "kabc,kcd->abd", inputs, disco_weight, preferred_element_type=jnp.float32
    )
    mixed, local_part, inputs = tie(mixed, local_part, inputs)
    waves = wave_blocks(mixed, corner, synthesis_parts, False)
    waves, cotangent = tie(waves, cotangent)
    waves = between_chips(waves)
    fetched = [
        pltpu.VMEM((2, LON_DEV, 512), jnp.bfloat16),
        pltpu.VMEM(BLOCK, jnp.float32),
        pltpu.SemaphoreType.DMA((2,)),
    ]
    block_output, hidden_grad = on_device(
        activate_kernel,
        block_shapes * 2,
        (core.reshape(1), backward_tables, waves, swap_cores(waves), local_part, cotangent),
        "activate",
        WAVE_FLOPS,
        1,
        fetched,
        (1, 4),
    )

    blocks = to_wave_blocks(hidden_grad, swap_cores(hidden_grad), forward_table)
    blocks, hidden_grad = tie(blocks, hidden_grad)
    above, below = row_halo(hidden_grad)
    grad_spectra = between_chips(blocks)
    grad_rows, grad_corner = coefficient_blocks(grad_spectra, synthesis_parts)
    grad_rows, inputs = tie(grad_rows, inputs)
    grad_rows = between_degrees(grad_rows)
    inputs, above, below = tie(inputs, above, below)
    local_grad = jnp.einsum(
        "kabc,abd->kcd", inputs, hidden_grad, preferred_element_type=jnp.float32
    ) * (1.0 / math.sqrt(64 * LON_CELLS))
    halves = local_grad.reshape(2, 2 * CHANNELS, CHANNELS)
    kept = lax.dynamic_index_in_dim(halves, core, 0, keepdims=False)
    given = lax.dynamic_index_in_dim(halves, 1 - core, 0, keepdims=False)
    rider = (kept + swap_cores(given)).astype(jnp.bfloat16).reshape(96, 8, CHANNELS)
    left, right = column_halo(above, hidden_grad, below)
    grad_rows, left, right, rider = tie(grad_rows, left, right, rider)
    corner, back = mix(rank, grad_rows, grad_corner, spectral_weight, order, rider)
    back, left, right = tie(back, left, right)
    back = between_degrees(back)
    back_inputs = stencil(
        above, hidden_grad, below, left, right, disco_kernel, neighbour_offsets, lat_first, -1
    )
    local_back = jnp.einsum(
        "kabd,kcd->abc", back_inputs, disco_weight, preferred_element_type=jnp.float32
    )
    back, local_back = tie(back, local_back)
    waves_back = wave_blocks(back, corner, analysis_parts, True)
    waves_back, grad_rows = tie(waves_back, grad_rows)
    waves_back = between_chips(waves_back)
    (spectral_grad,) = on_device(
        outer_kernel,
        [((2, 2, 2, CHANNELS, CHANNELS), jnp.float32)],
        (rank.reshape(1), modes, modes_corner, grad_rows, grad_corner, order),
        "outer",
        2 * 1536 * 768 * 768,
        1,
        [
            *(pltpu.VMEM(size, jnp.bfloat16) for size in UNFOLDED * 2),
            *[pltpu.VMEM((DEVICES, 16, CHANNELS), jnp.bfloat16)] * 2,
            pltpu.SemaphoreType.DMA((2,)),
        ],
        (1, 3),
    )
    waves_back, spectral_grad = tie(waves_back, spectral_grad)
    waves_other = swap_cores(waves_back)
    sums = (2, 48, 2, 8, CHANNELS)
    field_grad, disco_grad = on_device(
        finish_kernel,
        [(BLOCK, jnp.bfloat16), (sums, jnp.float32)],
        (core.reshape(1), backward_tables, waves_back, waves_other, local_back),
        "finish",
        WAVE_FLOPS,
        1,
        [pltpu.VMEM(sums, jnp.float32), pltpu.SemaphoreType.DMA((2,)), *fetched],
        (1, 4),
        (1,),
    )
    return (
        block_output,
        field_grad,
        spectral_grad,
        disco_grad.reshape(4, CHANNELS, CHANNELS),
    )


def solution(mesh):
    forward_all, backward_all = wave_tables()
    place = np.arange(256)
    order = (place[:, None] == (place % 16 * 16 + place // 16)[None, :]).astype(ml_dtypes.bfloat16)
    split = Mesh(mesh.devices.reshape(32, 2, 2), ALL)
    lon = ("zhi", "core")
    return jax.shard_map(
        functools.partial(
            local,
            forward_all=forward_all,
            backward_all=backward_all,
            spread=spread_matrix(),
            order=order,
        ),
        mesh=split,
        in_specs=(
            P("lat", lon, None),
            P("lat", lon, None),
            P(None, ALL, None, None),
            P(None, ALL, None, None),
            P(None, ALL, None, None, None),
            P(),
            P(),
            P(),
        ),
        out_specs=(
            P("lat", lon, None),
            P("lat", lon, None),
            P(None, ALL, None, None, None),
            P(),
        ),
        check_vma=False,
    )
```

```python
import functools
import math

import jax
import jax.numpy as jnp
import ml_dtypes
import numpy as np
from jax import lax
from jax.experimental import pallas as pl
from jax.experimental.pallas import tpu as pltpu
from jax.sharding import Mesh
from jax.sharding import PartitionSpec as P

HALO_REACH = 2
LON_CELLS = 1440
LON_DEV = 360
CHANNELS = 384
DEGREES = 512
HALF = 256
DEVICES = 128
ALL = ("lat", "zhi", "core")
CHIPS = ("lat", "zhi")
SWAP = [(0, 1), (1, 0)]


def wave_tables():
    e, lh, p, ri = np.meshgrid(*map(np.arange, (64, 2, 2, 2)), indexing="ij")
    e, lh, p, ri = (v.reshape(-1) for v in (e, lh, p, ri))
    forward = np.zeros((2, 2, 512, LON_DEV), np.float32)
    backward = np.zeros((2, 2, LON_DEV, 512), np.float32)

    def basis(wave_core, cell_core):
        base = 4 * e + 2 * wave_core + p
        wave = np.where(lh == 0, base, DEGREES - 1 - base)
        column = np.arange(LON_DEV) + LON_DEV * cell_core
        angle = (wave[:, None] * column[None, :] % LON_CELLS) * (2.0 * math.pi / LON_CELLS)
        return np.where(ri[:, None] == 0, np.cos(angle), -np.sin(angle)) / math.sqrt(LON_CELLS)

    for core in range(2):
        for other in range(2):
            forward[core, other] = basis(core, core ^ other)
            backward[core, other] = basis(core ^ other, core).T
    return forward.astype(ml_dtypes.bfloat16), backward.astype(ml_dtypes.bfloat16)


def spread_matrix():
    row, lh, cp, cri = (
        v.reshape(-1) for v in np.meshgrid(*map(np.arange, (64, 2, 2, 2)), indexing="ij")
    )
    slh, sp, sa = (v.reshape(-1) for v in np.meshgrid(*map(np.arange, (2, 2, 64)), indexing="ij"))
    spread = (
        (slh[:, None] == lh[None, :]) & (sp[:, None] == cp[None, :]) & (sa[:, None] == row[None, :])
    )
    return spread.astype(np.float32).astype(ml_dtypes.bfloat16)


def tie(*values):
    return lax.optimization_barrier(values)


def dot(left, right):
    return jnp.dot(left, right, preferred_element_type=jnp.float32)


def dot_nt(left, right):
    return lax.dot_general(
        left, right, (((1,), (1,)), ((), ())), preferred_element_type=jnp.float32
    )


def one_hot(wanted, shape):
    degree = lax.broadcasted_iota(jnp.int32, shape, 1)
    return jnp.where(degree == wanted, 1.0, 0.0).astype(jnp.bfloat16)


def keep(rows, cols, values):
    return jnp.where(rows == cols, values, 0.0).astype(jnp.bfloat16)


def legendre_kernel(
    rank_ref,
    table_ref,
    spread_ref,
    turned_ref,
    matrix_hbm,
    flipped_hbm,
    matrix_ref,
    flipped_ref,
    sems,
):
    rank = rank_ref[0]
    saves = []
    lower = table_ref[0].reshape(128, DEGREES)
    upper = table_ref[1].reshape(128, DEGREES)
    spread = spread_ref[...]
    turned = turned_ref[...]

    def attributes(place):
        p, kind = (place >> 2) & 1, (place >> 3) & 1
        fold = 2 * (place >> 4) + (place & 1)
        high = jnp.where(2 * rank + p > fold, kind, 0)
        return kind, fold, ((place >> 1) & 3) + 4 * high

    for block in range(8):
        rows = slice(256 * block, 256 * (block + 1))
        place = lax.broadcasted_iota(jnp.int32, (256, 1), 0) + 256 * block
        kind, fold, code = attributes(place)
        last = DEGREES - 1 - fold
        low = one_hot(jnp.where(kind == 0, last, fold), (256, DEGREES))
        high = one_hot(jnp.where(kind == 0, -1, last), (256, DEGREES))
        picked = jnp.concatenate([dot_nt(low, lower), dot_nt(high, upper)], axis=1)
        picked = picked.astype(jnp.bfloat16)
        column = lax.broadcasted_iota(jnp.int32, (1, 512), 1) & 7
        matrix_ref[rows, :] = keep(code, column, dot(picked, spread))
        _, _, across = attributes(lax.broadcasted_iota(jnp.int32, (1, 256), 1) + 256 * block)
        down = lax.broadcasted_iota(jnp.int32, (512, 1), 0) & 7
        flipped_ref[:, rows] = keep(down, across, dot_nt(turned, picked))
        saves.append(started(matrix_ref.at[rows], matrix_hbm.at[rows], sems.at[0, block]))
        saves.append(started(flipped_ref.at[:, rows], flipped_hbm.at[:, rows], sems.at[1, block]))
    place = lax.broadcasted_iota(jnp.int32, (128, 1), 0)
    wanted = jnp.where(place < 4, DEGREES - 1 - (2 * rank + (place >> 1)), -1)
    edge = dot_nt(one_hot(wanted, (128, DEGREES)), upper).astype(jnp.bfloat16)
    column = lax.broadcasted_iota(jnp.int32, (1, 512), 1) & 7
    matrix_ref[2048:2064, :] = keep(place[:16] + 4, column, dot(edge[:16], spread[128:]))
    across = lax.broadcasted_iota(jnp.int32, (1, 128), 1) + 4
    down = lax.broadcasted_iota(jnp.int32, (512, 1), 0) & 7
    flipped_ref[:, 2048:2176] = keep(down, across, dot_nt(turned[:, 128:], edge))
    rows = slice(2048, 2064)
    saves.append(started(matrix_ref.at[rows], matrix_hbm.at[rows], sems.at[0, 8]))
    rows = slice(2048, 2176)
    saves.append(started(flipped_ref.at[:, rows], flipped_hbm.at[:, rows], sems.at[1, 8]))
    for save in saves:
        save.wait()


def chip_signs():
    line = lax.broadcasted_iota(jnp.int32, (1, 16, CHANNELS), 1)
    odd = ((line >> 2) ^ (line >> 1)) & 1
    return jnp.where(odd == 1, -1.0, 1.0)


def to_coefficients_kernel(
    matrix_hbm,
    spectra_hbm,
    out_hbm,
    corner_ref,
    matrix_ref,
    out_ref,
    in_sems,
    out_sems,
    spectra_ref,
    spectra_sem,
):
    arrival = started(spectra_hbm, spectra_ref, spectra_sem)
    parts = [slice(512 * block, 512 * (block + 1)) for block in range(3)] + [slice(1536, 2064)]
    loads = [
        started(matrix_hbm.at[rows], matrix_ref.at[rows], in_sems.at[n])
        for n, rows in enumerate(parts)
    ]
    saves = []
    arrival.wait()
    both = spectra_ref[...].astype(jnp.float32)
    spectra = (both[:, 0] + chip_signs() * both[:, 1]).reshape(512, CHANNELS).astype(jnp.bfloat16)
    for block, rows in enumerate(parts):
        loads[block].wait()
        sums = dot(matrix_ref[rows, :], spectra).astype(jnp.bfloat16)
        places = slice(32 * block, 32 * (block + 1))
        out_ref[places] = sums[:512].reshape(32, 16, CHANNELS)
        saves.append(started(out_ref.at[places], out_hbm.at[places], out_sems.at[block]))
    corner = sums[512:]
    corner_ref[...] = corner.astype(jnp.float32)
    for save in saves:
        save.wait()


def from_modes_kernel(
    flipped_hbm,
    rows_ref,
    corner_ref,
    out_hbm,
    flipped_ref,
    out_ref,
    in_sems,
    out_sems,
    *,
    rider,
):
    parts = [slice(256 * block, 256 * (block + 1)) for block in range(2)]
    loads = [
        started(flipped_hbm.at[lines], flipped_ref.at[lines], in_sems.at[n])
        for n, lines in enumerate(parts)
    ]
    saves = []
    rows = rows_ref[:, 0:16, :].reshape(2048, CHANNELS)
    corner = corner_ref[...].astype(jnp.bfloat16)
    if rider:
        shares = rows_ref[...].astype(jnp.float32).reshape(64, 2, 24, CHANNELS)[:, :, 16:24, :]
        owned = jnp.sum(shares, axis=0).reshape(16, CHANNELS).astype(jnp.bfloat16)
        out_ref[:, :, 16:32, :] = jnp.broadcast_to(owned[None, None], (32, 2, 16, CHANNELS))
    for block, lines in enumerate(parts):
        loads[block].wait()
        waves = dot(flipped_ref[lines, 0:2048], rows) + dot(flipped_ref[lines, 2048:2064], corner)
        waves = waves.reshape(16, 16, CHANNELS)
        places = slice(16 * block, 16 * (block + 1))
        out_ref[places, 0, 0:16, :] = waves.astype(jnp.bfloat16)
        out_ref[places, 1, 0:16, :] = (waves * chip_signs()).astype(jnp.bfloat16)
        saves.append(started(out_ref.at[places], out_hbm.at[places], out_sems.at[block]))
    for save in saves:
        save.wait()


def legendre_matrices(table, rank, spread, flops):
    shapes = [((2064, 512), jnp.bfloat16), ((512, 2176), jnp.bfloat16)]
    operands = (rank.reshape(1), table, jnp.asarray(spread), jnp.asarray(spread.T))
    scratch = [
        pltpu.VMEM((2064, 512), jnp.bfloat16),
        pltpu.VMEM((512, 2176), jnp.bfloat16),
        pltpu.SemaphoreType.DMA((2, 9)),
    ]
    return on_device(
        legendre_kernel, shapes, operands, "legendre", flops, 1, scratch, (), (0, 1)
    )


def unfold(rows_of, order, edge_ref, rank, high_ref, low_ref):
    for block in range(8):
        turned = dot(order, rows_of(block)).astype(jnp.bfloat16)
        for q in range(16):
            kind, p, ri, j = q >> 3, (q >> 2) & 1, (q >> 1) & 1, q & 1
            piece = turned[16 * q : 16 * (q + 1), :]
            row = 128 * p + 16 * block
            lanes = slice(CHANNELS * ri, CHANNELS * (ri + 1))
            if kind == 0:
                high_ref[j, row : row + 16, lanes] = piece
            else:
                low_ref[j, row : row + 16, lanes] = piece
    base = wave_places()
    for j in range(2):
        fold = 2 * rank + j
        both = low_ref[j].astype(jnp.float32)
        edge = jnp.concatenate(
            [edge_ref[2 * j : 2 * j + 1, :], edge_ref[2 * j + 1 : 2 * j + 2, :]], axis=1
        )
        high_ref[j, 256:512, :] = jnp.where(
            base > fold, both, jnp.where(base == fold, edge, 0.0)
        ).astype(jnp.bfloat16)
        low_ref[j] = jnp.where(base <= fold, both, 0.0).astype(jnp.bfloat16)


def wave_places():
    place = lax.broadcasted_iota(jnp.int32, (256, 2 * CHANNELS), 0)
    return 2 * (place & 127) + (place >> 7)


def complete(weight_ref, loads):
    c = CHANNELS
    for load in loads:
        load.wait()
    weight_ref[c:, c:] = weight_ref[:c, :c]
    weight_ref[c:, :c] = -weight_ref[:c, c:]


def mix_kernel(rank_ref, rows_hbm, edge_ref, order_ref, weight_hbm, *refs, back):
    rider_ref, refs = (refs[0], refs[1:]) if back else (None, refs)
    edge_out_ref, out_hbm, rows_ref, weight_ref, out_ref, high_ref, low_ref, mixed, *sems = refs
    row_sems, weight_sems, out_sems = sems
    arrivals = []
    for block in range(4):
        sources = slice(32 * block, 32 * (block + 1))
        arrivals.append(started(rows_hbm.at[sources], rows_ref.at[sources], row_sems.at[block]))
    loads = {}
    for n, (kind, j) in enumerate(((1, 0), (0, 0), (1, 1), (0, 1))):
        loads[kind, j] = [
            started(
                weight_hbm.at[kind, j, ri],
                weight_ref.at[kind, j, 0:CHANNELS, CHANNELS * ri : CHANNELS * (ri + 1)],
                weight_sems.at[n, ri],
            )
            for ri in range(2)
        ]
    order = order_ref[...]

    def rows_of(block):
        if block % 2 == 0:
            arrivals[block // 2].wait()
        return rows_ref[16 * block : 16 * block + 16].reshape(256, CHANNELS)

    unfold(rows_of, order, edge_ref, rank_ref[0], high_ref, low_ref)
    base = wave_places()
    product = dot_nt if back else dot
    for j in range(2):
        fold = 2 * rank_ref[0] + j
        complete(weight_ref.at[1, j], loads[1, j])
        shared = product(high_ref[j], weight_ref[1, j])
        mixed[0, j] = shared[:256].astype(jnp.bfloat16)
        high = shared[256:]
        complete(weight_ref.at[0, j], loads[0, j])
        low = product(low_ref[j], weight_ref[0, j])
        mixed[1, j] = jnp.where(base <= fold, low, high).astype(jnp.bfloat16)
        corner = jnp.sum(jnp.where(base == fold, high, 0.0), axis=0, keepdims=True)
        edge_out_ref[2 * j : 2 * j + 1, :] = corner[:, :CHANNELS]
        edge_out_ref[2 * j + 1 : 2 * j + 2, :] = corner[:, CHANNELS:]
    edge_out_ref[4:16, :] = jnp.zeros((12, CHANNELS), jnp.float32)
    if rider_ref is not None:
        out_ref[0:96, 16:24, :] = rider_ref[...]
        out_ref[96:128, 16:24, :] = jnp.zeros((32, 8, CHANNELS), jnp.bfloat16)
    saves = []
    for block in range(8):
        pieces = []
        for q in range(16):
            kind, p, ri, j = q >> 3, (q >> 2) & 1, (q >> 1) & 1, q & 1
            row = 128 * p + 16 * block
            pieces.append(mixed[kind, j, row : row + 16, CHANNELS * ri : CHANNELS * (ri + 1)])
        turned = dot(order, jnp.concatenate(pieces, axis=0))
        owners = slice(16 * block, 16 * (block + 1))
        out_ref[owners, 0:16, :] = turned.astype(jnp.bfloat16).reshape(16, 16, CHANNELS)
        if block % 2 == 1:
            pair = slice(16 * (block - 1), 16 * (block + 1))
            saves.append(started(out_ref.at[pair], out_hbm.at[pair], out_sems.at[block // 2]))
    for save in saves:
        save.wait()


UNFOLDED = ((2, 512, 2 * CHANNELS), (2, 256, 2 * CHANNELS))


def mix(rank, rows, edge, weights, order, rider=None):
    back = rider is not None
    flops = 2 * 1536 * 768 * 768 + 4 * 2048 * 256 * 384
    blocks = (DEVICES, 24 if back else 16, CHANNELS)
    operands = (rank.reshape(1), rows, edge, order, weights) + ((rider,) if back else ())
    shapes = [((16, CHANNELS), jnp.float32), (blocks, jnp.bfloat16)]
    scratch = [
        pltpu.VMEM((DEVICES, 16, CHANNELS), jnp.bfloat16),
        pltpu.VMEM((2, 2, 2 * CHANNELS, 2 * CHANNELS), jnp.bfloat16),
        pltpu.VMEM(blocks, jnp.bfloat16),
        pltpu.VMEM(UNFOLDED[0], jnp.bfloat16),
        pltpu.VMEM(UNFOLDED[1], jnp.bfloat16),
        pltpu.VMEM((2, 2, 256, 2 * CHANNELS), jnp.bfloat16),
        pltpu.SemaphoreType.DMA((4,)),
        pltpu.SemaphoreType.DMA((4, 2)),
        pltpu.SemaphoreType.DMA((4,)),
    ]
    return on_device(
        functools.partial(mix_kernel, back=back),
        shapes,
        operands,
        "mix_back" if back else "mix_modes",
        flops,
        1,
        scratch,
        (1, 4),
        (1,),
    )


def forward_kernel(table_ref, mine_ref, other_ref, out_ref):
    for part in range(4):
        rows = slice(128 * part, 128 * (part + 1))
        lines = []
        for a in range(2):
            sums = dot(table_ref[0, rows, :], mine_ref[a]) + dot(table_ref[1, rows, :], other_ref[a])
            lines.append(sums.reshape(16, 8, CHANNELS))
        out_ref[16 * part : 16 * (part + 1)] = jnp.concatenate(lines, axis=1).astype(jnp.bfloat16)


def fetch(core_ref, table_hbm, table_ref, local_hbm, local_ref, sems):
    return [
        started(table_hbm.at[core_ref[0]], table_ref, sems.at[0]),
        started(local_hbm, local_ref, sems.at[1]),
    ]


def inverse_rows(table_ref, mine, other, a):
    def pick(waves):
        return waves[:, 8 * a : 8 * (a + 1), :].reshape(512, CHANNELS).astype(jnp.bfloat16)

    sums = dot(table_ref[0], pick(mine)) + dot(table_ref[1], pick(other))
    return sums.astype(jnp.bfloat16).astype(jnp.float32)


def activate_kernel(
    table_ref,
    mine_ref,
    other_ref,
    local_hbm,
    cotangent_ref,
    out_ref,
    grad_ref,
    local_ref,
    fetch_sem,
):
    load = started(local_hbm, local_ref, fetch_sem)
    mine = mine_ref[:, 0:16, :].astype(jnp.float32)
    other = other_ref[:, 0:16, :].astype(jnp.float32)
    scale = math.sqrt(2.0 / math.pi)
    for a in range(2):
        sums = inverse_rows(table_ref, mine, other, a)
        if a == 0:
            load.wait()
        v = sums + local_ref[a]
        square = v * v
        t = jnp.tanh(scale * (v + 0.044715 * (v * square)))
        half = 0.5 * (1.0 + t)
        out_ref[a] = (v * half).astype(jnp.bfloat16)
        slope = half + 0.5 * v * (1.0 - t * t) * (scale * (1.0 + 3 * 0.044715 * square))
        grad_ref[a] = (cotangent_ref[a].astype(jnp.float32) * slope).astype(jnp.bfloat16)


def finish_kernel(
    core_ref,
    table_hbm,
    mine_ref,
    other_ref,
    local_hbm,
    out_ref,
    sums_hbm,
    sums_ref,
    sems,
    table_ref,
    local_ref,
    fetch_sems,
):
    loads = fetch(core_ref, table_hbm, table_ref, local_hbm, local_ref, fetch_sems)
    mine = mine_ref[...].astype(jnp.float32)
    other = other_ref[...].astype(jnp.float32)
    saves = []
    for half in range(2):
        rows = slice(16 + 8 * half, 24 + 8 * half)
        pair = [mine[:48, rows, :], other[:48, rows, :]]
        for core in range(2):
            kept = jnp.where(core_ref[0] == core, pair[0], pair[1])
            sums_ref[half, :, core] = kept
        saves.append(started(sums_ref.at[half], sums_hbm.at[half], sems.at[half]))
    loads[0].wait()
    for a in range(2):
        sums = inverse_rows(table_ref, mine[:, :16], other[:, :16], a)
        if a == 0:
            loads[1].wait()
        total = sums + local_ref[a]
        out_ref[a] = total.astype(jnp.bfloat16)
    for save in saves:
        save.wait()


MARGIN = 8
CHUNK = 40


def stencil_kernel(
    weight_ref,
    corner_ref,
    above_ref,
    mine_ref,
    below_ref,
    left_ref,
    right_ref,
    out_ref,
    line,
    shifted,
    sums,
    *,
    sign,
):
    blocks = (above_ref, mine_ref, below_ref)
    for row in range(6):
        line[MARGIN : MARGIN + LON_DEV, :] = blocks[row // 2][row % 2].astype(jnp.float32)
        line[MARGIN - HALO_REACH : MARGIN, :] = left_ref[row]
        line[MARGIN + LON_DEV : MARGIN + LON_DEV + HALO_REACH, :] = right_ref[row]
        for shift in range(5):
            first = MARGIN - HALO_REACH + shift
            shifted[shift, row] = line[first : first + LON_DEV, :]

    def step(index, carry):
        first = pl.multiple_of(index * CHUNK, 8)
        for a in range(2):
            for lane in range(3):
                lanes = slice(128 * lane, 128 * (lane + 1))
                totals = [jnp.zeros((CHUNK, 128), jnp.float32)] * 4
                for n in range(9):
                    row = sign * corner_ref[n, 0] + HALO_REACH + a
                    column = sign * corner_ref[n, 1] + HALO_REACH
                    cells = shifted[column, row, pl.ds(first, CHUNK), lanes]
                    totals = [totals[k] + weight_ref[8 * n + 2 * k + a] * cells for k in range(4)]
                for k in range(4):
                    sums[k, a, pl.ds(first, CHUNK), lanes] = totals[k]
        return carry

    lax.fori_loop(0, LON_DEV // CHUNK, step, 0)
    for k in range(4):
        for a in range(2):
            out_ref[k, a] = sums[k, a].astype(jnp.bfloat16)


def outer_kernel(
    rank_ref, rows_hbm, edge_ref, grad_rows_hbm, grad_edge_ref, order_ref, out_ref, *refs
):
    high_ref, low_ref, high_grad_ref, low_grad_ref, rows_ref, grad_rows_ref, sems = refs
    loads = [
        started(rows_hbm, rows_ref, sems.at[0]),
        started(grad_rows_hbm, grad_rows_ref, sems.at[1]),
    ]
    order = order_ref[...]
    for load in loads:
        load.wait()

    def taken(ref):
        return lambda block: ref[16 * block : 16 * block + 16].reshape(256, CHANNELS)

    unfold(taken(rows_ref), order, edge_ref, rank_ref[0], high_ref, low_ref)
    unfold(taken(grad_rows_ref), order, grad_edge_ref, rank_ref[0], high_grad_ref, low_grad_ref)
    c = CHANNELS
    for kind, (left_ref, right_ref) in enumerate(((low_ref, low_grad_ref), (high_ref, high_grad_ref))):
        for j in range(2):
            right = right_ref[j]
            across = (((0,), (0,)), ((), ()))
            first = lax.dot_general(
                left_ref[j, :, :c], right, across, preferred_element_type=jnp.float32
            )
            second = lax.dot_general(
                left_ref[j, :, c:], right, across, preferred_element_type=jnp.float32
            )
            out_ref[kind, j, 0] = first[:, :c] + second[:, c:]
            out_ref[kind, j, 1] = first[:, c:] - second[:, :c]


def on_device(
    kernel, shapes, operands, name, flops, scalars=0, scratch=(), far_in=(), far_out=()
):
    vmem = pl.BlockSpec(memory_space=pltpu.VMEM)
    smem = pl.BlockSpec(memory_space=pltpu.SMEM)
    far = pl.BlockSpec(memory_space=pltpu.HBM)
    moved = sum(math.prod(v.shape) * v.dtype.itemsize for v in operands)
    moved += sum(math.prod(size) * jnp.dtype(kind).itemsize for size, kind in shapes)
    shapes = [
        pltpu.HBM(*s) if n in far_out else jax.ShapeDtypeStruct(*s) for n, s in enumerate(shapes)
    ]
    operands = [
        pltpu.with_memory_space_constraint(v, pltpu.HBM) if n in far_in else v
        for n, v in enumerate(operands)
    ]
    ins = [smem if n < scalars else far if n in far_in else vmem for n in range(len(operands))]
    return pl.pallas_call(
        kernel,
        out_shape=tuple(shapes),
        in_specs=ins,
        out_specs=tuple(far if n in far_out else vmem for n in range(len(shapes))),
        scratch_shapes=list(scratch),
        compiler_params=pltpu.CompilerParams(vmem_limit_bytes=48 * 1024 * 1024),
        cost_estimate=pl.CostEstimate(flops=flops, bytes_accessed=moved, transcendentals=0),
        name=name,
    )(*operands)


def started(source, target, sem):
    copy = pltpu.make_async_copy(source, target, sem)
    copy.start()
    return copy


BLOCK = (2, LON_DEV, CHANNELS)
WAVE_FLOPS = 2 * 512 * 720 * 768


def swap_cores(values):
    return lax.ppermute(values, "core", SWAP)


def edges_kernel(above_ref, block_ref, below_ref, tail_ref, head_ref):
    for n, ref in enumerate((above_ref, block_ref, below_ref)):
        for a in range(2):
            cells = ref[a].astype(jnp.float32)
            tail_ref[2 * n + a] = cells[LON_DEV - HALO_REACH :]
            head_ref[2 * n + a] = cells[:HALO_REACH]


def to_wave_blocks(mine, other, table):
    shapes = [((64, 16, CHANNELS), jnp.bfloat16)]
    return on_device(forward_kernel, shapes, (table, mine, other), "to_waves", WAVE_FLOPS)[0]


def between_chips(blocks):
    return lax.all_to_all(blocks, CHIPS, split_axis=0, concat_axis=0, tiled=True)


def between_degrees(blocks):
    return lax.all_to_all(blocks, ALL, split_axis=0, concat_axis=0, tiled=True)


def coefficient_blocks(spectra, matrices):
    matrix, flipped = matrices
    operands = (matrix, spectra.reshape(32, 2, 16, CHANNELS))
    blocks = (DEVICES, 16, CHANNELS)
    shapes = [(blocks, jnp.bfloat16), ((16, CHANNELS), jnp.float32)]
    scratch = [
        pltpu.VMEM((2064, 512), jnp.bfloat16),
        pltpu.VMEM(blocks, jnp.bfloat16),
        pltpu.SemaphoreType.DMA((4,)),
        pltpu.SemaphoreType.DMA((4,)),
        pltpu.VMEM((32, 2, 16, CHANNELS), jnp.bfloat16),
        pltpu.SemaphoreType.DMA(()),
    ]
    flops = 2 * 2048 * 512 * 512
    return on_device(
        to_coefficients_kernel, shapes, operands, "to_coefficients", flops, 0, scratch, (0, 1), (0,)
    )


def wave_blocks(rows, corner, matrices, rider):
    matrix, flipped = matrices
    blocks = (32, 2, 32 if rider else 16, CHANNELS)
    scratch = [
        pltpu.VMEM((512, 2176), jnp.bfloat16),
        pltpu.VMEM(blocks, jnp.bfloat16),
        pltpu.SemaphoreType.DMA((2,)),
        pltpu.SemaphoreType.DMA((2,)),
    ]
    (out,) = on_device(
        functools.partial(from_modes_kernel, rider=rider),
        [(blocks, jnp.bfloat16)],
        (flipped, rows, corner),
        "from_modes",
        2 * 2048 * 512 * 512,
        0,
        scratch,
        (0,),
        (0,),
    )
    return out.reshape(64, -1, CHANNELS)


def row_halo(block):
    above = lax.ppermute(block, "lat", [(i, i + 1) for i in range(31)])
    below = lax.ppermute(block, "lat", [(i + 1, i) for i in range(31)])
    return above, below


def column_halo(above, block, below):
    shapes = [((6, HALO_REACH, CHANNELS), jnp.float32)] * 2
    tails, heads = on_device(edges_kernel, shapes, (above, block, below), "edges", 0)
    lon = ("zhi", "core")
    left = lax.ppermute(tails, lon, [(i, (i + 1) % 4) for i in range(4)])
    right = lax.ppermute(heads, lon, [((i + 1) % 4, i) for i in range(4)])
    return left, right


def stencil(above, block, below, left, right, disco_kernel, offsets, lat_first, sign):
    row = lat_first + jnp.arange(2, dtype=jnp.int32)[None, :]
    row = row - offsets[:, :1] if sign < 0 else row + jnp.zeros_like(offsets[:, :1])
    chosen = row[:, :, None] == jnp.arange(64, dtype=jnp.int32)[None, None, :]
    weights = jnp.sum(
        jnp.where(chosen[:, None], disco_kernel[:, :, None, :], 0.0), axis=-1
    ).reshape(-1)
    operands = (weights, offsets, above, block, below, left, right)
    scratch = [
        pltpu.VMEM((LON_DEV + 2 * MARGIN, CHANNELS), jnp.float32),
        pltpu.VMEM((5, 6, LON_DEV, CHANNELS), jnp.float32),
        pltpu.VMEM((4, *BLOCK), jnp.float32),
    ]
    shapes = [((4, *BLOCK), jnp.bfloat16)]
    name = "stencil" if sign > 0 else "stencil_back"
    flops = 2 * 36 * math.prod(BLOCK) * 16
    kernel = functools.partial(stencil_kernel, sign=sign)
    return on_device(kernel, shapes, operands, name, flops, 2, scratch)[0]


def local(
    grid_field,
    cotangent,
    analysis_table,
    synthesis_table,
    spectral_weight,
    disco_weight,
    disco_kernel,
    neighbour_offsets,
    *,
    forward_all,
    backward_all,
    spread,
    order,
):
    lat, zhi, core = (lax.axis_index(name) for name in ALL)
    rank = lat * 4 + zhi * 2 + core
    lat_first = lat * 2
    forward_table = lax.dynamic_index_in_dim(jnp.asarray(forward_all), core, 0, keepdims=False)
    order = jnp.asarray(order)
    block_shapes = [(BLOCK, jnp.bfloat16)]

    grid_other = swap_cores(grid_field)
    above, below = row_halo(grid_field)
    blocks = to_wave_blocks(grid_field, grid_other, forward_table)
    blocks, analysis_table = tie(blocks, analysis_table)
    backward_tables = jnp.asarray(backward_all)
    spectra = between_chips(blocks)
    analysis_parts = legendre_matrices(analysis_table, rank, spread, 0)
    spectra, synthesis_table, *analysis_parts = tie(spectra, synthesis_table, *analysis_parts)
    synthesis_table, above, below = tie(synthesis_table, above, below)
    rows, modes_corner = coefficient_blocks(spectra, analysis_parts)
    modes = between_degrees(rows)
    synthesis_parts = legendre_matrices(synthesis_table, rank, spread, 16_000_000_000)
    left, right = column_halo(above, grid_field, below)
    modes, left, right, *synthesis_parts = tie(modes, left, right, *synthesis_parts)
    corner, mixed = mix(rank, modes, modes_corner, spectral_weight, order)
    mixed, left, right = tie(mixed, left, right)
    mixed = between_degrees(mixed)
    inputs = stencil(
        above, grid_field, below, left, right, disco_kernel, neighbour_offsets, lat_first, 1
    )
    local_part = jnp.einsum(
        "kabc,kcd->abd", inputs, disco_weight, preferred_element_type=jnp.float32
    )
    mixed, local_part, inputs = tie(mixed, local_part, inputs)
    waves = wave_blocks(mixed, corner, synthesis_parts, False)
    waves, cotangent = tie(waves, cotangent)
    waves = between_chips(waves)
    fetched = [
        pltpu.VMEM((2, LON_DEV, 512), jnp.bfloat16),
        pltpu.VMEM(BLOCK, jnp.float32),
        pltpu.SemaphoreType.DMA((2,)),
    ]
    block_output, hidden_grad = on_device(
        activate_kernel,
        block_shapes * 2,
        (
            lax.dynamic_index_in_dim(backward_tables, core, 0, keepdims=False),
            waves,
            swap_cores(waves),
            local_part,
            cotangent,
        ),
        "activate",
        WAVE_FLOPS,
        0,
        [pltpu.VMEM(BLOCK, jnp.float32), pltpu.SemaphoreType.DMA(())],
        (3,),
    )

    blocks = to_wave_blocks(hidden_grad, swap_cores(hidden_grad), forward_table)
    blocks, hidden_grad = tie(blocks, hidden_grad)
    above, below = row_halo(hidden_grad)
    grad_spectra = between_chips(blocks)
    grad_rows, grad_corner = coefficient_blocks(grad_spectra, synthesis_parts)
    grad_rows, inputs = tie(grad_rows, inputs)
    grad_rows = between_degrees(grad_rows)
    inputs, above, below = tie(inputs, above, below)
    local_grad = jnp.einsum(
        "kabc,abd->kcd", inputs, hidden_grad, preferred_element_type=jnp.float32
    ) * (1.0 / math.sqrt(64 * LON_CELLS))
    halves = local_grad.reshape(2, 2 * CHANNELS, CHANNELS)
    kept = lax.dynamic_index_in_dim(halves, core, 0, keepdims=False)
    given = lax.dynamic_index_in_dim(halves, 1 - core, 0, keepdims=False)
    rider = (kept + swap_cores(given)).astype(jnp.bfloat16).reshape(96, 8, CHANNELS)
    left, right = column_halo(above, hidden_grad, below)
    grad_rows, left, right, rider = tie(grad_rows, left, right, rider)
    corner, back = mix(rank, grad_rows, grad_corner, spectral_weight, order, rider)
    back, left, right = tie(back, left, right)
    back = between_degrees(back)
    back_inputs = stencil(
        above, hidden_grad, below, left, right, disco_kernel, neighbour_offsets, lat_first, -1
    )
    local_back = jnp.einsum(
        "kabd,kcd->abc", back_inputs, disco_weight, preferred_element_type=jnp.float32
    )
    back, local_back = tie(back, local_back)
    waves_back = wave_blocks(back, corner, analysis_parts, True)
    waves_back, grad_rows = tie(waves_back, grad_rows)
    waves_back = between_chips(waves_back)
    (spectral_grad,) = on_device(
        outer_kernel,
        [((2, 2, 2, CHANNELS, CHANNELS), jnp.float32)],
        (rank.reshape(1), modes, modes_corner, grad_rows, grad_corner, order),
        "outer",
        2 * 1536 * 768 * 768,
        1,
        [
            *(pltpu.VMEM(size, jnp.bfloat16) for size in UNFOLDED * 2),
            *[pltpu.VMEM((DEVICES, 16, CHANNELS), jnp.bfloat16)] * 2,
            pltpu.SemaphoreType.DMA((2,)),
        ],
        (1, 3),
    )
    waves_back, spectral_grad = tie(waves_back, spectral_grad)
    waves_other = swap_cores(waves_back)
    sums = (2, 48, 2, 8, CHANNELS)
    field_grad, disco_grad = on_device(
        finish_kernel,
        [(BLOCK, jnp.bfloat16), (sums, jnp.float32)],
        (core.reshape(1), backward_tables, waves_back, waves_other, local_back),
        "finish",
        WAVE_FLOPS,
        1,
        [pltpu.VMEM(sums, jnp.float32), pltpu.SemaphoreType.DMA((2,)), *fetched],
        (1, 4),
        (1,),
    )
    return (
        block_output,
        field_grad,
        spectral_grad,
        disco_grad.reshape(4, CHANNELS, CHANNELS),
    )


def solution(mesh):
    forward_all, backward_all = wave_tables()
    place = np.arange(256)
    order = (place[:, None] == (place % 16 * 16 + place // 16)[None, :]).astype(ml_dtypes.bfloat16)
    split = Mesh(mesh.devices.reshape(32, 2, 2), ALL)
    lon = ("zhi", "core")
    return jax.shard_map(
        functools.partial(
            local,
            forward_all=forward_all,
            backward_all=backward_all,
            spread=spread_matrix(),
            order=order,
        ),
        mesh=split,
        in_specs=(
            P("lat", lon, None),
            P("lat", lon, None),
            P(None, ALL, None, None),
            P(None, ALL, None, None),
            P(None, ALL, None, None, None),
            P(),
            P(),
            P(),
        ),
        out_specs=(
            P("lat", lon, None),
            P("lat", lon, None),
            P(None, ALL, None, None, None),
            P(),
        ),
        check_vma=False,
    )
```
